256 devices in a mesh: section: 2 (over core), row: 16 (over z, x_lo), col: 8 (over y, x_hi).
Axes of the slice: x: 4 (x_hi: 2, x_lo: 2; x = x_hi * 2 + x_lo), y: 4, z: 8, core: 2. Of those that a mesh axis runs over, the one named last changes fastest.
Arguments:
- inputs: bfloat16 [2, 128, 6144], P(None, None, 'row'), may hold values from -6 to 6
- cotangent: bfloat16 [2, 128, 6144], P(None, None, 'row'), may hold values from -1.5 to 1.5
- w_up: bfloat16 [2, 6144, 24576], P('section', 'row', 'col'), may hold values from -0.078125 to 0.078125
- w_down: bfloat16 [2, 24576, 6144], P('section', 'col', 'row'), may hold values from -0.0390625 to 0.0390625
Outputs:
- states: bfloat16 [2, 2, 128, 6144], P('section', None, 'col', 'row')
- input_grads: bfloat16 [2, 2, 128, 6144], P('section', None, 'col', 'row')
- w_up_grad: float32 [2, 6144, 24576], P('section', 'row', 'col')
- w_down_grad: float32 [2, 24576, 6144], P('section', 'col', 'row')
The draws below stay inside these ranges and needn't reach their ends.
All inputs are finite; a program needn't handle non-finite values.
Results may differ from the reference program's by a relative error of at most 0.009.
Values may be sent and summed in bfloat16 or wider, within the bound.
No kernel may reach another device: no remote copies, remote signals or barrier semaphores. Data moves between devices by JAX's collectives and lax.ppermute only.
A program may use at most 64 MiB of HBM per device.

```python
import jax
import jax.numpy as jnp

D = 6144
FF = 24576
MICRO = 2
TOK = 128
LAYERS = 2


def block_scale(stream_key, shape, cuts, smallest, largest):
    level, own = 1.0, jax.random.fold_in(stream_key, 6)
    for axis_at, shards_of in cuts:
        heights = jnp.exp(jax.random.uniform(jax.random.fold_in(own, axis_at), (shards_of,), jnp.float32, smallest / len(cuts), largest / len(cuts)))
        level = level * jnp.repeat(heights, shape[axis_at] // shards_of).reshape([-1 if axis == axis_at else 1 for axis in range(len(shape))])
    return level


def centred(key, dims, scale, reach, split=(), held_as=jnp.bfloat16):
    drawn = scale * jax.random.normal(key, dims, jnp.float32)
    if split:
        drawn = drawn * block_scale(key, dims, split, -0.22, 0.18)
    return jnp.clip(drawn, -reach, reach).astype(held_as)


def setup_inputs(seed: int = 0) -> dict:
    seeds = jax.random.split(jax.random.key(seed), 5)
    inputs = centred(seeds[0], (MICRO, TOK, D), 1.0, 6.0, ((2, 16),))
    cotangent = centred(seeds[1], (MICRO, TOK, D), 0.25, 1.5, ((2, 16),))
    w_up = centred(seeds[2], (LAYERS, D, FF), D ** -0.5, 0.078125, ((0, 2), (1, 16), (2, 8)))
    w_down = centred(seeds[3], (LAYERS, FF, D), FF ** -0.5, 0.0390625, ((0, 2), (1, 8), (2, 16)))
    return {"inputs": inputs, "cotangent": cotangent, "w_up": w_up, "w_down": w_down}


root_two_over_pi = 0.7978845608028654
cubic = 0.044715


def gelu_value(pre):
    inner = root_two_over_pi * (pre + cubic * pre * pre * pre)
    return 0.5 * pre * (1.0 + jnp.tanh(inner))


def gelu_slope(pre):
    inner = root_two_over_pi * (pre + cubic * pre * pre * pre)
    tangent = jnp.tanh(inner)
    return 0.5 * (1.0 + tangent) + 0.5 * pre * (1.0 - tangent * tangent) * root_two_over_pi * (1.0 + 3.0 * cubic * pre * pre)


def reference(inputs, cotangent, w_up, w_down):
    layers = LAYERS
    saved_in = [[None] * MICRO for l in range(layers)]
    saved_pre = [[None] * MICRO for l in range(layers)]
    outputs = [[None] * MICRO for l in range(layers)]
    for batch in range(MICRO):
        current = inputs[batch]
        for l in range(layers):
            pre = jnp.dot(current, w_up[l], preferred_element_type=jnp.float32)
            hidden = gelu_value(pre).astype(jnp.bfloat16)
            result = (current.astype(jnp.float32) + jnp.dot(hidden, w_down[l], preferred_element_type=jnp.float32)).astype(jnp.bfloat16)
            saved_in[l][batch] = current
            saved_pre[l][batch] = pre
            outputs[l][batch] = result
            current = result
    grad_ups = [jnp.zeros((D, FF), jnp.float32) for l in range(layers)]
    grad_downs = [jnp.zeros((FF, D), jnp.float32) for l in range(layers)]
    in_grads = [[None] * MICRO for l in range(layers)]
    for batch in range(MICRO):
        grad = cotangent[batch]
        for l in reversed(range(layers)):
            current = saved_in[l][batch]
            pre = saved_pre[l][batch]
            hidden = gelu_value(pre).astype(jnp.bfloat16)
            d_hidden = jnp.dot(grad, w_down[l].T, preferred_element_type=jnp.float32)
            d_pre = (d_hidden * gelu_slope(pre)).astype(jnp.bfloat16)
            grad_downs[l] = grad_downs[l] + jnp.dot(hidden.T, grad, preferred_element_type=jnp.float32)
            grad_ups[l] = grad_ups[l] + jnp.dot(current.T, d_pre, preferred_element_type=jnp.float32)
            back = jnp.dot(d_pre, w_up[l].T, preferred_element_type=jnp.float32)
            result = (grad.astype(jnp.float32) + back).astype(jnp.bfloat16)
            in_grads[l][batch] = result
            grad = result
    states = jnp.stack([jnp.stack(outputs[l]) for l in range(layers)])
    input_grads = jnp.stack([jnp.stack(in_grads[l]) for l in range(layers)])
    up_grad = jnp.stack(grad_ups)
    down_grad = jnp.stack(grad_downs)
    return states, input_grads, up_grad, down_grad
```

```python
import functools

import jax
import jax.numpy as jnp
from jax import lax
from jax.experimental import pallas as pl
from jax.experimental.pallas import tpu as pltpu
from jax.sharding import Mesh, PartitionSpec as P

root_two_over_pi = 0.7978845608028654
cubic = 0.044715
f32 = jnp.float32
bf16 = jnp.bfloat16
CHUNK = 512
VMEM = pl.BlockSpec(memory_space=pltpu.VMEM)
HBM = pl.BlockSpec(memory_space=pltpu.HBM)
ANY = pl.BlockSpec(memory_space=pl.ANY)
LIMIT = pltpu.CompilerParams(vmem_limit_bytes=14 * 1024 * 1024)


def gelu_both(pre):
    inner = root_two_over_pi * (pre + cubic * pre * pre * pre)
    tangent = jnp.tanh(inner)
    value = 0.5 * pre * (1.0 + tangent)
    slope = 0.5 * (1.0 + tangent) + 0.5 * pre * (1.0 - tangent * tangent) * root_two_over_pi * (
        1.0 + 3.0 * cubic * pre * pre
    )
    return value, slope


def dot(left, right, dims):
    return lax.dot_general(left, right, (dims, ((), ())), preferred_element_type=f32)


def shape_of(shape, dtype=bf16):
    return jax.ShapeDtypeStruct(shape, dtype)


def load_weights(layer, by_rows, refs, held, sems):
    mine = lax.axis_index("section") == layer

    def copy(source, part, i):
        where = pl.ds(i * CHUNK, CHUNK)
        block = source.at[where, :] if by_rows else source.at[:, where]
        return pltpu.make_async_copy(block, held.at[part, i], sems.at[part, i])

    def start(which):
        for i in range(held.shape[1]):
            for part, pair in enumerate(refs):
                copy(pair[which], part, i).start()

    pl.when(mine)(lambda: start(0))
    pl.when(jnp.logical_not(mine))(lambda: start(1))
    return lambda part, i: copy(refs[part][0], part, i).wait()


def widen(xs, by_rows, wait, held, put):
    for i in range(held.shape[1]):
        total = None
        for part, x in enumerate(xs):
            wait(part, i)
            got = dot(x, held[part, i], ((1,), (1 if by_rows else 0,)))
            total = got if total is None else total + got
        put(i, total)


def widen_first_kernel(layer, by_rows, x_ref, own, other, out_ref, held, sems, stage, out_sems):
    wait = load_weights(layer, by_rows, ((own, other),), held, sems)
    per_half = stage.shape[4] // CHUNK

    def out_copy(half):
        return pltpu.make_async_copy(stage.at[:, half], out_ref.at[:, half], out_sems.at[half])

    def put(i, total):
        half, at = i // per_half, (i % per_half) * CHUNK
        total = total.astype(stage.dtype).reshape(stage.shape[2], stage.shape[0], stage.shape[3], CHUNK)
        for mate in range(stage.shape[2]):
            stage[:, half, mate, :, pl.ds(at, CHUNK)] = total[mate]
        if i % per_half == per_half - 1:
            out_copy(half).start()

    widen((x_ref[...],), by_rows, wait, held, put)
    out_copy(0).wait()
    out_copy(1).wait()


def widen_next_kernel(
    layer, by_rows, arrived, base, own, other, own_mate, other_mate, out_ref, x_out, held, sems, stage, out_sems
):
    wait = load_weights(layer, by_rows, ((own, other), (own_mate, other_mate)), held, sems)
    width, per_half = base.shape[1] // 2, stage.shape[3] // CHUNK
    total = arrived[0].astype(f32)
    for i in range(1, arrived.shape[0]):
        total = total + arrived[i].astype(f32)
    x = (base[...].astype(f32) + total).astype(bf16)
    x_out[...] = x

    def out_copy(half):
        return pltpu.make_async_copy(stage.at[:, half], out_ref.at[:, half], out_sems.at[half])

    def put(i, total):
        half, at = i // per_half, (i % per_half) * CHUNK
        stage[:, half, :, pl.ds(at, CHUNK)] = total.astype(bf16).reshape(stage.shape[0], stage.shape[2], CHUNK)
        if i % per_half == per_half - 1:
            out_copy(half).start()

    widen((x[:, :width], x[:, width:]), by_rows, wait, held, put)
    out_copy(0).wait()
    out_copy(1).wait()


def narrow(by_rows, which, arrived, wait, held):
    per_half = arrived.shape[4] // CHUNK
    totals = [None, None]
    for i in range(held.shape[1]):
        left = arrived[:, i // per_half, which, :, pl.ds((i % per_half) * CHUNK, CHUNK)]
        left = left.reshape(left.shape[0] * left.shape[1], CHUNK)
        for part in range(2):
            wait(part, i)
            got = dot(left, held[part, i], ((1,), (0 if by_rows else 1,)))
            totals[part] = got if i == 0 else totals[part] + got
    return [total.astype(bf16) for total in totals]


def narrow_kernel(
    layer, by_rows, which, arrived, own, other, own_mate, other_mate, out_ref, held, sems, stage, out_sems
):
    wait = load_weights(layer, by_rows, ((own, other), (own_mate, other_mate)), held, sems)
    near, far = narrow(by_rows, which, arrived, wait, held)
    width = near.shape[1]
    stage[:, :width] = near
    stage[:, width:] = far
    copies = [
        pltpu.make_async_copy(stage, out_ref.at[i], out_sems.at[i]) for i in range(out_ref.shape[0])
    ]
    for copy in copies:
        copy.start()
    for copy in copies:
        copy.wait()


def narrow_last_kernel(
    layer, by_rows, arrived, own, other, own_mate, other_mate, beside, out_ref, held, sems, stage, out_sems
):
    wait = load_weights(layer, by_rows, ((own, other), (own_mate, other_mate)), held, sems)
    near, far = narrow(by_rows, 0, arrived, wait, held)
    width = near.shape[1]
    groups, _, tokens, _ = stage.shape
    stage[:, 0] = beside[...].reshape(groups, tokens, 2 * width)
    stage[:, 1, :, :width] = near.reshape(groups, tokens, width)
    stage[:, 1, :, width:] = far.reshape(groups, tokens, width)
    copies = [pltpu.make_async_copy(stage, out_ref.at[i], out_sems.at[i]) for i in range(2)]
    for copy in copies:
        copy.start()
    for copy in copies:
        copy.wait()


def held_scratch(weight, by_rows, parts):
    units = max(weight.shape)
    chunk = (CHUNK, weight.shape[1]) if by_rows else (weight.shape[0], CHUNK)
    return [
        pltpu.VMEM((parts, units // CHUNK) + chunk, bf16),
        pltpu.SemaphoreType.DMA((parts, units // CHUNK)),
    ]


def kernel_call(body, outs, out_specs, in_specs, scratch, operands, flops=0, moved=0):
    return pl.pallas_call(
        body,
        out_shape=outs,
        in_specs=in_specs,
        out_specs=out_specs,
        scratch_shapes=scratch,
        compiler_params=LIMIT,
        cost_estimate=pl.CostEstimate(flops=flops, bytes_accessed=moved, transcendentals=0),
    )(*operands)


def widen_first(layer, by_rows, x, weights, shape, dtype):
    return kernel_call(
        functools.partial(widen_first_kernel, layer, by_rows),
        shape_of(shape, dtype),
        HBM,
        [VMEM, HBM, HBM],
        held_scratch(weights[0], by_rows, 1) + [pltpu.VMEM(shape, dtype), pltpu.SemaphoreType.DMA((2,))],
        (x,) + weights[:2],
        flops=2 * x.shape[0] * weights[0].size,
        moved=2 * weights[0].size,
    )


def widen_next(layer, by_rows, arrived, base, weights, shape):
    return kernel_call(
        functools.partial(widen_next_kernel, layer, by_rows),
        (shape_of(shape), shape_of(base.shape)),
        (HBM, VMEM),
        [VMEM, VMEM] + [HBM] * 4,
        held_scratch(weights[0], by_rows, 2) + [pltpu.VMEM(shape, bf16), pltpu.SemaphoreType.DMA((2,))],
        (arrived, base) + weights,
        flops=4 * base.shape[0] * weights[0].size,
        moved=4 * weights[0].size,
    )


def narrow_next(layer, by_rows, which, arrived, weights, copies):
    tokens, width = arrived.shape[0] * arrived.shape[3], 2 * min(weights[0].shape)
    return kernel_call(
        functools.partial(narrow_kernel, layer, by_rows, which),
        shape_of((copies, tokens, width)),
        HBM,
        [VMEM] + [HBM] * 4,
        held_scratch(weights[0], by_rows, 2)
        + [pltpu.VMEM((tokens, width), bf16), pltpu.SemaphoreType.DMA((copies,))],
        (arrived,) + weights,
        flops=4 * tokens * weights[0].size,
        moved=4 * weights[0].size,
    )


def narrow_last(layer, by_rows, arrived, weights, beside):
    groups, tokens, width = arrived.shape[0], arrived.shape[3], 2 * min(weights[0].shape)
    return kernel_call(
        functools.partial(narrow_last_kernel, layer, by_rows),
        shape_of((2, groups, 2, tokens, width)),
        HBM,
        [VMEM] + [HBM] * 4 + [VMEM],
        held_scratch(weights[0], by_rows, 2)
        + [pltpu.VMEM((groups, 2, tokens, width), bf16), pltpu.SemaphoreType.DMA((2,))],
        (arrived,) + weights + (beside,),
        flops=4 * groups * tokens * weights[0].size,
        moved=4 * weights[0].size,
    )


def summed(ref, place):
    total = ref[0, :, place].astype(f32)
    for i in range(1, ref.shape[0]):
        total = total + ref[i, :, place].astype(f32)
    return total


def spread(stage, out_ref, sems):
    copies = [pltpu.make_async_copy(stage, out_ref.at[i], sems.at[i]) for i in range(out_ref.shape[0])]
    for copy in copies:
        copy.start()
    for copy in copies:
        copy.wait()


def act_first_kernel(arrived, out_ref, slope_ref, stage, sems):
    for at in range(0, arrived.shape[2], CHUNK):
        place = pl.ds(at, CHUNK)
        value, slope = gelu_both(summed(arrived, place))
        stage[0, :, place] = value.astype(bf16)
        slope_ref[:, place] = slope
    spread(stage, out_ref, sems)


def act_last_kernel(arrived, d_hid, out_ref, stage, sems):
    for at in range(0, arrived.shape[2], CHUNK):
        place = pl.ds(at, CHUNK)
        value, slope = gelu_both(summed(arrived, place))
        stage[0, :, place] = (d_hid[:, place] * slope).astype(bf16)
        stage[1, :, place] = value.astype(bf16)
    spread(stage, out_ref, sems)


def act_back_kernel(arrived, slope_ref, out_ref, stage, sems):
    for at in range(0, arrived.shape[2], CHUNK):
        place = pl.ds(at, CHUNK)
        stage[0, :, place] = (summed(arrived, place) * slope_ref[:, place]).astype(bf16)
    spread(stage, out_ref, sems)


def activation(body, kinds, peers, piece, operands, in_specs, slope=False):
    outs, out_specs = [shape_of((peers, kinds) + piece)], [HBM]
    if slope:
        outs, out_specs = outs + [shape_of(piece, f32)], out_specs + [VMEM]
    return kernel_call(
        body,
        outs,
        out_specs,
        in_specs,
        [pltpu.VMEM((kinds,) + piece, bf16), pltpu.SemaphoreType.DMA((peers,))],
        operands,
        flops=2000000,
        moved=2000000,
    )


def grad_down_kernel(*refs):
    lefts, right, out_ref = refs[:4], refs[4], refs[-1]
    left = jnp.concatenate([ref[...].reshape(-1, CHUNK) for ref in lefts])
    out_ref[...] = dot(left, right[...], ((0,), (0,)))


def grad_down(hids, grads):
    groups, halves, tokens, wide = hids[0].shape
    per_half, units, width = wide // CHUNK, halves * wide, grads.shape[1]
    block = pl.BlockSpec((groups, 1, tokens, CHUNK), lambda i: (0, i // per_half, 0, i % per_half))
    return pl.pallas_call(
        grad_down_kernel,
        out_shape=shape_of((units, width), f32),
        grid=(units // CHUNK,),
        in_specs=[block] * 4 + [pl.BlockSpec(grads.shape, lambda i: (0, 0))],
        out_specs=pl.BlockSpec((CHUNK, width), lambda i: (i, 0)),
        compiler_params=LIMIT,
        cost_estimate=pl.CostEstimate(
            flops=2 * grads.size * units, bytes_accessed=4 * width * units, transcendentals=0
        ),
    )(*hids, grads)


def grad_up_kernel(x_ref, *refs):
    choices, (out_ref, held, turned, sems) = (refs[:4], refs[4:8]), refs[8:]
    step = pl.program_id(0)
    section = lax.axis_index("section")

    def copy(choice, i):
        return pltpu.make_async_copy(choices[choice][i], held.at[i], sems.at[i])

    @pl.when(step == 0)
    def _():
        for choice in range(2):

            @pl.when(section == choice)
            def _():
                for i in range(4):
                    copy(choice, i).start()

        turned[...] = x_ref[...].T
        for i in range(4):
            copy(0, i).wait()

    per_half = held.shape[4] // CHUNK
    place = pl.ds(pl.multiple_of((step % per_half) * CHUNK, CHUNK), CHUNK)
    right = held[:, :, step // per_half, :, place]
    out_ref[...] = dot(turned[...], right.reshape(-1, CHUNK), ((1,), (0,)))


def grad_up(xs, layer0, layer1):
    groups, halves, tokens, wide = layer0[0].shape
    units, (all_tokens, width) = halves * wide, xs.shape
    return pl.pallas_call(
        grad_up_kernel,
        out_shape=shape_of((width, units), f32),
        grid=(units // CHUNK,),
        in_specs=[pl.BlockSpec(xs.shape, lambda i: (0, 0))] + [ANY] * 8,
        out_specs=pl.BlockSpec((width, CHUNK), lambda i: (0, i)),
        scratch_shapes=[
            pltpu.VMEM((4,) + layer0[0].shape, bf16),
            pltpu.VMEM((width, all_tokens), bf16),
            pltpu.SemaphoreType.DMA((4,)),
        ],
        compiler_params=LIMIT,
        cost_estimate=pl.CostEstimate(
            flops=2 * xs.size * units, bytes_accessed=4 * width * units, transcendentals=0
        ),
    )(xs, *layer0, *layer1)


def exchange(blocks, axes):
    return lax.all_to_all(blocks, axes, 0, 0)


CORES = ("section", "x_lo")


def to_other_core(block):
    return lax.ppermute(block, "section", [(0, 1), (1, 0)])


def to_mate(block):
    return lax.ppermute(block, "x_lo", [(0, 1), (1, 0)])


def to_other_core_of_mate(block):
    return lax.ppermute(block, CORES, [(0, 3), (3, 0), (1, 2), (2, 1)])


def only_to_mate(block, section):
    at = 2 * section
    return lax.ppermute(block, CORES, [(at, at + 1), (at + 1, at)])


def only_to_core(block, section):
    return lax.ppermute(block, "section", [(1 - section, section)])


def only_to_core_of_mate(block, section):
    at, source = 2 * section, 2 * (1 - section)
    return lax.ppermute(block, CORES, [(source, at + 1), (source + 1, at)])


def late(block, after):
    return lax.optimization_barrier((block, after))[0]


def local(inputs, cotangent, w_up, w_down):
    col = ("y", "x_hi")
    section, mate_pos, col_pos = (lax.axis_index(name) for name in ("section", "x_lo", col))
    first = section == 0
    own_up, own_down = w_up[0], w_down[0]
    tokens, width = inputs.shape[1:]
    half_len = tokens // 2
    rings = lax.axis_size("z")
    piece = (tokens // rings, own_up.shape[1] // 2)
    blocks = (half_len // piece[0], 2) + piece
    wide_blocks = (blocks[0], 2, 2) + piece

    def half_of(array, which):
        return lax.dynamic_slice_in_dim(array, which * half_len, half_len, 0)

    def batch(array, which):
        return lax.dynamic_index_in_dim(array, which, 0, keepdims=False)

    def both_widths(array):
        return jnp.concatenate([half_of(array, mate_pos), to_mate(half_of(array, 1 - mate_pos))], axis=1)

    x0, g2 = batch(inputs, section), batch(cotangent, section)
    other_up = to_other_core(own_up)
    other_down = to_other_core(own_down)

    x0_both, g2_both = both_widths(x0), both_widths(g2)
    mate_down0 = only_to_mate(late(own_down, (x0_both, g2_both)), 0)
    mate_up1 = only_to_mate(late(own_up, (x0_both, g2_both)), 1)

    arrived = widen_first(0, False, x0, (own_up, other_up), wide_blocks, bf16)
    g2 = late(g2, arrived)
    arrived = exchange(arrived.reshape((2 * rings,) + piece), ("z", "x_lo"))
    d_hid1 = widen_first(1, True, g2, (own_down, other_down), wide_blocks, f32)
    d_hid1 = lax.psum_scatter(
        d_hid1.reshape(2 * tokens, piece[1]), ("z", "x_lo"), scatter_dimension=0, tiled=True
    )
    value0, slope0 = activation(act_first_kernel, 1, rings, piece, (arrived,), [VMEM], slope=True)
    mate_down0 = late(mate_down0, value0)
    down0 = own_down, other_down, mate_down0, only_to_core(mate_down0, 1)
    hid0 = exchange(value0, "z").reshape(blocks[:2] + (1,) + piece)
    part = narrow_next(0, True, 0, hid0, down0, lax.axis_size(col))
    mate_up1 = late(mate_up1, part)
    up1 = own_up, other_up, mate_up1, only_to_core(mate_up1, 0)
    mate_down1 = only_to_mate(late(own_down, down0[3]), 1)
    mate_up0 = only_to_mate(late(own_up, up1[3]), 0)
    arrived = exchange(part, col)

    pre1, x1 = widen_next(1, False, arrived, x0_both, up1, blocks)
    arrived = exchange(pre1.reshape((rings,) + piece), "z")
    (acts1,) = activation(act_last_kernel, 2, rings, piece, (arrived, d_hid1), [VMEM, VMEM])
    acts1 = exchange(acts1, "z").reshape(blocks[:2] + (2,) + piece)
    part = narrow_next(1, False, 0, acts1, up1, lax.axis_size(col))
    mate_down1 = late(mate_down1, part)
    down1 = own_down, other_down, mate_down1, only_to_core(mate_down1, 0)
    arrived = exchange(part, col)

    d_hid0, g1 = widen_next(0, True, arrived, g2_both, down0, blocks)
    hid0, acts1, mate_up0, x1, g1 = late((hid0, acts1, mate_up0, x1, g1), d_hid0)
    up0 = own_up, other_up, mate_up0, only_to_core(mate_up0, 1)
    arrived = exchange(d_hid0.reshape((rings,) + piece), "z")
    x2_part = narrow_next(1, True, 1, acts1, down1, 1)
    (d_pre0,) = activation(act_back_kernel, 1, rings, piece, late((arrived, slope0), x2_part), [VMEM, VMEM])
    after_act = d_pre0
    d_pre0 = exchange(d_pre0, "z").reshape(blocks[:2] + (1,) + piece)

    hid0, d_pre1, hid1 = hid0[:, :, 0], acts1[:, :, 0], acts1[:, :, 1]
    kept, given = jnp.where(first, hid0, hid1), jnp.where(first, hid1, hid0)
    hids = kept, to_other_core(given), to_mate(kept), to_other_core_of_mate(given)
    near, far = slice(None, width), slice(width, None)
    traded = (
        jnp.where(first, g1[:, near], x1[:, near]),
        to_other_core(jnp.where(first, x1[:, near], g1[:, near])),
        to_mate(jnp.where(first, g1[:, far], x1[:, far])),
        to_other_core_of_mate(jnp.where(first, x1[:, far], g1[:, far])),
    )

    def all_tokens(array):
        return [
            half_of(batch(array, which), half)
            for half in (mate_pos, 1 - mate_pos)
            for which in (section, 1 - section)
        ]

    traded = jnp.concatenate(traded)
    xs = jnp.where(first, jnp.concatenate(all_tokens(inputs)), traded)
    gs = jnp.where(first, traded, jnp.concatenate(all_tokens(cotangent)))
    down_grad = grad_down(late(hids, after_act), gs)

    out = narrow_last(0, False, late(d_pre0, down_grad), up0, x2_part[0])
    arrived = exchange(out.reshape((lax.axis_size(col),) + out.shape[2:]), col)

    d_pre0 = d_pre0[:, :, 0]

    def gathered(array, section):
        return (
            array,
            only_to_core(array, section),
            only_to_mate(array, section),
            only_to_core_of_mate(array, section),
        )

    up_grad = grad_up(xs, gathered(d_pre0, 0), gathered(d_pre1, 1))

    out_len = out.shape[3]
    here = col_pos // blocks[0] == mate_pos
    x1, g1 = (lax.dynamic_slice_in_dim(a, (col_pos % blocks[0]) * out_len, out_len, 0) for a in (x1, g1))
    ended = jnp.sum(arrived.astype(f32), axis=0)
    x2 = (x1.astype(f32) + ended[0]).astype(bf16)
    g0 = (g1.astype(f32) + ended[1]).astype(bf16)
    layer0, layer1 = jnp.stack([x1, g0]), jnp.stack([x2, g1])
    kept, given = jnp.where(first, layer0, layer1), jnp.where(first, layer1, layer0)
    kept, given = (
        jnp.where(here, kept[..., near], to_mate(kept[..., far])),
        jnp.where(here, to_other_core(given[..., near]), to_other_core_of_mate(given[..., far])),
    )
    states, grads = (
        jnp.where(first, jnp.stack([kept[i], given[i]]), jnp.stack([given[i], kept[i]]))[None] for i in (0, 1)
    )
    return states, grads, up_grad[None], down_grad[None]


def solution(mesh):
    sections, rows, cols = mesh.devices.shape
    finer = Mesh(
        mesh.devices.reshape(sections, rows // 2, 2, cols // 2, 2),
        ("section", "z", "x_lo", "y", "x_hi"),
    )
    row, col = ("z", "x_lo"), ("y", "x_hi")
    in_specs = (
        P(None, None, row),
        P(None, None, row),
        P("section", row, col),
        P("section", col, row),
    )
    out_specs = (
        P("section", None, col, row),
        P("section", None, col, row),
        P("section", row, col),
        P("section", col, row),
    )
    return jax.shard_map(local, mesh=finer, in_specs=in_specs, out_specs=out_specs, check_vma=False)
```

```python
import functools

import jax
import jax.numpy as jnp
from jax import lax
from jax.experimental import pallas as pl
from jax.experimental.pallas import tpu as pltpu
from jax.sharding import Mesh, PartitionSpec as P

root_two_over_pi = 0.7978845608028654
cubic = 0.044715
f32 = jnp.float32
bf16 = jnp.bfloat16
CHUNK = 512
VMEM = pl.BlockSpec(memory_space=pltpu.VMEM)
HBM = pl.BlockSpec(memory_space=pltpu.HBM)
ANY = pl.BlockSpec(memory_space=pl.ANY)
LIMIT = pltpu.CompilerParams(vmem_limit_bytes=64 * 1024 * 1024)


def gelu_both(pre):
    inner = root_two_over_pi * (pre + cubic * pre * pre * pre)
    tangent = jnp.tanh(inner)
    value = 0.5 * pre * (1.0 + tangent)
    slope = 0.5 * (1.0 + tangent) + 0.5 * pre * (1.0 - tangent * tangent) * root_two_over_pi * (
        1.0 + 3.0 * cubic * pre * pre
    )
    return value, slope


def dot(left, right, dims):
    return lax.dot_general(left, right, (dims, ((), ())), preferred_element_type=f32)


def shape_of(shape, dtype=bf16):
    return jax.ShapeDtypeStruct(shape, dtype)


def load_weights(layer, by_rows, refs, held, sems):
    mine = lax.axis_index("section") == layer

    def copy(source, part, i):
        where = pl.ds(i * CHUNK, CHUNK)
        block = source.at[where, :] if by_rows else source.at[:, where]
        return pltpu.make_async_copy(block, held.at[part, i], sems.at[part, i])

    def start(which):
        for i in range(held.shape[1]):
            for part, pair in enumerate(refs):
                copy(pair[which], part, i).start()

    pl.when(mine)(lambda: start(0))
    pl.when(jnp.logical_not(mine))(lambda: start(1))
    return lambda part, i: copy(refs[part][0], part, i).wait()


def widen(xs, by_rows, wait, held, put):
    for i in range(held.shape[1]):
        total = None
        for part, x in enumerate(xs):
            wait(part, i)
            got = dot(x, held[part, i], ((1,), (1 if by_rows else 0,)))
            total = got if total is None else total + got
        put(i, total)


def widen_first_kernel(layer, by_rows, mate_at, x_ref, own, other, out_ref, held, sems, stage, out_sems):
    wait = load_weights(layer, by_rows, ((own, other),), held, sems)
    groups, tokens, wide = stage.shape[1 if mate_at == 0 else 0], stage.shape[3], stage.shape[4]
    per_half = wide // CHUNK

    def out_copy(half):
        where = (slice(None),) * (2 if mate_at == 0 else 1) + (half,)
        return pltpu.make_async_copy(stage.at[where], out_ref.at[where], out_sems.at[half])

    def put(i, total):
        half, place = i // per_half, pl.ds((i % per_half) * CHUNK, CHUNK)
        total = total.astype(bf16).reshape(2, groups, tokens, CHUNK)
        for mate in range(2):
            if mate_at == 0:
                stage[mate, :, half, :, place] = total[mate]
            else:
                stage[:, half, mate, :, place] = total[mate]
        if i % per_half == per_half - 1:
            out_copy(half).start()

    widen((x_ref[...],), by_rows, wait, held, put)
    out_copy(0).wait()
    out_copy(1).wait()


def widen_next_kernel(layer, by_rows, riders, arrived, base, own, other, own_mate, other_mate, *rest):
    out_ref, x_out, held, sems, stage, out_sems = rest[riders:]
    wait = load_weights(layer, by_rows, ((own, other), (own_mate, other_mate)), held, sems)
    copies = [
        pltpu.make_async_copy(rest[i], out_ref.at[:, :, 1 + i], out_sems.at[2 + i]) for i in range(riders)
    ]
    for copy in copies:
        copy.start()
    width, per_half = base.shape[1] // 2, stage.shape[3] // CHUNK
    total = arrived[0].astype(f32)
    for i in range(1, arrived.shape[0]):
        total = total + arrived[i].astype(f32)
    x = (base[...].astype(f32) + total).astype(bf16)
    x_out[...] = x

    def out_copy(half):
        return pltpu.make_async_copy(stage.at[:, half], out_ref.at[:, half, 0], out_sems.at[half])

    def put(i, total):
        half, at = i // per_half, (i % per_half) * CHUNK
        stage[:, half, :, pl.ds(at, CHUNK)] = total.astype(bf16).reshape(stage.shape[0], stage.shape[2], CHUNK)
        if i % per_half == per_half - 1:
            out_copy(half).start()

    widen((x[:, :width], x[:, width:]), by_rows, wait, held, put)
    for copy in [out_copy(0), out_copy(1)] + copies:
        copy.wait()


def narrow(by_rows, which, arrived, wait, held):
    per_half = arrived.shape[4] // CHUNK
    totals = [None, None]
    for i in range(held.shape[1]):
        left = arrived[:, i // per_half, which, :, pl.ds((i % per_half) * CHUNK, CHUNK)]
        left = left.reshape(left.shape[0] * left.shape[1], CHUNK)
        for part in range(2):
            wait(part, i)
            got = dot(left, held[part, i], ((1,), (0 if by_rows else 1,)))
            totals[part] = got if i == 0 else totals[part] + got
    return [total.astype(bf16) for total in totals]


def narrow_kernel(
    layer, by_rows, which, arrived, own, other, own_mate, other_mate, out_ref, held, sems, stage, out_sems
):
    wait = load_weights(layer, by_rows, ((own, other), (own_mate, other_mate)), held, sems)
    near, far = narrow(by_rows, which, arrived, wait, held)
    width = near.shape[1]
    stage[:, :width] = near
    stage[:, width:] = far
    copies = [
        pltpu.make_async_copy(stage, out_ref.at[i], out_sems.at[i]) for i in range(out_ref.shape[0])
    ]
    for copy in copies:
        copy.start()
    for copy in copies:
        copy.wait()


def held_scratch(weight, by_rows, parts):
    units = max(weight.shape)
    chunk = (CHUNK, weight.shape[1]) if by_rows else (weight.shape[0], CHUNK)
    return [
        pltpu.VMEM((parts, units // CHUNK) + chunk, bf16),
        pltpu.SemaphoreType.DMA((parts, units // CHUNK)),
    ]


def kernel_call(body, outs, out_specs, in_specs, scratch, operands, flops=0, moved=0):
    return pl.pallas_call(
        body,
        out_shape=outs,
        in_specs=in_specs,
        out_specs=out_specs,
        scratch_shapes=scratch,
        compiler_params=LIMIT,
        cost_estimate=pl.CostEstimate(flops=flops, bytes_accessed=moved, transcendentals=0),
    )(*operands)


def widen_first(layer, by_rows, mate_at, x, weights, blocks):
    shape = blocks[:mate_at] + (2,) + blocks[mate_at:]
    return kernel_call(
        functools.partial(widen_first_kernel, layer, by_rows, mate_at),
        shape_of(shape),
        HBM,
        [VMEM, HBM, HBM],
        held_scratch(weights[0], by_rows, 1) + [pltpu.VMEM(shape, bf16), pltpu.SemaphoreType.DMA((2,))],
        (x,) + weights[:2],
        flops=2 * x.shape[0] * weights[0].size,
        moved=2 * weights[0].size,
    )


def widen_next(layer, by_rows, arrived, base, weights, blocks, riders=()):
    return kernel_call(
        functools.partial(widen_next_kernel, layer, by_rows, len(riders)),
        (shape_of(blocks[:2] + (1 + len(riders),) + blocks[2:]), shape_of(base.shape)),
        (HBM, VMEM),
        [VMEM, VMEM] + [HBM] * (4 + len(riders)),
        held_scratch(weights[0], by_rows, 2)
        + [pltpu.VMEM(blocks, bf16), pltpu.SemaphoreType.DMA((2 + len(riders),))],
        (arrived, base) + weights + riders,
        flops=4 * base.shape[0] * weights[0].size,
        moved=4 * weights[0].size,
    )


def narrow_next(layer, by_rows, which, arrived, weights, copies):
    tokens, width = arrived.shape[0] * arrived.shape[3], 2 * min(weights[0].shape)
    return kernel_call(
        functools.partial(narrow_kernel, layer, by_rows, which),
        shape_of((copies, tokens, width)),
        HBM,
        [VMEM] + [HBM] * 4,
        held_scratch(weights[0], by_rows, 2)
        + [pltpu.VMEM((tokens, width), bf16), pltpu.SemaphoreType.DMA((copies,))],
        (arrived,) + weights,
        flops=4 * tokens * weights[0].size,
        moved=4 * weights[0].size,
    )


def summed(ref, kind, place):
    total = ref[0, kind, :, place].astype(f32)
    for i in range(1, ref.shape[0]):
        total = total + ref[i, kind, :, place].astype(f32)
    return total


def spread(stage, out_ref, sems):
    copies = [pltpu.make_async_copy(stage, out_ref.at[i], sems.at[i]) for i in range(out_ref.shape[0])]
    for copy in copies:
        copy.start()
    for copy in copies:
        copy.wait()


def act_first_kernel(arrived, out_ref, slope_ref, stage, sems):
    for at in range(0, arrived.shape[3], CHUNK):
        place = pl.ds(at, CHUNK)
        value, slope = gelu_both(summed(arrived, 0, place))
        stage[0, :, place] = value.astype(bf16)
        slope_ref[:, place] = slope
    spread(stage, out_ref, sems)


def act_last_kernel(arrived, out_ref, stage, sems):
    for at in range(0, arrived.shape[3], CHUNK):
        place = pl.ds(at, CHUNK)
        value, slope = gelu_both(summed(arrived, 0, place))
        stage[0, :, place] = (summed(arrived, 1, place) * slope).astype(bf16)
        stage[1, :, place] = value.astype(bf16)
    spread(stage, out_ref, sems)


def act_back_kernel(arrived, slope_ref, out_ref, stage, sems):
    for at in range(0, arrived.shape[3], CHUNK):
        place = pl.ds(at, CHUNK)
        stage[0, :, place] = (summed(arrived, 0, place) * slope_ref[:, place]).astype(bf16)
    spread(stage, out_ref, sems)


def activation(body, kinds, peers, piece, operands, in_specs, slope=False):
    outs, out_specs = [shape_of((peers, kinds) + piece)], [HBM]
    if slope:
        outs, out_specs = outs + [shape_of(piece, f32)], out_specs + [VMEM]
    return kernel_call(
        body,
        outs,
        out_specs,
        in_specs,
        [pltpu.VMEM((kinds,) + piece, bf16), pltpu.SemaphoreType.DMA((peers,))],
        operands,
        flops=2000000,
        moved=2000000,
    )


def pick_copies(layer0, layer1, kind, held, sems, start):
    section = lax.axis_index("section")

    def copy(layer, i):
        source = (layer0, layer1)[layer][i].at[:, :, 0 if layer == 0 else kind]
        return pltpu.make_async_copy(source, held.at[i], sems.at[i])

    if start:
        for layer in range(2):

            @pl.when(section == layer)
            def _():
                for i in range(4):
                    copy(layer, i).start()
    else:
        for i in range(4):
            copy(0, i).wait()


def step_chunk(held, step):
    per_half = held.shape[4] // CHUNK
    place = pl.ds(pl.multiple_of((step % per_half) * CHUNK, CHUNK), CHUNK)
    return held[:, :, step // per_half, :, place].reshape(-1, CHUNK)


def grad_down_kernel(g_ref, *refs):
    layer0, layer1, (out_ref, held, sems) = refs[:4], refs[4:8], refs[8:]
    step = pl.program_id(0)

    @pl.when(step == 0)
    def _():
        pick_copies(layer0, layer1, 1, held, sems, True)
        pick_copies(layer0, layer1, 1, held, sems, False)

    out_ref[...] = dot(step_chunk(held, step), g_ref[...], ((0,), (0,)))


def grad_up_kernel(x_ref, *refs):
    layer0, layer1, (out_ref, held, turned, sems) = refs[:4], refs[4:8], refs[8:]
    step = pl.program_id(0)

    @pl.when(step == 0)
    def _():
        pick_copies(layer0, layer1, 0, held, sems, True)
        turned[...] = x_ref[...].T
        pick_copies(layer0, layer1, 0, held, sems, False)

    out_ref[...] = dot(turned[...], step_chunk(held, step), ((1,), (0,)))


def weight_grad(down, narrow, layer0, layer1):
    groups, halves, _, tokens, wide = layer0[0].shape
    units, (all_tokens, width) = halves * wide, narrow.shape
    shape, block = ((units, width), (CHUNK, width)) if down else ((width, units), (width, CHUNK))
    turned = [] if down else [pltpu.VMEM((width, all_tokens), bf16)]
    return pl.pallas_call(
        grad_down_kernel if down else grad_up_kernel,
        out_shape=shape_of(shape, f32),
        grid=(units // CHUNK,),
        in_specs=[pl.BlockSpec(narrow.shape, lambda i: (0, 0))] + [HBM] * 8,
        out_specs=pl.BlockSpec(block, lambda i: (i, 0) if down else (0, i)),
        scratch_shapes=[pltpu.VMEM((4, groups, halves, tokens, wide), bf16)]
        + turned
        + [pltpu.SemaphoreType.DMA((4,))],
        compiler_params=LIMIT,
        cost_estimate=pl.CostEstimate(
            flops=2 * narrow.size * units, bytes_accessed=4 * width * units, transcendentals=0
        ),
    )(narrow, *layer0, *layer1)


def last_kernel(up, down, *refs):
    layer0, layer1, rest = refs[:4], refs[4:8], refs[8:]
    out_ref, held, up_held, down_held, stage, sems, up_sems, down_sems, out_sem = rest
    section, mate_pos = lax.axis_index("section"), lax.axis_index("x_lo")
    groups, halves, tokens, wide = held.shape[1:]
    per_half, count = wide // CHUNK, up_held.shape[0]
    pick_copies(layer0, layer1, 1, held, sems, True)

    def run(weight, by_rows, weight_held, weight_sems):
        copies = []
        for i in range(count):
            where = pl.ds(i * CHUNK, CHUNK)
            source = weight.at[where, :] if by_rows else weight.at[:, where]
            copies.append(pltpu.make_async_copy(source, weight_held.at[i], weight_sems.at[i]))
        for copy in copies:
            copy.start()
        pick_copies(layer0, layer1, 1, held, sems, False)
        total = None
        for i in range(count):
            left = held[:, :, i // per_half, :, pl.ds((i % per_half) * CHUNK, CHUNK)].reshape(-1, CHUNK)
            copies[i].wait()
            got = dot(left, weight_held[i], ((1,), (0 if by_rows else 1,)))
            total = got if total is None else total + got
        total = total.astype(bf16).reshape(4, groups, tokens, -1)
        for i in range(4):
            half = mate_pos if i < 2 else 1 - mate_pos
            which = section if i % 2 == 0 else 1 - section
            stage[pl.ds(half * groups, groups), which] = total[i]

    pl.when(section == 0)(lambda: run(up, False, up_held, up_sems))
    pl.when(section == 1)(lambda: run(down, True, down_held, down_sems))
    copy = pltpu.make_async_copy(stage, out_ref, out_sem)
    copy.start()
    copy.wait()


def last_product(up, down, layer0, layer1):
    groups, halves, _, tokens, wide = layer0[0].shape
    width, units = up.shape
    out = (2 * groups, 2, tokens, width)
    return kernel_call(
        last_kernel,
        shape_of(out),
        HBM,
        [HBM] * 10,
        [
            pltpu.VMEM((4, groups, halves, tokens, wide), bf16),
            pltpu.VMEM((units // CHUNK, width, CHUNK), bf16),
            pltpu.VMEM((units // CHUNK, CHUNK, width), bf16),
            pltpu.VMEM(out, bf16),
            pltpu.SemaphoreType.DMA((4,)),
            pltpu.SemaphoreType.DMA((units // CHUNK,)),
            pltpu.SemaphoreType.DMA((units // CHUNK,)),
            pltpu.SemaphoreType.DMA,
        ],
        (up, down) + layer0 + layer1,
        flops=8 * groups * tokens * up.size,
        moved=6 * up.size,
    )


def exchange(blocks, axes):
    return lax.all_to_all(blocks, axes, 0, 0)


CORES = ("section", "x_lo")


def to_other_core(block):
    return lax.ppermute(block, "section", [(0, 1), (1, 0)])


def to_mate(block):
    return lax.ppermute(block, "x_lo", [(0, 1), (1, 0)])


def to_other_core_of_mate(block):
    return lax.ppermute(block, CORES, [(0, 3), (3, 0), (1, 2), (2, 1)])


def only_to_mate(block, section):
    at = 2 * section
    return lax.ppermute(block, CORES, [(at, at + 1), (at + 1, at)])


def only_to_core(block, section):
    return lax.ppermute(block, "section", [(1 - section, section)])


def to_owner(block, section):
    at, source = 2 * section, 2 * (1 - section)
    across = lax.ppermute(block, CORES, [(source, at + 1), (source + 1, at)])
    return block, only_to_core(block, section), only_to_mate(block, section), across


def late(block, after):
    return lax.optimization_barrier((block, after))[0]


def local(inputs, cotangent, w_up, w_down):
    col = ("y", "x_hi")
    section, mate_pos, col_pos = (lax.axis_index(name) for name in ("section", "x_lo", col))
    first = section == 0
    own_up, own_down = w_up[0], w_down[0]
    tokens, width = inputs.shape[1:]
    half_len = tokens // 2
    rings = lax.axis_size("z")
    piece = (tokens // rings, own_up.shape[1] // 2)
    blocks = (half_len // piece[0], 2) + piece

    def half_of(array, which):
        return lax.dynamic_slice_in_dim(array, which * half_len, half_len, 0)

    def batch(array, which):
        return lax.dynamic_index_in_dim(array, which, 0, keepdims=False)

    def both_widths(array):
        return jnp.concatenate([half_of(array, mate_pos), to_mate(half_of(array, 1 - mate_pos))], axis=1)

    x0, g2 = batch(inputs, section), batch(cotangent, section)
    other_up = to_other_core(own_up)
    first_part = widen_first(0, False, 2, x0, (own_up, other_up), blocks)
    mate_down0 = only_to_mate(late(own_down, other_up), 0)
    arrived = exchange(first_part.reshape((2 * rings, 1) + piece), ("z", "x_lo"))

    other_down = to_other_core(late(own_down, other_up))
    d_hid1 = widen_first(1, True, 0, late(g2, first_part), (own_down, other_down), blocks)
    arrived, mate_down0 = late((arrived, mate_down0), d_hid1)
    d_hid1, given = batch(d_hid1, mate_pos), to_mate(batch(d_hid1, 1 - mate_pos))
    down0 = own_down, other_down, mate_down0, only_to_core(mate_down0, 1)

    value0, slope0 = activation(act_first_kernel, 1, rings, piece, (arrived,), [VMEM], slope=True)
    mate_up1 = only_to_mate(late(own_up, value0), 1)
    hid0 = exchange(value0, "z").reshape(blocks[:2] + (1,) + piece)
    x0_both, g2_both = (both_widths(late(array, value0)) for array in (x0, g2))
    d_hid1 = (d_hid1.astype(f32) + late(given, value0).astype(f32)).astype(bf16)
    hid0 = late(hid0, d_hid1)
    part = narrow_next(0, True, 0, hid0, down0, lax.axis_size(col))
    mate_up1, x0_both, g2_both = late((mate_up1, x0_both, g2_both), part)
    up1 = own_up, other_up, mate_up1, only_to_core(mate_up1, 0)
    arrived = exchange(part, col)

    pre1, x1 = widen_next(1, False, arrived, x0_both, up1, blocks, (d_hid1,))
    hid0s = to_owner(late(hid0, pre1), 0)
    arrived = exchange(pre1.reshape((rings, 2) + piece), "z")
    (acts1,) = activation(act_last_kernel, 2, rings, piece, (arrived,), [VMEM])
    acts1 = late(exchange(acts1, "z").reshape(blocks[:2] + (2,) + piece), hid0s)
    part = narrow_next(1, False, 0, acts1, up1, lax.axis_size(col))
    arrived = exchange(part, col)

    d_hid0, g1 = widen_next(0, True, arrived, g2_both, down0, blocks)
    acts1, both1 = late((acts1, jnp.stack([x1, g1])), d_hid0)
    acts1s = to_owner(acts1, 1)
    arrived = exchange(d_hid0.reshape((rings, 1) + piece), "z")
    near, far = both1[..., :width], both1[..., width:]
    both1 = jnp.stack([near, to_other_core(near), to_mate(far), to_other_core_of_mate(far)])
    both1 = both1.reshape((2, 2) + near.shape)

    def all_tokens(array):
        return jnp.concatenate(
            [
                half_of(batch(array, which), half)
                for half in (mate_pos, 1 - mate_pos)
                for which in (section, 1 - section)
            ]
        )

    x1s, g1s = both1[:, :, 0].reshape(2 * tokens, width), both1[:, :, 1].reshape(2 * tokens, width)
    xs = jnp.where(first, all_tokens(inputs), x1s)
    gs = jnp.where(first, g1s, all_tokens(cotangent))

    (d_pre0,) = activation(act_back_kernel, 1, rings, piece, (arrived, slope0), [VMEM, VMEM])
    d_pre0 = late(exchange(d_pre0, "z").reshape(blocks[:2] + (1,) + piece), acts1s)
    down_grad = weight_grad(True, late(gs, d_pre0), hid0s, acts1s)
    d_pre0s = late(to_owner(d_pre0, 0), down_grad)

    last = last_product(own_up, own_down, d_pre0s, acts1s)
    xs, d_pre0s = late((xs, d_pre0s), last)
    arrived = exchange(last, col)
    up_grad = weight_grad(False, xs, d_pre0s, acts1s)

    out_len = tokens // lax.axis_size(col)
    per_half = half_len // out_len
    away = jnp.where(col_pos // per_half == mate_pos, 0, 1)
    pieces = lax.dynamic_index_in_dim(both1, away, 0, keepdims=False)
    pieces = lax.dynamic_slice_in_dim(pieces, (col_pos % per_half) * out_len, out_len, 2)
    pieces = jnp.where(first, pieces, pieces[::-1])
    x1, g1 = pieces[:, 0], pieces[:, 1]
    ended = jnp.sum(arrived.astype(f32), axis=0)
    ended = (jnp.where(first, g1, x1).astype(f32) + ended).astype(bf16)
    states, grads = jnp.where(first, x1, ended), jnp.where(first, ended, g1)
    return states[None], grads[None], up_grad[None], down_grad[None]


def solution(mesh):
    sections, rows, cols = mesh.devices.shape
    finer = Mesh(
        mesh.devices.reshape(sections, rows // 2, 2, cols // 2, 2),
        ("section", "z", "x_lo", "y", "x_hi"),
    )
    row, col = ("z", "x_lo"), ("y", "x_hi")
    in_specs = (
        P(None, None, row),
        P(None, None, row),
        P("section", row, col),
        P("section", col, row),
    )
    out_specs = (
        P("section", None, col, row),
        P("section", None, col, row),
        P("section", row, col),
        P("section", col, row),
    )
    return jax.shard_map(local, mesh=finer, in_specs=in_specs, out_specs=out_specs, check_vma=False)
```

```python
import functools

import jax
import jax.numpy as jnp
from jax import lax
from jax.experimental import pallas as pl
from jax.experimental.pallas import tpu as pltpu
from jax.sharding import Mesh, PartitionSpec as P

root_two_over_pi = 0.7978845608028654
cubic = 0.044715
f32 = jnp.float32
bf16 = jnp.bfloat16
CHUNK = 512
VMEM = pl.BlockSpec(memory_space=pltpu.VMEM)
HBM = pl.BlockSpec(memory_space=pltpu.HBM)
ANY = pl.BlockSpec(memory_space=pl.ANY)
LIMIT = pltpu.CompilerParams(vmem_limit_bytes=64 * 1024 * 1024)


def gelu_both(pre):
    inner = root_two_over_pi * (pre + cubic * pre * pre * pre)
    tangent = jnp.tanh(inner)
    value = 0.5 * pre * (1.0 + tangent)
    slope = 0.5 * (1.0 + tangent) + 0.5 * pre * (1.0 - tangent * tangent) * root_two_over_pi * (
        1.0 + 3.0 * cubic * pre * pre
    )
    return value, slope


def dot(left, right, dims):
    return lax.dot_general(left, right, (dims, ((), ())), preferred_element_type=f32)


def shape_of(shape, dtype=bf16):
    return jax.ShapeDtypeStruct(shape, dtype)


def load_weights(layer, by_rows, refs, held, sems):
    mine = lax.axis_index("section") == layer

    def copy(source, part, i):
        units = pl.ds(i * CHUNK, CHUNK)
        if by_rows:
            width = source.shape[1]
            block, place = source.at[units, :], held.at[i, :, pl.ds(part * width, width)]
        else:
            width = source.shape[0]
            block, place = source.at[:, units], held.at[i, pl.ds(part * width, width), :]
        return pltpu.make_async_copy(block, place, sems.at[part, i])

    def start(which):
        for i in range(held.shape[0]):
            for part, pair in enumerate(refs):
                copy(pair[which], part, i).start()

    pl.when(mine)(lambda: start(0))
    pl.when(jnp.logical_not(mine))(lambda: start(1))

    def wait(i):
        for part, pair in enumerate(refs):
            copy(pair[0], part, i).wait()

    return wait


def wait_all(copies):
    for copy in copies:
        copy.wait()


def start_kernel(x_ref, g_ref, up, down, *rest):
    outs, (up_held, down_held, stage, up_sems, down_sems, out_sems) = rest[:4], rest[4:]
    section, mate_pos = lax.axis_index("section"), lax.axis_index("x_lo")
    groups, tokens, wide = stage.shape[1], stage.shape[3], stage.shape[4]
    per_half, count = wide // CHUNK, up_held.shape[0]

    def out_copies(half):
        return [
            pltpu.make_async_copy(stage.at[i, :, half], outs[i].at[:, half], out_sems.at[half, i])
            for i in range(4)
        ]

    def run(left_ref, weight, by_rows, held, sems):
        copies = []
        for i in range(count):
            units = pl.ds(i * CHUNK, CHUNK)
            source = weight.at[units, :] if by_rows else weight.at[:, units]
            copies.append(pltpu.make_async_copy(source, held.at[i], sems.at[i]))
            copies[-1].start()
        left = left_ref[...].reshape(-1, left_ref.shape[2])
        for i in range(count):
            half, place = i // per_half, pl.ds((i % per_half) * CHUNK, CHUNK)
            copies[i].wait()
            total = dot(left, held[i], ((1,), (1 if by_rows else 0,))).astype(bf16)
            total = total.reshape(2, 2, groups, tokens, CHUNK)
            for which in range(2):
                for token_half in range(2):
                    away = jnp.where(token_half == mate_pos, 0, 2) + jnp.where(which == section, 0, 1)
                    stage[away, :, half, :, place] = total[which, token_half]
            if i % per_half == per_half - 1:
                for copy in out_copies(half):
                    copy.start()
        wait_all(out_copies(0) + out_copies(1))

    pl.when(section == 0)(lambda: run(x_ref, up, False, up_held, up_sems))
    pl.when(section == 1)(lambda: run(g_ref, down, True, down_held, down_sems))


def start_products(x, g, up, down, blocks):
    width, units = up.shape
    count = units // CHUNK
    return kernel_call(
        start_kernel,
        [shape_of(blocks)] * 4,
        [HBM] * 4,
        [VMEM, VMEM, HBM, HBM],
        [
            pltpu.VMEM((count, width, CHUNK), bf16),
            pltpu.VMEM((count, CHUNK, width), bf16),
            pltpu.VMEM((4,) + blocks, bf16),
            pltpu.SemaphoreType.DMA((count,)),
            pltpu.SemaphoreType.DMA((count,)),
            pltpu.SemaphoreType.DMA((2, 4)),
        ],
        (x, g, up, down),
        flops=2 * x.shape[0] * x.shape[1] * up.size,
        moved=4 * up.size,
    )


def add_kernel(layer, kept, mates, other, across, out_ref, held, sems):
    mine = lax.axis_index("section") == layer

    def copies(refs):
        return [pltpu.make_async_copy(ref, held.at[i], sems.at[i]) for i, ref in enumerate(refs)]

    @pl.when(mine)
    def _():
        for copy in copies((kept, mates)):
            copy.start()

    @pl.when(jnp.logical_not(mine))
    def _():
        for copy in copies((other, across)):
            copy.start()

    wait_all(copies((kept, mates)))
    held[0] = (held[0].astype(f32) + held[1].astype(f32)).astype(bf16)
    copy = pltpu.make_async_copy(held.at[0], out_ref, sems.at[2])
    copy.start()
    copy.wait()


def add_terms(layer, terms):
    shape = terms[0].shape
    return kernel_call(
        functools.partial(add_kernel, layer),
        shape_of(shape),
        HBM,
        [HBM] * 4,
        [pltpu.VMEM((2,) + shape, bf16), pltpu.SemaphoreType.DMA((3,))],
        terms,
        flops=terms[0].size,
        moved=6 * terms[0].size,
    )


def widen_kernel(layer, by_rows, riders, arrived_ref, base, own, other, own_mate, other_mate, *rest):
    out_ref, x_out, held, sems, stage, out_sems, arrived, in_sems = rest[riders:]
    arrival = pltpu.make_async_copy(arrived_ref, arrived, in_sems.at[0])
    arrival.start()
    wait = load_weights(layer, by_rows, ((own, other), (own_mate, other_mate)), held, sems)
    rides = [
        pltpu.make_async_copy(rest[i], stage.at[:, :, 1 + i], in_sems.at[1 + i]) for i in range(riders)
    ]
    for copy in rides:
        copy.start()
    per_half = stage.shape[4] // CHUNK
    arrival.wait()
    total = arrived[0].astype(f32)
    for i in range(1, arrived.shape[0]):
        total = total + arrived[i].astype(f32)
    x = (base[...].astype(f32) + total).astype(bf16)
    x_out[...] = x
    wait_all(rides)

    def out_copy(half):
        return pltpu.make_async_copy(stage.at[:, half], out_ref.at[:, half], out_sems.at[half])

    for i in range(held.shape[0]):
        half, place = i // per_half, pl.ds((i % per_half) * CHUNK, CHUNK)
        wait(i)
        got = dot(x, held[i], ((1,), (1 if by_rows else 0,))).astype(bf16)
        stage[:, half, 0, :, place] = got.reshape(stage.shape[0], stage.shape[3], CHUNK)
        if i % per_half == per_half - 1:
            out_copy(half).start()
    wait_all([out_copy(0), out_copy(1)])


def narrow_kernel(
    layer, by_rows, arrived_ref, own, other, own_mate, other_mate, out_ref, held, sems, stage, out_sems, arrived, in_sem
):
    arrival = pltpu.make_async_copy(arrived_ref.at[:, :, 0], arrived, in_sem)
    arrival.start()
    wait = load_weights(layer, by_rows, ((own, other), (own_mate, other_mate)), held, sems)
    per_half = arrived.shape[3] // CHUNK
    total = None
    arrival.wait()
    for i in range(held.shape[0]):
        left = arrived[:, i // per_half, :, pl.ds((i % per_half) * CHUNK, CHUNK)].reshape(-1, CHUNK)
        wait(i)
        got = dot(left, held[i], ((1,), (0 if by_rows else 1,)))
        total = got if total is None else total + got
    stage[...] = total.astype(bf16)
    copies = [
        pltpu.make_async_copy(stage, out_ref.at[i], out_sems.at[i]) for i in range(out_ref.shape[0])
    ]
    for copy in copies:
        copy.start()
    wait_all(copies)


def held_scratch(weight, by_rows):
    count, width = max(weight.shape) // CHUNK, 2 * min(weight.shape)
    chunk = (CHUNK, width) if by_rows else (width, CHUNK)
    return [pltpu.VMEM((count,) + chunk, bf16), pltpu.SemaphoreType.DMA((2, count))]


def kernel_call(body, outs, out_specs, in_specs, scratch, operands, flops=0, moved=0):
    return pl.pallas_call(
        body,
        out_shape=outs,
        in_specs=in_specs,
        out_specs=out_specs,
        scratch_shapes=scratch,
        compiler_params=LIMIT,
        cost_estimate=pl.CostEstimate(flops=flops, bytes_accessed=moved, transcendentals=0),
    )(*operands)


def widen(layer, by_rows, arrived, base, weights, blocks, riders=()):
    shape = blocks[:2] + (1 + len(riders),) + blocks[2:]
    return kernel_call(
        functools.partial(widen_kernel, layer, by_rows, len(riders)),
        (shape_of(shape), shape_of(base.shape)),
        (HBM, VMEM),
        [HBM, VMEM] + [HBM] * (4 + len(riders)),
        held_scratch(weights[0], by_rows)
        + [
            pltpu.VMEM(shape, bf16),
            pltpu.SemaphoreType.DMA((2,)),
            pltpu.VMEM(arrived.shape, bf16),
            pltpu.SemaphoreType.DMA((1 + len(riders),)),
        ],
        (arrived, base) + weights + riders,
        flops=4 * base.shape[0] * weights[0].size,
        moved=4 * weights[0].size,
    )


def narrow(layer, by_rows, arrived, weights, copies):
    groups, halves, _, tokens, wide = arrived.shape
    out = groups * tokens, 2 * min(weights[0].shape)
    return kernel_call(
        functools.partial(narrow_kernel, layer, by_rows),
        shape_of((copies,) + out),
        HBM,
        [HBM] * 5,
        held_scratch(weights[0], by_rows)
        + [
            pltpu.VMEM(out, bf16),
            pltpu.SemaphoreType.DMA((copies,)),
            pltpu.VMEM((groups, halves, tokens, wide), bf16),
            pltpu.SemaphoreType.DMA,
        ],
        (arrived,) + weights,
        flops=4 * out[0] * weights[0].size,
        moved=4 * weights[0].size,
    )


def act_kernel(body, slopes, arrived_ref, *refs):
    slope_in, rest = (refs[0], refs[1:]) if slopes == "in" else (None, refs)
    out_ref, rest = rest[0], rest[1:]
    slope_out, rest = (rest[0], rest[1:]) if slopes == "out" else (None, rest)
    arrived, stage, in_sems, out_sems = rest
    steps = arrived.shape[3] // CHUNK
    places = [pl.ds(i * CHUNK, CHUNK) for i in range(steps)]
    arrivals = [
        pltpu.make_async_copy(arrived_ref.at[:, :, :, place], arrived.at[:, :, :, place], in_sems.at[i])
        for i, place in enumerate(places)
    ]
    for copy in arrivals:
        copy.start()
    copies = []
    for i, place in enumerate(places):
        arrivals[i].wait()
        sums = []
        for kind in range(arrived.shape[1]):
            total = arrived[0, kind, :, place].astype(f32)
            for source in range(1, arrived.shape[0]):
                total = total + arrived[source, kind, :, place].astype(f32)
            sums.append(total)
        values, slope = body(sums, None if slope_in is None else slope_in[:, place])
        for kind, value in enumerate(values):
            stage[kind, :, place] = value.astype(bf16)
        if slope_out is not None:
            slope_out[:, place] = slope
        for to in range(out_ref.shape[0]):
            copies.append(
                pltpu.make_async_copy(stage.at[:, :, place], out_ref.at[to, :, :, place], out_sems.at[i, to])
            )
            copies[-1].start()
    wait_all(copies)


def act_first(sums, _):
    value, slope = gelu_both(sums[0])
    return [value], slope


def act_last(sums, _):
    value, slope = gelu_both(sums[0])
    return [sums[1] * slope, value], None


def act_back(sums, slope):
    return [sums[0] * slope], None


def activation(body, arrived, kinds, slope_out=False, slope=None):
    peers, piece = arrived.shape[0], arrived.shape[2:]
    outs, out_specs, slopes = [shape_of((peers, kinds) + piece)], [HBM], "in" if slope is not None else ""
    if slope_out:
        outs, out_specs, slopes = outs + [shape_of(piece, f32)], out_specs + [VMEM], "out"
    steps = piece[1] // CHUNK
    return kernel_call(
        functools.partial(act_kernel, body, slopes),
        outs,
        out_specs,
        [HBM] + ([VMEM] if slope is not None else []),
        [
            pltpu.VMEM(arrived.shape, bf16),
            pltpu.VMEM((kinds,) + piece, bf16),
            pltpu.SemaphoreType.DMA((steps,)),
            pltpu.SemaphoreType.DMA((steps, peers)),
        ],
        (arrived,) + (() if slope is None else (slope,)),
        flops=2000000,
        moved=2000000,
    )


def finish_kernel(arrived, x1, g1, states, grads):
    total = arrived[0].astype(f32)
    for i in range(1, arrived.shape[0]):
        total = total + arrived[i].astype(f32)

    def ended(base):
        return (base[...].astype(f32) + total).astype(bf16)

    @pl.when(lax.axis_index("section") == 0)
    def _():
        states[...] = x1[...]
        grads[...] = ended(g1)

    @pl.when(lax.axis_index("section") == 1)
    def _():
        states[...] = ended(x1)
        grads[...] = g1[...]


def pick_copies(layer0, layer1, kind, held, sems, start):
    section = lax.axis_index("section")

    def copy(layer, i):
        source = (layer0, layer1)[layer][i].at[:, :, 0 if layer == 0 else kind]
        return pltpu.make_async_copy(source, held.at[i], sems.at[i])

    if start:
        for layer in range(2):

            @pl.when(section == layer)
            def _():
                for i in range(4):
                    copy(layer, i).start()
    else:
        for i in range(4):
            copy(0, i).wait()


def step_chunk(held, step):
    per_half = held.shape[4] // CHUNK
    place = pl.ds(pl.multiple_of((step % per_half) * CHUNK, CHUNK), CHUNK)
    return held[:, :, step // per_half, :, place].reshape(-1, CHUNK)


def grad_down_kernel(g_ref, *refs):
    layer0, layer1, (out_ref, held, sems) = refs[:4], refs[4:8], refs[8:]
    step = pl.program_id(0)

    @pl.when(step == 0)
    def _():
        pick_copies(layer0, layer1, 1, held, sems, True)
        pick_copies(layer0, layer1, 1, held, sems, False)

    out_ref[...] = dot(step_chunk(held, step), g_ref[...], ((0,), (0,)))


def grad_up_kernel(x_ref, *refs):
    layer0, layer1, (out_ref, held, turned, sems) = refs[:4], refs[4:8], refs[8:]
    step = pl.program_id(0)

    @pl.when(step == 0)
    def _():
        pick_copies(layer0, layer1, 0, held, sems, True)
        turned[...] = x_ref[...].T
        pick_copies(layer0, layer1, 0, held, sems, False)

    out_ref[...] = dot(turned[...], step_chunk(held, step), ((1,), (0,)))


def weight_grad(down, narrow, layer0, layer1):
    groups, halves, _, tokens, wide = layer0[0].shape
    units, (all_tokens, width) = halves * wide, narrow.shape
    shape, block = ((units, width), (CHUNK, width)) if down else ((width, units), (width, CHUNK))
    turned = [] if down else [pltpu.VMEM((width, all_tokens), bf16)]
    return pl.pallas_call(
        grad_down_kernel if down else grad_up_kernel,
        out_shape=shape_of(shape, f32),
        grid=(units // CHUNK,),
        in_specs=[pl.BlockSpec(narrow.shape, lambda i: (0, 0))] + [HBM] * 8,
        out_specs=pl.BlockSpec(block, lambda i: (i, 0) if down else (0, i)),
        scratch_shapes=[pltpu.VMEM((4, groups, halves, tokens, wide), bf16)]
        + turned
        + [pltpu.SemaphoreType.DMA((4,))],
        compiler_params=LIMIT,
        cost_estimate=pl.CostEstimate(
            flops=2 * narrow.size * units, bytes_accessed=4 * width * units, transcendentals=0
        ),
    )(narrow, *layer0, *layer1)


def last_kernel(up, down, *refs):
    layer0, layer1, rest = refs[:4], refs[4:8], refs[8:]
    out_ref, held, up_held, down_held, stage, sems, up_sems, down_sems, out_sem = rest
    section, mate_pos = lax.axis_index("section"), lax.axis_index("x_lo")
    groups, halves, tokens, wide = held.shape[1:]
    per_half, count = wide // CHUNK, up_held.shape[0]
    pick_copies(layer0, layer1, 1, held, sems, True)

    def run(weight, by_rows, weight_held, weight_sems):
        copies = []
        for i in range(count):
            where = pl.ds(i * CHUNK, CHUNK)
            source = weight.at[where, :] if by_rows else weight.at[:, where]
            copies.append(pltpu.make_async_copy(source, weight_held.at[i], weight_sems.at[i]))
        for copy in copies:
            copy.start()
        pick_copies(layer0, layer1, 1, held, sems, False)
        total = None
        for i in range(count):
            left = held[:, :, i // per_half, :, pl.ds((i % per_half) * CHUNK, CHUNK)].reshape(-1, CHUNK)
            copies[i].wait()
            got = dot(left, weight_held[i], ((1,), (0 if by_rows else 1,)))
            total = got if total is None else total + got
        total = total.astype(bf16).reshape(4, groups, tokens, -1)
        for i in range(4):
            half = mate_pos if i < 2 else 1 - mate_pos
            which = section if i % 2 == 0 else 1 - section
            stage[pl.ds(half * groups, groups), which] = total[i]

    pl.when(section == 0)(lambda: run(up, False, up_held, up_sems))
    pl.when(section == 1)(lambda: run(down, True, down_held, down_sems))
    copy = pltpu.make_async_copy(stage, out_ref, out_sem)
    copy.start()
    copy.wait()


def last_product(up, down, layer0, layer1):
    groups, halves, _, tokens, wide = layer0[0].shape
    width, units = up.shape
    out = (2 * groups, 2, tokens, width)
    return kernel_call(
        last_kernel,
        shape_of(out),
        HBM,
        [HBM] * 10,
        [
            pltpu.VMEM((4, groups, halves, tokens, wide), bf16),
            pltpu.VMEM((units // CHUNK, width, CHUNK), bf16),
            pltpu.VMEM((units // CHUNK, CHUNK, width), bf16),
            pltpu.VMEM(out, bf16),
            pltpu.SemaphoreType.DMA((4,)),
            pltpu.SemaphoreType.DMA((units // CHUNK,)),
            pltpu.SemaphoreType.DMA((units // CHUNK,)),
            pltpu.SemaphoreType.DMA,
        ],
        (up, down) + layer0 + layer1,
        flops=8 * groups * tokens * up.size,
        moved=6 * up.size,
    )


def exchange(blocks, axes):
    return lax.all_to_all(blocks, axes, 0, 0)


CORES = ("section", "x_lo")


def to_other_core(block):
    return lax.ppermute(block, "section", [(0, 1), (1, 0)])


def to_mate(block):
    return lax.ppermute(block, "x_lo", [(0, 1), (1, 0)])


def to_other_core_of_mate(block):
    return lax.ppermute(block, CORES, [(0, 3), (3, 0), (1, 2), (2, 1)])


def only_to_mate(block, section):
    at = 2 * section
    return lax.ppermute(block, CORES, [(at, at + 1), (at + 1, at)])


def only_to_core(block, section):
    return lax.ppermute(block, "section", [(1 - section, section)])


def only_across(block, section):
    at, source = 2 * section, 2 * (1 - section)
    return lax.ppermute(block, CORES, [(source, at + 1), (source + 1, at)])


def to_owner(block, section):
    return block, only_to_core(block, section), only_to_mate(block, section), only_across(block, section)


def late(block, after):
    return lax.optimization_barrier((block, after))[0]


def local(inputs, cotangent, w_up, w_down):
    col = ("y", "x_hi")
    section, mate_pos, col_pos = (lax.axis_index(name) for name in ("section", "x_lo", col))
    first = section == 0
    own_up, own_down = w_up[0], w_down[0]
    tokens, width = inputs.shape[1:]
    half_len = tokens // 2
    rings = lax.axis_size("z")
    piece = (tokens // rings, own_up.shape[1] // 2)
    blocks = (half_len // piece[0], 2) + piece

    def half_of(array, which):
        return lax.dynamic_slice_in_dim(array, which * half_len, half_len, 0)

    def batch(array, which):
        return lax.dynamic_index_in_dim(array, which, 0, keepdims=False)

    def halves_of(pair, which):
        return lax.dynamic_slice_in_dim(pair, which * half_len, half_len, 1)

    keep_own, keep_other, send_own, send_other = start_products(inputs, cotangent, own_up, own_down, blocks)
    terms = (
        keep_own,
        only_to_mate(send_own, 0),
        only_to_core(keep_other, 1),
        only_across(send_other, 1),
    )
    x0, g2 = late((inputs, cotangent), keep_own)
    ends = jnp.stack([batch(x0, section), batch(g2, section)])
    ends_mate = to_mate(halves_of(ends, 1 - mate_pos))
    pre0 = add_terms(0, terms)
    arrived = exchange(pre0.reshape((rings, 1) + piece), "z")
    own_down_late, own_up_late = late((own_down, own_up), (pre0, ends_mate))
    mate_down0 = only_to_mate(own_down_late, 0)
    other_down = only_to_core(own_down_late, 1)
    other_up = only_to_core(own_up_late, 0)

    value0, slope0 = activation(act_first, arrived, 1, slope_out=True)
    hid0 = exchange(value0, "z").reshape(blocks[:2] + (1,) + piece)
    ends, ends_mate = late((halves_of(ends, mate_pos), ends_mate), value0)
    g2_both = jnp.concatenate([ends[1], ends_mate[1]], axis=1)
    mate_down0 = late(mate_down0, g2_both)
    down0 = own_down, other_down, mate_down0, only_to_core(mate_down0, 1)
    mate_up1 = only_to_mate(late(own_up, mate_down0), 1)
    part = narrow(0, True, hid0, down0, lax.axis_size(col))
    arrived = exchange(part, col)

    ends, ends_mate = late((ends, ends_mate), part)
    x0_both = jnp.concatenate([ends[0], ends_mate[0]], axis=1)
    mate_up1 = late(mate_up1, x0_both)
    up1 = own_up, other_up, mate_up1, only_to_core(mate_up1, 0)
    keep_own, keep_other, send_own, send_other = late((keep_own, keep_other, send_own, send_other), mate_up1)
    d_hid1 = add_terms(
        1,
        (keep_own, only_to_mate(send_own, 1), only_to_core(keep_other, 0), only_across(send_other, 0)),
    )
    pre1, x1 = widen(1, False, arrived, x0_both, up1, blocks, (d_hid1,))
    hid0s = to_owner(late(hid0, pre1), 0)
    arrived = late(exchange(pre1.reshape((rings, 2) + piece), "z"), hid0s)
    (acts1,) = activation(act_last, arrived, 2)
    acts1 = exchange(acts1, "z").reshape(blocks[:2] + (2,) + piece)
    part = narrow(1, False, acts1, up1, lax.axis_size(col))
    arrived = exchange(part, col)

    d_hid0, g1 = widen(0, True, arrived, g2_both, down0, blocks)
    acts1, both1 = late((acts1, jnp.stack([x1, g1])), d_hid0)
    acts1s = to_owner(acts1, 1)
    arrived = exchange(d_hid0.reshape((rings, 1) + piece), "z")
    near, far = both1[..., :width], both1[..., width:]
    both1 = jnp.stack([near, to_other_core(near), to_mate(far), to_other_core_of_mate(far)])
    both1 = both1.reshape((2, 2) + near.shape)

    def all_tokens(array):
        return jnp.concatenate(
            [
                half_of(batch(array, which), half)
                for half in (mate_pos, 1 - mate_pos)
                for which in (section, 1 - section)
            ]
        )

    x1s, g1s = both1[:, :, 0].reshape(2 * tokens, width), both1[:, :, 1].reshape(2 * tokens, width)
    xs = jnp.where(first, all_tokens(inputs), x1s)
    gs = jnp.where(first, g1s, all_tokens(cotangent))

    (d_pre0,) = activation(act_back, arrived, 1, slope=slope0)
    d_pre0 = late(exchange(d_pre0, "z").reshape(blocks[:2] + (1,) + piece), acts1s)
    down_grad = weight_grad(True, late(gs, d_pre0), hid0s, acts1s)
    d_pre0s = late(to_owner(d_pre0, 0), down_grad)

    last = last_product(own_up, own_down, d_pre0s, acts1s)
    xs, d_pre0s = late((xs, d_pre0s), last)
    arrived = exchange(last, col)
    up_grad = weight_grad(False, xs, d_pre0s, acts1s)

    out_len = tokens // lax.axis_size(col)
    per_half = half_len // out_len
    away = jnp.where(col_pos // per_half == mate_pos, 0, 1)
    pieces = lax.dynamic_index_in_dim(both1, away, 0, keepdims=False)
    pieces = lax.dynamic_slice_in_dim(pieces, (col_pos % per_half) * out_len, out_len, 2)
    pieces = jnp.where(first, pieces, pieces[::-1])
    states, grads = kernel_call(
        finish_kernel,
        [shape_of(pieces[:, 0].shape)] * 2,
        [VMEM] * 2,
        [VMEM] * 3,
        [],
        (arrived, pieces[:, 0], pieces[:, 1]),
        flops=100000,
        moved=200000,
    )
    return states[None], grads[None], up_grad[None], down_grad[None]


def solution(mesh):
    sections, rows, cols = mesh.devices.shape
    finer = Mesh(
        mesh.devices.reshape(sections, rows // 2, 2, cols // 2, 2),
        ("section", "z", "x_lo", "y", "x_hi"),
    )
    row, col = ("z", "x_lo"), ("y", "x_hi")
    in_specs = (
        P(None, None, row),
        P(None, None, row),
        P("section", row, col),
        P("section", col, row),
    )
    out_specs = (
        P("section", None, col, row),
        P("section", None, col, row),
        P("section", row, col),
        P("section", col, row),
    )
    return jax.shard_map(local, mesh=finer, in_specs=in_specs, out_specs=out_specs, check_vma=False)
```

```python
import functools

import jax
import jax.numpy as jnp
from jax import lax
from jax.experimental import pallas as pl
from jax.experimental.pallas import tpu as pltpu
from jax.sharding import Mesh, PartitionSpec as P

root_two_over_pi = 0.7978845608028654
cubic = 0.044715
f32 = jnp.float32
bf16 = jnp.bfloat16
CHUNK = 512
VMEM = pl.BlockSpec(memory_space=pltpu.VMEM)
HBM = pl.BlockSpec(memory_space=pltpu.HBM)
ANY = pl.BlockSpec(memory_space=pl.ANY)
LIMIT = pltpu.CompilerParams(vmem_limit_bytes=64 * 1024 * 1024)


def gelu_both(pre):
    inner = root_two_over_pi * (pre + cubic * pre * pre * pre)
    tangent = jnp.tanh(inner)
    value = 0.5 * pre * (1.0 + tangent)
    slope = 0.5 * (1.0 + tangent) + 0.5 * pre * (1.0 - tangent * tangent) * root_two_over_pi * (
        1.0 + 3.0 * cubic * pre * pre
    )
    return value, slope


def dot(left, right, dims):
    return lax.dot_general(left, right, (dims, ((), ())), preferred_element_type=f32)


def shape_of(shape, dtype=bf16):
    return jax.ShapeDtypeStruct(shape, dtype)


def load_weights(layer, by_rows, refs, held, sems):
    mine = lax.axis_index("section") == layer

    def copy(source, part, i):
        units = pl.ds(i * CHUNK, CHUNK)
        if by_rows:
            width = source.shape[1]
            block, place = source.at[units, :], held.at[i, :, pl.ds(part * width, width)]
        else:
            width = source.shape[0]
            block, place = source.at[:, units], held.at[i, pl.ds(part * width, width), :]
        return pltpu.make_async_copy(block, place, sems.at[part, i])

    def start(which):
        for i in range(held.shape[0]):
            for part, pair in enumerate(refs):
                copy(pair[which], part, i).start()

    pl.when(mine)(lambda: start(0))
    pl.when(jnp.logical_not(mine))(lambda: start(1))

    def wait(i):
        for part, pair in enumerate(refs):
            copy(pair[0], part, i).wait()

    return wait


def wait_all(copies):
    for copy in copies:
        copy.wait()


def start_kernel(x_ref, g_ref, up, down, *rest):
    outs, (up_held, down_held, stage, up_sems, down_sems, out_sems) = rest[:4], rest[4:]
    section, mate_pos = lax.axis_index("section"), lax.axis_index("x_lo")
    groups, tokens, wide = stage.shape[1], stage.shape[3], stage.shape[4]
    per_half, count = wide // CHUNK, up_held.shape[0]

    def out_copies(half):
        return [
            pltpu.make_async_copy(stage.at[i, :, half], outs[i].at[:, half], out_sems.at[half, i])
            for i in range(4)
        ]

    def run(left_ref, weight, by_rows, held, sems):
        copies = []
        for i in range(count):
            units = pl.ds(i * CHUNK, CHUNK)
            source = weight.at[units, :] if by_rows else weight.at[:, units]
            copies.append(pltpu.make_async_copy(source, held.at[i], sems.at[i]))
            copies[-1].start()
        left = left_ref[...].reshape(-1, left_ref.shape[2])
        for i in range(count):
            half, place = i // per_half, pl.ds((i % per_half) * CHUNK, CHUNK)
            copies[i].wait()
            total = dot(left, held[i], ((1,), (1 if by_rows else 0,))).astype(bf16)
            total = total.reshape(2, 2, groups, tokens, CHUNK)
            for which in range(2):
                for token_half in range(2):
                    away = jnp.where(token_half == mate_pos, 0, 2) + jnp.where(which == section, 0, 1)
                    stage[away, :, half, :, place] = total[which, token_half]
            if i % per_half == per_half - 1:
                for copy in out_copies(half):
                    copy.start()
        wait_all(out_copies(0) + out_copies(1))

    pl.when(section == 0)(lambda: run(x_ref, up, False, up_held, up_sems))
    pl.when(section == 1)(lambda: run(g_ref, down, True, down_held, down_sems))


def start_products(x, g, up, down, blocks):
    width, units = up.shape
    count = units // CHUNK
    return kernel_call(
        start_kernel,
        [shape_of(blocks)] * 4,
        [HBM] * 4,
        [VMEM, VMEM, HBM, HBM],
        [
            pltpu.VMEM((count, width, CHUNK), bf16),
            pltpu.VMEM((count, CHUNK, width), bf16),
            pltpu.VMEM((4,) + blocks, bf16),
            pltpu.SemaphoreType.DMA((count,)),
            pltpu.SemaphoreType.DMA((count,)),
            pltpu.SemaphoreType.DMA((2, 4)),
        ],
        (x, g, up, down),
        flops=2 * x.shape[0] * x.shape[1] * up.size,
        moved=4 * up.size,
    )


def add_kernel(kept, mates, other, across, out_ref, held, sems):
    section = lax.axis_index("section")
    copies = [
        pltpu.make_async_copy(ref, held.at[i], sems.at[i]) for i, ref in enumerate((kept, mates, other, across))
    ]
    for copy in copies:
        copy.start()
    outs = []
    for i, kind in enumerate((section, 1 - section)):
        copies[2 * i].wait()
        copies[2 * i + 1].wait()
        held[2 * i] = (held[2 * i].astype(f32) + held[2 * i + 1].astype(f32)).astype(bf16)
        outs.append(pltpu.make_async_copy(held.at[2 * i], out_ref.at[:, :, kind], sems.at[4 + i]))
        outs[-1].start()
    wait_all(outs)


def add_terms(terms):
    shape = terms[0].shape
    return kernel_call(
        add_kernel,
        shape_of(shape[:2] + (2,) + shape[2:]),
        HBM,
        [HBM] * 4,
        [pltpu.VMEM((4,) + shape, bf16), pltpu.SemaphoreType.DMA((6,))],
        terms,
        flops=2 * terms[0].size,
        moved=12 * terms[0].size,
    )


def widen_kernel(layer, by_rows, kind, arrived_ref, base, base_mate, own, other, own_mate, other_mate, *rest):
    out_ref, x_out, held, sems, stage, out_sems, arrived, in_sem = rest
    arrival = pltpu.make_async_copy(arrived_ref, arrived, in_sem)
    arrival.start()
    wait = load_weights(layer, by_rows, ((own, other), (own_mate, other_mate)), held, sems)
    per_half = stage.shape[3] // CHUNK
    arrival.wait()
    total = arrived[0].astype(f32)
    for i in range(1, arrived.shape[0]):
        total = total + arrived[i].astype(f32)
    x = jnp.concatenate([base[kind], base_mate[kind]], axis=1)
    x = (x.astype(f32) + total).astype(bf16)
    x_out[...] = x

    def out_copy(half):
        return pltpu.make_async_copy(stage.at[:, half], out_ref.at[:, half], out_sems.at[half])

    for i in range(held.shape[0]):
        half, place = i // per_half, pl.ds((i % per_half) * CHUNK, CHUNK)
        wait(i)
        got = dot(x, held[i], ((1,), (1 if by_rows else 0,))).astype(bf16)
        stage[:, half, :, place] = got.reshape(stage.shape[0], stage.shape[2], CHUNK)
        if i % per_half == per_half - 1:
            out_copy(half).start()
    wait_all([out_copy(0), out_copy(1)])


def narrow_kernel(
    layer, by_rows, arrived_ref, own, other, own_mate, other_mate, out_ref, held, sems, stage, out_sems, arrived, in_sem
):
    arrival = pltpu.make_async_copy(arrived_ref.at[:, :, 0], arrived, in_sem)
    arrival.start()
    wait = load_weights(layer, by_rows, ((own, other), (own_mate, other_mate)), held, sems)
    per_half = arrived.shape[3] // CHUNK
    total = None
    arrival.wait()
    for i in range(held.shape[0]):
        left = arrived[:, i // per_half, :, pl.ds((i % per_half) * CHUNK, CHUNK)].reshape(-1, CHUNK)
        wait(i)
        got = dot(left, held[i], ((1,), (0 if by_rows else 1,)))
        total = got if total is None else total + got
    stage[...] = total.astype(bf16)
    copies = [
        pltpu.make_async_copy(stage, out_ref.at[i], out_sems.at[i]) for i in range(out_ref.shape[0])
    ]
    for copy in copies:
        copy.start()
    wait_all(copies)


def held_scratch(weight, by_rows):
    count, width = max(weight.shape) // CHUNK, 2 * min(weight.shape)
    chunk = (CHUNK, width) if by_rows else (width, CHUNK)
    return [pltpu.VMEM((count,) + chunk, bf16), pltpu.SemaphoreType.DMA((2, count))]


def kernel_call(body, outs, out_specs, in_specs, scratch, operands, flops=0, moved=0):
    return pl.pallas_call(
        body,
        out_shape=outs,
        in_specs=in_specs,
        out_specs=out_specs,
        scratch_shapes=scratch,
        compiler_params=LIMIT,
        cost_estimate=pl.CostEstimate(flops=flops, bytes_accessed=moved, transcendentals=0),
    )(*operands)


def widen(layer, by_rows, arrived, kind, bases, weights, blocks):
    return kernel_call(
        functools.partial(widen_kernel, layer, by_rows, kind),
        (shape_of(blocks), shape_of(arrived.shape[1:])),
        (HBM, VMEM),
        [HBM, VMEM, VMEM] + [HBM] * 4,
        held_scratch(weights[0], by_rows)
        + [
            pltpu.VMEM(blocks, bf16),
            pltpu.SemaphoreType.DMA((2,)),
            pltpu.VMEM(arrived.shape, bf16),
            pltpu.SemaphoreType.DMA,
        ],
        (arrived,) + bases + weights,
        flops=4 * arrived.shape[1] * weights[0].size,
        moved=4 * weights[0].size,
    )


def narrow(layer, by_rows, arrived, weights, copies):
    groups, halves, _, tokens, wide = arrived.shape
    out = groups * tokens, 2 * min(weights[0].shape)
    return kernel_call(
        functools.partial(narrow_kernel, layer, by_rows),
        shape_of((copies,) + out),
        HBM,
        [HBM] * 5,
        held_scratch(weights[0], by_rows)
        + [
            pltpu.VMEM(out, bf16),
            pltpu.SemaphoreType.DMA((copies,)),
            pltpu.VMEM((groups, halves, tokens, wide), bf16),
            pltpu.SemaphoreType.DMA,
        ],
        (arrived,) + weights,
        flops=4 * out[0] * weights[0].size,
        moved=4 * weights[0].size,
    )


def act_kernel(body, ins, outs, arrived_ref, *refs):
    in_refs, out_ref, out_refs = refs[:ins], refs[ins], refs[ins + 1 : ins + 1 + outs]
    arrived, stage, in_sems, out_sems = refs[ins + 1 + outs :]
    steps = arrived.shape[3] // CHUNK
    places = [pl.ds(i * CHUNK, CHUNK) for i in range(steps)]
    arrivals = [
        pltpu.make_async_copy(arrived_ref.at[:, :, :, place], arrived.at[:, :, :, place], in_sems.at[i])
        for i, place in enumerate(places)
    ]
    for copy in arrivals:
        copy.start()
    copies = []
    for i, place in enumerate(places):
        arrivals[i].wait()
        sums = []
        for kind in range(arrived.shape[1]):
            total = arrived[0, kind, :, place].astype(f32)
            for source in range(1, arrived.shape[0]):
                total = total + arrived[source, kind, :, place].astype(f32)
            sums.append(total)
        spread, kept = body(sums, [ref[:, place] for ref in in_refs])
        for kind, value in enumerate(spread):
            stage[kind, :, place] = value.astype(bf16)
        for ref, value in zip(out_refs, kept):
            ref[:, place] = value
        for to in range(out_ref.shape[0]):
            copies.append(
                pltpu.make_async_copy(stage.at[:, :, place], out_ref.at[to, :, :, place], out_sems.at[i, to])
            )
            copies[-1].start()
    wait_all(copies)


def act_first(sums, _):
    value, slope = gelu_both(sums[0])
    return [value], [slope, sums[1]]


def act_last(sums, ins):
    value, slope = gelu_both(sums[0])
    return [ins[0] * slope, value], []


def act_back(sums, ins):
    return [sums[0] * ins[0]], []


def activation(body, arrived, kinds, ins=(), outs=0):
    peers, piece = arrived.shape[0], arrived.shape[2:]
    steps = piece[1] // CHUNK
    return kernel_call(
        functools.partial(act_kernel, body, len(ins), outs),
        [shape_of((peers, kinds) + piece)] + [shape_of(piece, f32)] * outs,
        [HBM] + [VMEM] * outs,
        [HBM] + [VMEM] * len(ins),
        [
            pltpu.VMEM(arrived.shape, bf16),
            pltpu.VMEM((kinds,) + piece, bf16),
            pltpu.SemaphoreType.DMA((steps,)),
            pltpu.SemaphoreType.DMA((steps, peers)),
        ],
        (arrived,) + tuple(ins),
        flops=2000000,
        moved=2000000,
    )


def finish_kernel(arrived, x1, g1, states, grads):
    total = arrived[0].astype(f32)
    for i in range(1, arrived.shape[0]):
        total = total + arrived[i].astype(f32)

    def ended(base):
        return (base[...].astype(f32) + total).astype(bf16)

    @pl.when(lax.axis_index("section") == 0)
    def _():
        states[...] = x1[...]
        grads[...] = ended(g1)

    @pl.when(lax.axis_index("section") == 1)
    def _():
        states[...] = ended(x1)
        grads[...] = g1[...]


def pick_copies(layer0, layer1, kind, held, sems, start):
    section = lax.axis_index("section")

    def copy(layer, i):
        source = (layer0, layer1)[layer][i].at[:, :, 0 if layer == 0 else kind]
        return pltpu.make_async_copy(source, held.at[i], sems.at[i])

    if start:
        for layer in range(2):

            @pl.when(section == layer)
            def _():
                for i in range(4):
                    copy(layer, i).start()
    else:
        for i in range(4):
            copy(0, i).wait()


def step_chunk(held, step):
    per_half = held.shape[4] // CHUNK
    place = pl.ds(pl.multiple_of((step % per_half) * CHUNK, CHUNK), CHUNK)
    return held[:, :, step // per_half, :, place].reshape(-1, CHUNK)


def grad_down_kernel(g_ref, *refs):
    layer0, layer1, (out_ref, held, sems) = refs[:4], refs[4:8], refs[8:]
    step = pl.program_id(0)

    @pl.when(step == 0)
    def _():
        pick_copies(layer0, layer1, 1, held, sems, True)
        pick_copies(layer0, layer1, 1, held, sems, False)

    out_ref[...] = dot(step_chunk(held, step), g_ref[...], ((0,), (0,)))


def grad_up_kernel(x_ref, *refs):
    layer0, layer1, (out_ref, held, turned, sems) = refs[:4], refs[4:8], refs[8:]
    step = pl.program_id(0)

    @pl.when(step == 0)
    def _():
        pick_copies(layer0, layer1, 0, held, sems, True)
        turned[...] = x_ref[...].T
        pick_copies(layer0, layer1, 0, held, sems, False)

    out_ref[...] = dot(turned[...], step_chunk(held, step), ((1,), (0,)))


def weight_grad(down, narrow, layer0, layer1):
    groups, halves, _, tokens, wide = layer0[0].shape
    units, (all_tokens, width) = halves * wide, narrow.shape
    shape, block = ((units, width), (CHUNK, width)) if down else ((width, units), (width, CHUNK))
    turned = [] if down else [pltpu.VMEM((width, all_tokens), bf16)]
    return pl.pallas_call(
        grad_down_kernel if down else grad_up_kernel,
        out_shape=shape_of(shape, f32),
        grid=(units // CHUNK,),
        in_specs=[pl.BlockSpec(narrow.shape, lambda i: (0, 0))] + [HBM] * 8,
        out_specs=pl.BlockSpec(block, lambda i: (i, 0) if down else (0, i)),
        scratch_shapes=[pltpu.VMEM((4, groups, halves, tokens, wide), bf16)]
        + turned
        + [pltpu.SemaphoreType.DMA((4,))],
        compiler_params=LIMIT,
        cost_estimate=pl.CostEstimate(
            flops=2 * narrow.size * units, bytes_accessed=4 * width * units, transcendentals=0
        ),
    )(narrow, *layer0, *layer1)


def last_kernel(up, down, *refs):
    layer0, layer1, rest = refs[:4], refs[4:8], refs[8:]
    out_ref, held, up_held, down_held, stage, sems, up_sems, down_sems, out_sem = rest
    section, mate_pos = lax.axis_index("section"), lax.axis_index("x_lo")
    groups, halves, tokens, wide = held.shape[1:]
    per_half, count = wide // CHUNK, up_held.shape[0]
    pick_copies(layer0, layer1, 1, held, sems, True)

    def run(weight, by_rows, weight_held, weight_sems):
        copies = []
        for i in range(count):
            where = pl.ds(i * CHUNK, CHUNK)
            source = weight.at[where, :] if by_rows else weight.at[:, where]
            copies.append(pltpu.make_async_copy(source, weight_held.at[i], weight_sems.at[i]))
        for copy in copies:
            copy.start()
        pick_copies(layer0, layer1, 1, held, sems, False)
        total = None
        for i in range(count):
            left = held[:, :, i // per_half, :, pl.ds((i % per_half) * CHUNK, CHUNK)].reshape(-1, CHUNK)
            copies[i].wait()
            got = dot(left, weight_held[i], ((1,), (0 if by_rows else 1,)))
            total = got if total is None else total + got
        total = total.astype(bf16).reshape(4, groups, tokens, -1)
        for i in range(4):
            half = mate_pos if i < 2 else 1 - mate_pos
            which = section if i % 2 == 0 else 1 - section
            stage[pl.ds(half * groups, groups), which] = total[i]

    pl.when(section == 0)(lambda: run(up, False, up_held, up_sems))
    pl.when(section == 1)(lambda: run(down, True, down_held, down_sems))
    copy = pltpu.make_async_copy(stage, out_ref, out_sem)
    copy.start()
    copy.wait()


def last_product(up, down, layer0, layer1):
    groups, halves, _, tokens, wide = layer0[0].shape
    width, units = up.shape
    out = (2 * groups, 2, tokens, width)
    return kernel_call(
        last_kernel,
        shape_of(out),
        HBM,
        [HBM] * 10,
        [
            pltpu.VMEM((4, groups, halves, tokens, wide), bf16),
            pltpu.VMEM((units // CHUNK, width, CHUNK), bf16),
            pltpu.VMEM((units // CHUNK, CHUNK, width), bf16),
            pltpu.VMEM(out, bf16),
            pltpu.SemaphoreType.DMA((4,)),
            pltpu.SemaphoreType.DMA((units // CHUNK,)),
            pltpu.SemaphoreType.DMA((units // CHUNK,)),
            pltpu.SemaphoreType.DMA,
        ],
        (up, down) + layer0 + layer1,
        flops=8 * groups * tokens * up.size,
        moved=6 * up.size,
    )


def exchange(blocks, axes):
    return lax.all_to_all(blocks, axes, 0, 0)


CORES = ("section", "x_lo")


def to_other_core(block):
    return lax.ppermute(block, "section", [(0, 1), (1, 0)])


def to_mate(block):
    return lax.ppermute(block, "x_lo", [(0, 1), (1, 0)])


def to_other_core_of_mate(block):
    return lax.ppermute(block, CORES, [(0, 3), (3, 0), (1, 2), (2, 1)])


def only_to_mate(block, section):
    at = 2 * section
    return lax.ppermute(block, CORES, [(at, at + 1), (at + 1, at)])


def only_to_core(block, section):
    return lax.ppermute(block, "section", [(1 - section, section)])


def only_across(block, section):
    at, source = 2 * section, 2 * (1 - section)
    return lax.ppermute(block, CORES, [(source, at + 1), (source + 1, at)])


def to_owner(block, section):
    return block, only_to_core(block, section), only_to_mate(block, section), only_across(block, section)


def late(block, after):
    return lax.optimization_barrier((block, after))[0]


def local(inputs, cotangent, w_up, w_down):
    col = ("y", "x_hi")
    section, mate_pos, col_pos = (lax.axis_index(name) for name in ("section", "x_lo", col))
    first = section == 0
    own_up, own_down = w_up[0], w_down[0]
    tokens, width = inputs.shape[1:]
    half_len = tokens // 2
    rings = lax.axis_size("z")
    piece = (tokens // rings, own_up.shape[1] // 2)
    blocks = (half_len // piece[0], 2) + piece

    def half_of(array, which):
        return lax.dynamic_slice_in_dim(array, which * half_len, half_len, 0)

    def batch(array, which):
        return lax.dynamic_index_in_dim(array, which, 0, keepdims=False)

    def halves_of(pair, which):
        return lax.dynamic_slice_in_dim(pair, which * half_len, half_len, 1)

    keep_own, keep_other, send_own, send_other = start_products(inputs, cotangent, own_up, own_down, blocks)
    terms = keep_own, to_mate(send_own), to_other_core(keep_other), to_other_core_of_mate(send_other)
    own_down_late, own_up_late = late((own_down, own_up), keep_own)
    other_down, other_up = only_to_core(own_down_late, 1), only_to_core(own_up_late, 0)
    both = add_terms(late(terms, other_up))
    own_down_late, x0, g2 = late((own_down, inputs, cotangent), both)
    mate_down0 = only_to_mate(own_down_late, 0)
    arrived = exchange(both.reshape((rings, 2) + piece), "z")
    ends = jnp.stack([batch(x0, section), batch(g2, section)])
    bases = halves_of(ends, mate_pos), to_mate(halves_of(ends, 1 - mate_pos))
    arrived = late(arrived, (bases, other_down))

    value0, slope0, d_hid1 = activation(act_first, arrived, 1, outs=2)
    mate_down0 = late(mate_down0, value0)
    down0 = own_down, other_down, mate_down0, only_to_core(mate_down0, 1)
    mate_up1 = only_to_mate(late(own_up, mate_down0), 1)
    hid0 = exchange(value0, "z").reshape(blocks[:2] + (1,) + piece)
    part = narrow(0, True, hid0, down0, lax.axis_size(col))
    mate_up1 = late(mate_up1, part)
    up1 = own_up, other_up, mate_up1, only_to_core(mate_up1, 0)
    arrived = exchange(part, col)

    pre1, x1 = widen(1, False, arrived, 0, bases, up1, blocks)
    hid0s = to_owner(late(hid0, pre1), 0)
    arrived = late(exchange(pre1.reshape((rings, 1) + piece), "z"), hid0s)
    (acts1,) = activation(act_last, arrived, 2, ins=(d_hid1,))
    acts1 = exchange(acts1, "z").reshape(blocks[:2] + (2,) + piece)
    part = narrow(1, False, acts1, up1, lax.axis_size(col))
    arrived = exchange(part, col)

    d_hid0, g1 = widen(0, True, arrived, 1, bases, down0, blocks)
    acts1s = to_owner(late(acts1, d_hid0), 1)
    arrived = exchange(d_hid0.reshape((rings, 1) + piece), "z")
    (d_pre0,) = activation(act_back, arrived, 1, ins=(slope0,))
    both1 = late(jnp.stack([x1, g1]), d_pre0)
    near, far = both1[..., :width], both1[..., width:]
    both1 = jnp.stack([near, to_other_core(near), to_mate(far), to_other_core_of_mate(far)])
    both1 = both1.reshape((2, 2) + near.shape)

    def all_tokens(array):
        return jnp.concatenate(
            [
                half_of(batch(array, which), half)
                for half in (mate_pos, 1 - mate_pos)
                for which in (section, 1 - section)
            ]
        )

    x1s, g1s = both1[:, :, 0].reshape(2 * tokens, width), both1[:, :, 1].reshape(2 * tokens, width)
    xs = jnp.where(first, all_tokens(inputs), x1s)
    gs = jnp.where(first, g1s, all_tokens(cotangent))

    down_grad = weight_grad(True, gs, hid0s, acts1s)
    d_pre0 = late(exchange(d_pre0, "z").reshape(blocks[:2] + (1,) + piece), down_grad)
    d_pre0s = to_owner(d_pre0, 0)

    last = last_product(own_up, own_down, d_pre0s, acts1s)
    xs, d_pre0s = late((xs, d_pre0s), last)
    arrived = exchange(last, col)
    up_grad = weight_grad(False, xs, d_pre0s, acts1s)

    out_len = tokens // lax.axis_size(col)
    per_half = half_len // out_len
    away = jnp.where(col_pos // per_half == mate_pos, 0, 1)
    pieces = lax.dynamic_index_in_dim(both1, away, 0, keepdims=False)
    pieces = lax.dynamic_slice_in_dim(pieces, (col_pos % per_half) * out_len, out_len, 2)
    pieces = jnp.where(first, pieces, pieces[::-1])
    states, grads = kernel_call(
        finish_kernel,
        [shape_of(pieces[:, 0].shape)] * 2,
        [VMEM] * 2,
        [VMEM] * 3,
        [],
        (arrived, pieces[:, 0], pieces[:, 1]),
        flops=100000,
        moved=200000,
    )
    return states[None], grads[None], up_grad[None], down_grad[None]


def solution(mesh):
    sections, rows, cols = mesh.devices.shape
    finer = Mesh(
        mesh.devices.reshape(sections, rows // 2, 2, cols // 2, 2),
        ("section", "z", "x_lo", "y", "x_hi"),
    )
    row, col = ("z", "x_lo"), ("y", "x_hi")
    in_specs = (
        P(None, None, row),
        P(None, None, row),
        P("section", row, col),
        P("section", col, row),
    )
    out_specs = (
        P("section", None, col, row),
        P("section", None, col, row),
        P("section", row, col),
        P("section", col, row),
    )
    return jax.shard_map(local, mesh=finer, in_specs=in_specs, out_specs=out_specs, check_vma=False)
```

```python
import functools

import jax
import jax.numpy as jnp
from jax import lax
from jax.experimental import pallas as pl
from jax.experimental.pallas import tpu as pltpu
from jax.sharding import Mesh, PartitionSpec as P

root_two_over_pi = 0.7978845608028654
cubic = 0.044715
f32 = jnp.float32
bf16 = jnp.bfloat16
CHUNK = 512
VMEM = pl.BlockSpec(memory_space=pltpu.VMEM)
HBM = pl.BlockSpec(memory_space=pltpu.HBM)
ANY = pl.BlockSpec(memory_space=pl.ANY)
LIMIT = pltpu.CompilerParams(vmem_limit_bytes=64 * 1024 * 1024)


def gelu_both(pre):
    inner = root_two_over_pi * (pre + cubic * pre * pre * pre)
    tangent = jnp.tanh(inner)
    value = 0.5 * pre * (1.0 + tangent)
    slope = 0.5 * (1.0 + tangent) + 0.5 * pre * (1.0 - tangent * tangent) * root_two_over_pi * (
        1.0 + 3.0 * cubic * pre * pre
    )
    return value, slope


def dot(left, right, dims):
    return lax.dot_general(left, right, (dims, ((), ())), preferred_element_type=f32)


def shape_of(shape, dtype=bf16):
    return jax.ShapeDtypeStruct(shape, dtype)


def load_weights(layer, by_rows, refs, held, sems):
    mine = lax.axis_index("section") == layer

    def copy(source, part, i):
        units = pl.ds(i * CHUNK, CHUNK)
        if by_rows:
            width = source.shape[1]
            block, place = source.at[units, :], held.at[i, :, pl.ds(part * width, width)]
        else:
            width = source.shape[0]
            block, place = source.at[:, units], held.at[i, pl.ds(part * width, width), :]
        return pltpu.make_async_copy(block, place, sems.at[part, i])

    def start(which):
        for i in range(held.shape[0]):
            for part, pair in enumerate(refs):
                copy(pair[which], part, i).start()

    pl.when(mine)(lambda: start(0))
    pl.when(jnp.logical_not(mine))(lambda: start(1))

    def wait(i):
        for part, pair in enumerate(refs):
            copy(pair[0], part, i).wait()

    return wait


def wait_all(copies):
    for copy in copies:
        copy.wait()


def first_kernel(layer, by_rows, pieces, x_ref, own, other, *rest):
    outs, (held, sems, stage, out_sems) = rest[: 1 if pieces else 2], rest[1 if pieces else 2 :]
    section, mate_pos = lax.axis_index("section"), lax.axis_index("x_lo")
    wait = load_weights(layer, by_rows, ((own, other),), held, sems)
    groups, tokens, wide = stage.shape[1], stage.shape[3], stage.shape[4]
    per_half = wide // CHUNK

    def out_copies(half):
        if pieces:
            pairs = [(stage.at[i, :, half], outs[0].at[:, half, i]) for i in range(2)]
        else:
            places = (mate_pos, 1 - mate_pos)
            pairs = [(stage.at[places[i], :, half], outs[i].at[:, half]) for i in range(2)]
        return [pltpu.make_async_copy(*pair, out_sems.at[half, i]) for i, pair in enumerate(pairs)]

    x = x_ref[section]
    for i in range(held.shape[0]):
        half, place = i // per_half, pl.ds((i % per_half) * CHUNK, CHUNK)
        wait(i)
        got = dot(x, held[i], ((1,), (1 if by_rows else 0,))).astype(bf16)
        stage[:, :, half, :, place] = got.reshape(2, groups, tokens, CHUNK)
        if i % per_half == per_half - 1:
            for copy in out_copies(half):
                copy.start()
    wait_all(out_copies(0) + out_copies(1))


def first_product(layer, by_rows, pieces, x, own, other, blocks):
    outs = [shape_of(blocks[:2] + (2,) + blocks[2:])] if pieces else [shape_of(blocks)] * 2
    return kernel_call(
        functools.partial(first_kernel, layer, by_rows, pieces),
        outs,
        [HBM] * len(outs),
        [VMEM, HBM, HBM],
        held_scratch(own, by_rows, 1)
        + [pltpu.VMEM((2,) + blocks, bf16), pltpu.SemaphoreType.DMA((2, 2))],
        (x, own, other),
        flops=2 * x.shape[1] * own.size,
        moved=2 * own.size,
    )


def widen_kernel(layer, by_rows, kind, riding, arrived_ref, base, base_mate, own, other, own_mate, other_mate, *rest):
    riders, rest = rest[: 2 * riding], rest[2 * riding :]
    out_ref, x_out, held, sems, stage, out_sems, arrived, in_sems = rest[:8]
    arrival = pltpu.make_async_copy(arrived_ref, arrived, in_sems.at[0])
    arrival.start()
    rides = [
        pltpu.make_async_copy(ref, rest[8].at[i], in_sems.at[1 + i]) for i, ref in enumerate(riders)
    ]
    for copy in rides:
        copy.start()
    wait = load_weights(layer, by_rows, ((own, other), (own_mate, other_mate)), held, sems)
    per_half = stage.shape[4] // CHUNK
    arrival.wait()
    total = arrived[0].astype(f32)
    for i in range(1, arrived.shape[0]):
        total = total + arrived[i].astype(f32)
    x = jnp.concatenate([base[kind], base_mate[kind]], axis=1)
    x = (x.astype(f32) + total).astype(bf16)
    x_out[...] = x
    if riding:
        wait_all(rides)
        stage[:, :, 1] = (rest[8][0].astype(f32) + rest[8][1].astype(f32)).astype(bf16)

    def out_copy(half):
        return pltpu.make_async_copy(stage.at[:, half], out_ref.at[:, half], out_sems.at[half])

    for i in range(held.shape[0]):
        half, place = i // per_half, pl.ds((i % per_half) * CHUNK, CHUNK)
        wait(i)
        got = dot(x, held[i], ((1,), (1 if by_rows else 0,))).astype(bf16)
        stage[:, half, 0, :, place] = got.reshape(stage.shape[0], stage.shape[3], CHUNK)
        if i % per_half == per_half - 1:
            out_copy(half).start()
    wait_all([out_copy(0), out_copy(1)])


def narrow_kernel(
    layer, by_rows, arrived_ref, own, other, own_mate, other_mate, out_ref, held, sems, stage, out_sems, arrived, in_sem
):
    arrival = pltpu.make_async_copy(arrived_ref.at[:, :, 0], arrived, in_sem)
    arrival.start()
    wait = load_weights(layer, by_rows, ((own, other), (own_mate, other_mate)), held, sems)
    per_half = arrived.shape[3] // CHUNK
    total = None
    arrival.wait()
    for i in range(held.shape[0]):
        left = arrived[:, i // per_half, :, pl.ds((i % per_half) * CHUNK, CHUNK)].reshape(-1, CHUNK)
        wait(i)
        got = dot(left, held[i], ((1,), (0 if by_rows else 1,)))
        total = got if total is None else total + got
    stage[...] = total.astype(bf16)
    copies = [
        pltpu.make_async_copy(stage, out_ref.at[i], out_sems.at[i]) for i in range(out_ref.shape[0])
    ]
    for copy in copies:
        copy.start()
    wait_all(copies)


def held_scratch(weight, by_rows, parts=2):
    count, width = max(weight.shape) // CHUNK, parts * min(weight.shape)
    chunk = (CHUNK, width) if by_rows else (width, CHUNK)
    return [pltpu.VMEM((count,) + chunk, bf16), pltpu.SemaphoreType.DMA((parts, count))]


def kernel_call(body, outs, out_specs, in_specs, scratch, operands, flops=0, moved=0):
    return pl.pallas_call(
        body,
        out_shape=outs,
        in_specs=in_specs,
        out_specs=out_specs,
        scratch_shapes=scratch,
        compiler_params=LIMIT,
        cost_estimate=pl.CostEstimate(flops=flops, bytes_accessed=moved, transcendentals=0),
    )(*operands)


def widen(layer, by_rows, arrived, kind, bases, weights, blocks, riders=()):
    shape = blocks[:2] + (2 if riders else 1,) + blocks[2:]
    return kernel_call(
        functools.partial(widen_kernel, layer, by_rows, kind, len(riders) // 2),
        (shape_of(shape), shape_of(arrived.shape[1:])),
        (HBM, VMEM),
        [HBM, VMEM, VMEM] + [HBM] * (4 + len(riders)),
        held_scratch(weights[0], by_rows)
        + [
            pltpu.VMEM(shape, bf16),
            pltpu.SemaphoreType.DMA((2,)),
            pltpu.VMEM(arrived.shape, bf16),
            pltpu.SemaphoreType.DMA((1 + len(riders),)),
        ]
        + ([pltpu.VMEM((2,) + blocks, bf16)] if riders else []),
        (arrived,) + bases + weights + riders,
        flops=4 * arrived.shape[1] * weights[0].size,
        moved=4 * weights[0].size,
    )


def narrow(layer, by_rows, arrived, weights, copies):
    groups, halves, _, tokens, wide = arrived.shape
    out = groups * tokens, 2 * min(weights[0].shape)
    return kernel_call(
        functools.partial(narrow_kernel, layer, by_rows),
        shape_of((copies,) + out),
        HBM,
        [HBM] * 5,
        held_scratch(weights[0], by_rows)
        + [
            pltpu.VMEM(out, bf16),
            pltpu.SemaphoreType.DMA((copies,)),
            pltpu.VMEM((groups, halves, tokens, wide), bf16),
            pltpu.SemaphoreType.DMA,
        ],
        (arrived,) + weights,
        flops=4 * out[0] * weights[0].size,
        moved=4 * weights[0].size,
    )


def act_kernel(body, ins, outs, arrived_ref, *refs):
    in_refs, out_ref, out_refs = refs[:ins], refs[ins], refs[ins + 1 : ins + 1 + outs]
    arrived, stage, in_sems, out_sems = refs[ins + 1 + outs :]
    steps = arrived.shape[3] // CHUNK
    places = [pl.ds(i * CHUNK, CHUNK) for i in range(steps)]
    arrivals = [
        pltpu.make_async_copy(arrived_ref.at[:, :, :, place], arrived.at[:, :, :, place], in_sems.at[i])
        for i, place in enumerate(places)
    ]
    for copy in arrivals:
        copy.start()
    copies = []
    for i, place in enumerate(places):
        arrivals[i].wait()
        sums = []
        for kind in range(arrived.shape[1]):
            total = arrived[0, kind, :, place].astype(f32)
            for source in range(1, arrived.shape[0]):
                total = total + arrived[source, kind, :, place].astype(f32)
            sums.append(total)
        spread, kept = body(sums, [ref[:, place] for ref in in_refs])
        for kind, value in enumerate(spread):
            stage[kind, :, place] = value.astype(bf16)
        for ref, value in zip(out_refs, kept):
            ref[:, place] = value
        for to in range(out_ref.shape[0]):
            copies.append(
                pltpu.make_async_copy(stage.at[:, :, place], out_ref.at[to, :, :, place], out_sems.at[i, to])
            )
            copies[-1].start()
    wait_all(copies)


def act_first(sums, _):
    value, slope = gelu_both(sums[0])
    return [value], [slope]


def act_last(sums, _):
    value, slope = gelu_both(sums[0])
    return [sums[1] * slope, value], []


def act_back(sums, ins):
    return [sums[0] * ins[0]], []


def activation(body, arrived, kinds, ins=(), outs=0, peers=None):
    peers, piece = peers or arrived.shape[0], arrived.shape[2:]
    steps = piece[1] // CHUNK
    return kernel_call(
        functools.partial(act_kernel, body, len(ins), outs),
        [shape_of((peers, kinds) + piece)] + [shape_of(piece, f32)] * outs,
        [HBM] + [VMEM] * outs,
        [HBM] + [VMEM] * len(ins),
        [
            pltpu.VMEM(arrived.shape, bf16),
            pltpu.VMEM((kinds,) + piece, bf16),
            pltpu.SemaphoreType.DMA((steps,)),
            pltpu.SemaphoreType.DMA((steps, peers)),
        ],
        (arrived,) + tuple(ins),
        flops=2000000,
        moved=2000000,
    )


def finish_kernel(arrived, x1, g1, states, grads):
    total = arrived[0].astype(f32)
    for i in range(1, arrived.shape[0]):
        total = total + arrived[i].astype(f32)

    def ended(base):
        return (base[...].astype(f32) + total).astype(bf16)

    @pl.when(lax.axis_index("section") == 0)
    def _():
        states[...] = x1[...]
        grads[...] = ended(g1)

    @pl.when(lax.axis_index("section") == 1)
    def _():
        states[...] = ended(x1)
        grads[...] = g1[...]


def pick_copies(layer0, layer1, kind, held, sems, start):
    section = lax.axis_index("section")

    def copy(layer, i):
        source = (layer0, layer1)[layer][i].at[:, :, 0 if layer == 0 else kind]
        return pltpu.make_async_copy(source, held.at[i], sems.at[i])

    if start:
        for layer in range(2):

            @pl.when(section == layer)
            def _():
                for i in range(4):
                    copy(layer, i).start()
    else:
        for i in range(4):
            copy(0, i).wait()


def step_chunk(held, step):
    per_half = held.shape[4] // CHUNK
    place = pl.ds(pl.multiple_of((step % per_half) * CHUNK, CHUNK), CHUNK)
    return held[:, :, step // per_half, :, place].reshape(-1, CHUNK)


def grad_down_kernel(g_ref, *refs):
    layer0, layer1, (out_ref, held, sems) = refs[:4], refs[4:8], refs[8:]
    step = pl.program_id(0)

    @pl.when(step == 0)
    def _():
        pick_copies(layer0, layer1, 1, held, sems, True)
        pick_copies(layer0, layer1, 1, held, sems, False)

    out_ref[...] = dot(step_chunk(held, step), g_ref[...], ((0,), (0,)))


def grad_up_kernel(x_ref, *refs):
    layer0, layer1, (out_ref, held, turned, sems) = refs[:4], refs[4:8], refs[8:]
    step = pl.program_id(0)

    @pl.when(step == 0)
    def _():
        pick_copies(layer0, layer1, 0, held, sems, True)
        turned[...] = x_ref[...].T
        pick_copies(layer0, layer1, 0, held, sems, False)

    out_ref[...] = dot(turned[...], step_chunk(held, step), ((1,), (0,)))


def weight_grad(down, narrow, layer0, layer1):
    groups, halves, _, tokens, wide = layer0[0].shape
    units, (all_tokens, width) = halves * wide, narrow.shape
    shape, block = ((units, width), (CHUNK, width)) if down else ((width, units), (width, CHUNK))
    turned = [] if down else [pltpu.VMEM((width, all_tokens), bf16)]
    return pl.pallas_call(
        grad_down_kernel if down else grad_up_kernel,
        out_shape=shape_of(shape, f32),
        grid=(units // CHUNK,),
        in_specs=[pl.BlockSpec(narrow.shape, lambda i: (0, 0))] + [HBM] * 8,
        out_specs=pl.BlockSpec(block, lambda i: (i, 0) if down else (0, i)),
        scratch_shapes=[pltpu.VMEM((4, groups, halves, tokens, wide), bf16)]
        + turned
        + [pltpu.SemaphoreType.DMA((4,))],
        compiler_params=LIMIT,
        cost_estimate=pl.CostEstimate(
            flops=2 * narrow.size * units, bytes_accessed=4 * width * units, transcendentals=0
        ),
    )(narrow, *layer0, *layer1)


def last_kernel(up, down, *refs):
    layer0, layer1, rest = refs[:4], refs[4:8], refs[8:]
    out_ref, held, up_held, down_held, stage, sems, up_sems, down_sems, out_sem = rest
    section, mate_pos = lax.axis_index("section"), lax.axis_index("x_lo")
    groups, halves, tokens, wide = held.shape[1:]
    per_half, count = wide // CHUNK, up_held.shape[0]
    pick_copies(layer0, layer1, 1, held, sems, True)

    def run(weight, by_rows, weight_held, weight_sems):
        copies = []
        for i in range(count):
            where = pl.ds(i * CHUNK, CHUNK)
            source = weight.at[where, :] if by_rows else weight.at[:, where]
            copies.append(pltpu.make_async_copy(source, weight_held.at[i], weight_sems.at[i]))
        for copy in copies:
            copy.start()
        pick_copies(layer0, layer1, 1, held, sems, False)
        total = None
        for i in range(count):
            left = held[:, :, i // per_half, :, pl.ds((i % per_half) * CHUNK, CHUNK)].reshape(-1, CHUNK)
            copies[i].wait()
            got = dot(left, weight_held[i], ((1,), (0 if by_rows else 1,)))
            total = got if total is None else total + got
        total = total.astype(bf16).reshape(4, groups, tokens, -1)
        for i in range(4):
            half = mate_pos if i < 2 else 1 - mate_pos
            which = section if i % 2 == 0 else 1 - section
            stage[pl.ds(half * groups, groups), which] = total[i]

    pl.when(section == 0)(lambda: run(up, False, up_held, up_sems))
    pl.when(section == 1)(lambda: run(down, True, down_held, down_sems))
    copy = pltpu.make_async_copy(stage, out_ref, out_sem)
    copy.start()
    copy.wait()


def last_product(up, down, layer0, layer1):
    groups, halves, _, tokens, wide = layer0[0].shape
    width, units = up.shape
    out = (2 * groups, 2, tokens, width)
    return kernel_call(
        last_kernel,
        shape_of(out),
        HBM,
        [HBM] * 10,
        [
            pltpu.VMEM((4, groups, halves, tokens, wide), bf16),
            pltpu.VMEM((units // CHUNK, width, CHUNK), bf16),
            pltpu.VMEM((units // CHUNK, CHUNK, width), bf16),
            pltpu.VMEM(out, bf16),
            pltpu.SemaphoreType.DMA((4,)),
            pltpu.SemaphoreType.DMA((units // CHUNK,)),
            pltpu.SemaphoreType.DMA((units // CHUNK,)),
            pltpu.SemaphoreType.DMA,
        ],
        (up, down) + layer0 + layer1,
        flops=8 * groups * tokens * up.size,
        moved=6 * up.size,
    )


def exchange(blocks, axes):
    return lax.all_to_all(blocks, axes, 0, 0)


CORES = ("section", "x_lo")


def to_other_core(block):
    return lax.ppermute(block, "section", [(0, 1), (1, 0)])


def to_mate(block):
    return lax.ppermute(block, "x_lo", [(0, 1), (1, 0)])


def to_other_core_of_mate(block):
    return lax.ppermute(block, CORES, [(0, 3), (3, 0), (1, 2), (2, 1)])


def only_to_mate(block, section):
    at = 2 * section
    return lax.ppermute(block, CORES, [(at, at + 1), (at + 1, at)])


def only_to_core(block, section):
    return lax.ppermute(block, "section", [(1 - section, section)])


def only_across(block, section):
    at, source = 2 * section, 2 * (1 - section)
    return lax.ppermute(block, CORES, [(source, at + 1), (source + 1, at)])


def to_owner(block, section):
    return block, only_to_core(block, section), only_to_mate(block, section), only_across(block, section)


def late(block, after):
    return lax.optimization_barrier((block, after))[0]


def local(inputs, cotangent, w_up, w_down):
    col = ("y", "x_hi")
    section, mate_pos, col_pos = (lax.axis_index(name) for name in ("section", "x_lo", col))
    first = section == 0
    own_up, own_down = w_up[0], w_down[0]
    tokens, width = inputs.shape[1:]
    half_len = tokens // 2
    rings = lax.axis_size("z")
    piece = (tokens // rings, own_up.shape[1] // 2)
    blocks = (half_len // piece[0], 2) + piece

    def half_of(array, which):
        return lax.dynamic_slice_in_dim(array, which * half_len, half_len, 0)

    def batch(array, which):
        return lax.dynamic_index_in_dim(array, which, 0, keepdims=False)

    def halves_of(pair, which):
        return lax.dynamic_slice_in_dim(pair, which * half_len, half_len, 1)

    mate_down0 = only_to_mate(own_down, 0)
    other_up = to_other_core(own_up)
    (pre0,) = first_product(0, False, True, inputs, own_up, other_up, blocks)
    arrived = exchange(pre0.reshape((2 * rings, 1) + piece), ("z", "x_lo"))

    other_down = to_other_core(late(own_down, other_up))
    x0, g2 = late((inputs, cotangent), pre0)
    keep, send = first_product(1, True, False, g2, own_down, other_down, blocks)
    d_hid1 = keep, to_mate(send)
    ends = jnp.stack([batch(x0, section), batch(g2, section)])
    bases = halves_of(ends, mate_pos), to_mate(halves_of(ends, 1 - mate_pos))
    arrived = late(arrived, (bases, d_hid1))

    mate_up1 = only_to_mate(late(own_up, arrived), 1)
    mate_down0 = late(mate_down0, arrived)
    down0 = own_down, other_down, mate_down0, only_to_core(mate_down0, 1)
    value0, slope0 = activation(act_first, arrived, 1, outs=1, peers=rings)
    hid0 = exchange(value0, "z").reshape(blocks[:2] + (1,) + piece)
    part = narrow(0, True, hid0, down0, lax.axis_size(col))
    mate_up1 = late(mate_up1, part)
    up1 = own_up, other_up, mate_up1, only_to_core(mate_up1, 0)
    arrived = exchange(part, col)

    pre1, x1 = widen(1, False, arrived, 0, bases, up1, blocks, d_hid1)
    hid0s = to_owner(late(hid0, pre1), 0)
    arrived = exchange(pre1.reshape((rings, 2) + piece), "z")
    (acts1,) = activation(act_last, arrived, 2)
    acts1 = late(exchange(acts1, "z").reshape(blocks[:2] + (2,) + piece), hid0s)
    part = narrow(1, False, acts1, up1, lax.axis_size(col))
    arrived = exchange(part, col)

    d_hid0, g1 = widen(0, True, arrived, 1, bases, down0, blocks)
    acts1s = to_owner(late(acts1, d_hid0), 1)
    arrived = exchange(d_hid0.reshape((rings, 1) + piece), "z")
    (d_pre0,) = activation(act_back, late(arrived, acts1s[1:3]), 1, ins=(slope0,))
    both1 = late(jnp.stack([x1, g1]), d_pre0)
    near, far = both1[..., :width], both1[..., width:]
    both1 = jnp.stack([near, to_other_core(near), to_mate(far), to_other_core_of_mate(far)])
    both1 = both1.reshape((2, 2) + near.shape)

    def all_tokens(array):
        return jnp.concatenate(
            [
                half_of(batch(array, which), half)
                for half in (mate_pos, 1 - mate_pos)
                for which in (section, 1 - section)
            ]
        )

    x1s, g1s = both1[:, :, 0].reshape(2 * tokens, width), both1[:, :, 1].reshape(2 * tokens, width)
    xs = jnp.where(first, all_tokens(inputs), x1s)
    gs = jnp.where(first, g1s, all_tokens(cotangent))

    d_pre0 = late(exchange(d_pre0, "z").reshape(blocks[:2] + (1,) + piece), acts1s[3])
    down_grad = weight_grad(True, late(gs, d_pre0), hid0s, acts1s)
    d_pre0s = late(to_owner(d_pre0, 0), down_grad)

    last = last_product(own_up, own_down, d_pre0s, acts1s)
    xs, d_pre0s = late((xs, d_pre0s), last)
    arrived = exchange(last, col)
    up_grad = weight_grad(False, xs, d_pre0s, acts1s)

    out_len = tokens // lax.axis_size(col)
    per_half = half_len // out_len
    away = jnp.where(col_pos // per_half == mate_pos, 0, 1)
    pieces = lax.dynamic_index_in_dim(both1, away, 0, keepdims=False)
    pieces = lax.dynamic_slice_in_dim(pieces, (col_pos % per_half) * out_len, out_len, 2)
    pieces = jnp.where(first, pieces, pieces[::-1])
    states, grads = kernel_call(
        finish_kernel,
        [shape_of(pieces[:, 0].shape)] * 2,
        [VMEM] * 2,
        [VMEM] * 3,
        [],
        (arrived, pieces[:, 0], pieces[:, 1]),
        flops=100000,
        moved=200000,
    )
    return states[None], grads[None], up_grad[None], down_grad[None]


def solution(mesh):
    sections, rows, cols = mesh.devices.shape
    finer = Mesh(
        mesh.devices.reshape(sections, rows // 2, 2, cols // 2, 2),
        ("section", "z", "x_lo", "y", "x_hi"),
    )
    row, col = ("z", "x_lo"), ("y", "x_hi")
    in_specs = (
        P(None, None, row),
        P(None, None, row),
        P("section", row, col),
        P("section", col, row),
    )
    out_specs = (
        P("section", None, col, row),
        P("section", None, col, row),
        P("section", row, col),
        P("section", col, row),
    )
    return jax.shard_map(local, mesh=finer, in_specs=in_specs, out_specs=out_specs, check_vma=False)
```

```python
import functools

import jax
import jax.numpy as jnp
from jax import lax
from jax.experimental import pallas as pl
from jax.experimental.pallas import tpu as pltpu
from jax.sharding import Mesh, PartitionSpec as P

root_two_over_pi = 0.7978845608028654
cubic = 0.044715
f32 = jnp.float32
bf16 = jnp.bfloat16
CHUNK = 512
VMEM = pl.BlockSpec(memory_space=pltpu.VMEM)
HBM = pl.BlockSpec(memory_space=pltpu.HBM)
ANY = pl.BlockSpec(memory_space=pl.ANY)
LIMIT = pltpu.CompilerParams(vmem_limit_bytes=64 * 1024 * 1024)


def gelu_both(pre):
    inner = root_two_over_pi * (pre + cubic * pre * pre * pre)
    tangent = jnp.tanh(inner)
    value = 0.5 * pre * (1.0 + tangent)
    slope = 0.5 * (1.0 + tangent) + 0.5 * pre * (1.0 - tangent * tangent) * root_two_over_pi * (
        1.0 + 3.0 * cubic * pre * pre
    )
    return value, slope


def dot(left, right, dims):
    return lax.dot_general(left, right, (dims, ((), ())), preferred_element_type=f32)


def shape_of(shape, dtype=bf16):
    return jax.ShapeDtypeStruct(shape, dtype)


def load_weights(layer, by_rows, refs, held, sems):
    mine = lax.axis_index("section") == layer

    def copy(source, part, i):
        units = pl.ds(i * CHUNK, CHUNK)
        if by_rows:
            width = source.shape[1]
            block, place = source.at[units, :], held.at[i, :, pl.ds(part * width, width)]
        else:
            width = source.shape[0]
            block, place = source.at[:, units], held.at[i, pl.ds(part * width, width), :]
        return pltpu.make_async_copy(block, place, sems.at[part, i])

    def start(which):
        for i in range(held.shape[0]):
            for part, pair in enumerate(refs):
                copy(pair[which], part, i).start()

    pl.when(mine)(lambda: start(0))
    pl.when(jnp.logical_not(mine))(lambda: start(1))

    def wait(i):
        for part, pair in enumerate(refs):
            copy(pair[0], part, i).wait()

    return wait


def wait_all(copies):
    for copy in copies:
        copy.wait()


def first_kernel(layer, by_rows, pieces, x_ref, own, other, *rest):
    outs, (held, sems, stage, out_sems) = rest[: 1 if pieces else 2], rest[1 if pieces else 2 :]
    section, mate_pos = lax.axis_index("section"), lax.axis_index("x_lo")
    wait = load_weights(layer, by_rows, ((own, other),), held, sems)
    groups, tokens, wide = stage.shape[1], stage.shape[3], stage.shape[4]
    per_half = wide // CHUNK

    def out_copies(half):
        if pieces:
            pairs = [(stage.at[i, :, half], outs[0].at[:, half, i]) for i in range(2)]
        else:
            places = (mate_pos, 1 - mate_pos)
            pairs = [(stage.at[places[i], :, half], outs[i].at[:, half]) for i in range(2)]
        return [pltpu.make_async_copy(*pair, out_sems.at[half, i]) for i, pair in enumerate(pairs)]

    x = x_ref[section]
    for i in range(held.shape[0]):
        half, place = i // per_half, pl.ds((i % per_half) * CHUNK, CHUNK)
        wait(i)
        got = dot(x, held[i], ((1,), (1 if by_rows else 0,))).astype(bf16)
        stage[:, :, half, :, place] = got.reshape(2, groups, tokens, CHUNK)
        if i % per_half == per_half - 1:
            for copy in out_copies(half):
                copy.start()
    wait_all(out_copies(0) + out_copies(1))


def first_product(layer, by_rows, pieces, x, own, other, blocks):
    outs = [shape_of(blocks[:2] + (2,) + blocks[2:])] if pieces else [shape_of(blocks)] * 2
    return kernel_call(
        functools.partial(first_kernel, layer, by_rows, pieces),
        outs,
        [HBM] * len(outs),
        [VMEM, HBM, HBM],
        held_scratch(own, by_rows, 1)
        + [pltpu.VMEM((2,) + blocks, bf16), pltpu.SemaphoreType.DMA((2, 2))],
        (x, own, other),
        flops=2 * x.shape[1] * own.size,
        moved=2 * own.size,
    )


def widen_kernel(layer, by_rows, kind, riding, arrived_ref, base, base_mate, own, other, own_mate, other_mate, *rest):
    riders, rest = rest[: 2 * riding], rest[2 * riding :]
    out_ref, x_out, held, sems, stage, out_sems, arrived, in_sems = rest[:8]
    arrival = pltpu.make_async_copy(arrived_ref, arrived, in_sems.at[0])
    arrival.start()
    rides = [
        pltpu.make_async_copy(ref, rest[8].at[i], in_sems.at[1 + i]) for i, ref in enumerate(riders)
    ]
    for copy in rides:
        copy.start()
    wait = load_weights(layer, by_rows, ((own, other), (own_mate, other_mate)), held, sems)
    per_half = stage.shape[4] // CHUNK
    arrival.wait()
    total = arrived[0].astype(f32)
    for i in range(1, arrived.shape[0]):
        total = total + arrived[i].astype(f32)
    x = jnp.concatenate([base[kind], base_mate[kind]], axis=1)
    x = (x.astype(f32) + total).astype(bf16)
    x_out[...] = x
    if riding:
        wait_all(rides)
        stage[:, :, 1] = (rest[8][0].astype(f32) + rest[8][1].astype(f32)).astype(bf16)

    def out_copy(half):
        return pltpu.make_async_copy(stage.at[:, half], out_ref.at[:, half], out_sems.at[half])

    for i in range(held.shape[0]):
        half, place = i // per_half, pl.ds((i % per_half) * CHUNK, CHUNK)
        wait(i)
        got = dot(x, held[i], ((1,), (1 if by_rows else 0,))).astype(bf16)
        stage[:, half, 0, :, place] = got.reshape(stage.shape[0], stage.shape[3], CHUNK)
        if i % per_half == per_half - 1:
            out_copy(half).start()
    wait_all([out_copy(0), out_copy(1)])


def narrow_kernel(
    layer, by_rows, arrived_ref, own, other, own_mate, other_mate, out_ref, held, sems, stage, out_sems, arrived, in_sem
):
    arrival = pltpu.make_async_copy(arrived_ref.at[:, :, 0], arrived, in_sem)
    arrival.start()
    wait = load_weights(layer, by_rows, ((own, other), (own_mate, other_mate)), held, sems)
    per_half = arrived.shape[3] // CHUNK
    total = None
    arrival.wait()
    for i in range(held.shape[0]):
        left = arrived[:, i // per_half, :, pl.ds((i % per_half) * CHUNK, CHUNK)].reshape(-1, CHUNK)
        wait(i)
        got = dot(left, held[i], ((1,), (0 if by_rows else 1,)))
        total = got if total is None else total + got
    stage[...] = total.astype(bf16)
    copies = [
        pltpu.make_async_copy(stage, out_ref.at[i], out_sems.at[i]) for i in range(out_ref.shape[0])
    ]
    for copy in copies:
        copy.start()
    wait_all(copies)


def held_scratch(weight, by_rows, parts=2):
    count, width = max(weight.shape) // CHUNK, parts * min(weight.shape)
    chunk = (CHUNK, width) if by_rows else (width, CHUNK)
    return [pltpu.VMEM((count,) + chunk, bf16), pltpu.SemaphoreType.DMA((parts, count))]


def kernel_call(body, outs, out_specs, in_specs, scratch, operands, flops=0, moved=0):
    return pl.pallas_call(
        body,
        out_shape=outs,
        in_specs=in_specs,
        out_specs=out_specs,
        scratch_shapes=scratch,
        compiler_params=LIMIT,
        cost_estimate=pl.CostEstimate(flops=flops, bytes_accessed=moved, transcendentals=0),
    )(*operands)


def widen(layer, by_rows, arrived, kind, bases, weights, blocks, riders=()):
    shape = blocks[:2] + (2 if riders else 1,) + blocks[2:]
    return kernel_call(
        functools.partial(widen_kernel, layer, by_rows, kind, len(riders) // 2),
        (shape_of(shape), shape_of(arrived.shape[1:])),
        (HBM, VMEM),
        [HBM, VMEM, VMEM] + [HBM] * (4 + len(riders)),
        held_scratch(weights[0], by_rows)
        + [
            pltpu.VMEM(shape, bf16),
            pltpu.SemaphoreType.DMA((2,)),
            pltpu.VMEM(arrived.shape, bf16),
            pltpu.SemaphoreType.DMA((1 + len(riders),)),
        ]
        + ([pltpu.VMEM((2,) + blocks, bf16)] if riders else []),
        (arrived,) + bases + weights + riders,
        flops=4 * arrived.shape[1] * weights[0].size,
        moved=4 * weights[0].size,
    )


def narrow(layer, by_rows, arrived, weights, copies):
    groups, halves, _, tokens, wide = arrived.shape
    out = groups * tokens, 2 * min(weights[0].shape)
    return kernel_call(
        functools.partial(narrow_kernel, layer, by_rows),
        shape_of((copies,) + out),
        HBM,
        [HBM] * 5,
        held_scratch(weights[0], by_rows)
        + [
            pltpu.VMEM(out, bf16),
            pltpu.SemaphoreType.DMA((copies,)),
            pltpu.VMEM((groups, halves, tokens, wide), bf16),
            pltpu.SemaphoreType.DMA,
        ],
        (arrived,) + weights,
        flops=4 * out[0] * weights[0].size,
        moved=4 * weights[0].size,
    )


def act_kernel(body, ins, outs, arrived_ref, *refs):
    in_refs, out_ref, out_refs = refs[:ins], refs[ins], refs[ins + 1 : ins + 1 + outs]
    arrived, stage, in_sems, out_sems = refs[ins + 1 + outs :]
    steps = arrived.shape[3] // CHUNK
    places = [pl.ds(i * CHUNK, CHUNK) for i in range(steps)]
    arrivals = [
        pltpu.make_async_copy(arrived_ref.at[:, :, :, place], arrived.at[:, :, :, place], in_sems.at[i])
        for i, place in enumerate(places)
    ]
    for copy in arrivals:
        copy.start()
    copies = []
    for i, place in enumerate(places):
        arrivals[i].wait()
        sums = []
        for kind in range(arrived.shape[1]):
            total = arrived[0, kind, :, place].astype(f32)
            for source in range(1, arrived.shape[0]):
                total = total + arrived[source, kind, :, place].astype(f32)
            sums.append(total)
        spread, kept = body(sums, [ref[:, place] for ref in in_refs])
        for kind, value in enumerate(spread):
            stage[kind, :, place] = value.astype(bf16)
        for ref, value in zip(out_refs, kept):
            ref[:, place] = value
        for to in range(out_ref.shape[0]):
            copies.append(
                pltpu.make_async_copy(stage.at[:, :, place], out_ref.at[to, :, :, place], out_sems.at[i, to])
            )
            copies[-1].start()
    wait_all(copies)


def act_first(sums, _):
    value, slope = gelu_both(sums[0])
    return [value], [slope]


def act_last(sums, _):
    value, slope = gelu_both(sums[0])
    return [sums[1] * slope, value], []


def act_back(sums, ins):
    return [sums[0] * ins[0]], []


def activation(body, arrived, kinds, ins=(), outs=0, peers=None):
    peers, piece = peers or arrived.shape[0], arrived.shape[2:]
    steps = piece[1] // CHUNK
    return kernel_call(
        functools.partial(act_kernel, body, len(ins), outs),
        [shape_of((peers, kinds) + piece)] + [shape_of(piece, f32)] * outs,
        [HBM] + [VMEM] * outs,
        [HBM] + [VMEM] * len(ins),
        [
            pltpu.VMEM(arrived.shape, bf16),
            pltpu.VMEM((kinds,) + piece, bf16),
            pltpu.SemaphoreType.DMA((steps,)),
            pltpu.SemaphoreType.DMA((steps, peers)),
        ],
        (arrived,) + tuple(ins),
        flops=2000000,
        moved=2000000,
    )


def finish_kernel(arrived, x1, g1, states, grads):
    total = arrived[0].astype(f32)
    for i in range(1, arrived.shape[0]):
        total = total + arrived[i].astype(f32)

    def ended(base):
        return (base[...].astype(f32) + total).astype(bf16)

    @pl.when(lax.axis_index("section") == 0)
    def _():
        states[...] = x1[...]
        grads[...] = ended(g1)

    @pl.when(lax.axis_index("section") == 1)
    def _():
        states[...] = ended(x1)
        grads[...] = g1[...]


def pick_copies(layer0, layer1, kind, held, sems, start):
    section = lax.axis_index("section")

    def copy(layer, i):
        source = (layer0, layer1)[layer][i].at[:, :, 0 if layer == 0 else kind]
        return pltpu.make_async_copy(source, held.at[i], sems.at[i])

    if start:
        for layer in range(2):

            @pl.when(section == layer)
            def _():
                for i in range(4):
                    copy(layer, i).start()
    else:
        for i in range(4):
            copy(0, i).wait()


def step_chunk(held, step):
    per_half = held.shape[4] // CHUNK
    place = pl.ds(pl.multiple_of((step % per_half) * CHUNK, CHUNK), CHUNK)
    return held[:, :, step // per_half, :, place].reshape(-1, CHUNK)


def grad_down_kernel(g_ref, *refs):
    layer0, layer1, (out_ref, held, sems) = refs[:4], refs[4:8], refs[8:]
    step = pl.program_id(0)

    @pl.when(step == 0)
    def _():
        pick_copies(layer0, layer1, 1, held, sems, True)
        pick_copies(layer0, layer1, 1, held, sems, False)

    out_ref[...] = dot(step_chunk(held, step), g_ref[...], ((0,), (0,)))


def grad_up_kernel(x_ref, *refs):
    layer0, layer1, (out_ref, held, turned, sems) = refs[:4], refs[4:8], refs[8:]
    step = pl.program_id(0)

    @pl.when(step == 0)
    def _():
        pick_copies(layer0, layer1, 0, held, sems, True)
        turned[...] = x_ref[...].T
        pick_copies(layer0, layer1, 0, held, sems, False)

    out_ref[...] = dot(turned[...], step_chunk(held, step), ((1,), (0,)))


def weight_grad(down, narrow, layer0, layer1):
    groups, halves, _, tokens, wide = layer0[0].shape
    units, (all_tokens, width) = halves * wide, narrow.shape
    shape, block = ((units, width), (CHUNK, width)) if down else ((width, units), (width, CHUNK))
    turned = [] if down else [pltpu.VMEM((width, all_tokens), bf16)]
    return pl.pallas_call(
        grad_down_kernel if down else grad_up_kernel,
        out_shape=shape_of(shape, f32),
        grid=(units // CHUNK,),
        in_specs=[pl.BlockSpec(narrow.shape, lambda i: (0, 0))] + [HBM] * 8,
        out_specs=pl.BlockSpec(block, lambda i: (i, 0) if down else (0, i)),
        scratch_shapes=[pltpu.VMEM((4, groups, halves, tokens, wide), bf16)]
        + turned
        + [pltpu.SemaphoreType.DMA((4,))],
        compiler_params=LIMIT,
        cost_estimate=pl.CostEstimate(
            flops=2 * narrow.size * units, bytes_accessed=4 * width * units, transcendentals=0
        ),
    )(narrow, *layer0, *layer1)


def last_kernel(up, down, *refs):
    layer0, layer1, rest = refs[:4], refs[4:8], refs[8:]
    out_ref, held, up_held, down_held, stage, sems, up_sems, down_sems, out_sem = rest
    section, mate_pos = lax.axis_index("section"), lax.axis_index("x_lo")
    groups, halves, tokens, wide = held.shape[1:]
    per_half, count = wide // CHUNK, up_held.shape[0]
    pick_copies(layer0, layer1, 1, held, sems, True)

    def run(weight, by_rows, weight_held, weight_sems):
        copies = []
        for i in range(count):
            where = pl.ds(i * CHUNK, CHUNK)
            source = weight.at[where, :] if by_rows else weight.at[:, where]
            copies.append(pltpu.make_async_copy(source, weight_held.at[i], weight_sems.at[i]))
        for copy in copies:
            copy.start()
        pick_copies(layer0, layer1, 1, held, sems, False)
        total = None
        for i in range(count):
            left = held[:, :, i // per_half, :, pl.ds((i % per_half) * CHUNK, CHUNK)].reshape(-1, CHUNK)
            copies[i].wait()
            got = dot(left, weight_held[i], ((1,), (0 if by_rows else 1,)))
            total = got if total is None else total + got
        total = total.astype(bf16).reshape(4, groups, tokens, -1)
        for i in range(4):
            half = mate_pos if i < 2 else 1 - mate_pos
            which = section if i % 2 == 0 else 1 - section
            stage[pl.ds(half * groups, groups), which] = total[i]

    pl.when(section == 0)(lambda: run(up, False, up_held, up_sems))
    pl.when(section == 1)(lambda: run(down, True, down_held, down_sems))
    copy = pltpu.make_async_copy(stage, out_ref, out_sem)
    copy.start()
    copy.wait()


def last_product(up, down, layer0, layer1):
    groups, halves, _, tokens, wide = layer0[0].shape
    width, units = up.shape
    out = (2 * groups, 2, tokens, width)
    return kernel_call(
        last_kernel,
        shape_of(out),
        HBM,
        [HBM] * 10,
        [
            pltpu.VMEM((4, groups, halves, tokens, wide), bf16),
            pltpu.VMEM((units // CHUNK, width, CHUNK), bf16),
            pltpu.VMEM((units // CHUNK, CHUNK, width), bf16),
            pltpu.VMEM(out, bf16),
            pltpu.SemaphoreType.DMA((4,)),
            pltpu.SemaphoreType.DMA((units // CHUNK,)),
            pltpu.SemaphoreType.DMA((units // CHUNK,)),
            pltpu.SemaphoreType.DMA,
        ],
        (up, down) + layer0 + layer1,
        flops=8 * groups * tokens * up.size,
        moved=6 * up.size,
    )


def exchange(blocks, axes):
    return lax.all_to_all(blocks, axes, 0, 0)


CORES = ("section", "x_lo")


def to_other_core(block):
    return lax.ppermute(block, "section", [(0, 1), (1, 0)])


def to_mate(block):
    return lax.ppermute(block, "x_lo", [(0, 1), (1, 0)])


def to_other_core_of_mate(block):
    return lax.ppermute(block, CORES, [(0, 3), (3, 0), (1, 2), (2, 1)])


def only_to_mate(block, section):
    at = 2 * section
    return lax.ppermute(block, CORES, [(at, at + 1), (at + 1, at)])


def only_to_core(block, section):
    return lax.ppermute(block, "section", [(1 - section, section)])


def only_across(block, section):
    at, source = 2 * section, 2 * (1 - section)
    return lax.ppermute(block, CORES, [(source, at + 1), (source + 1, at)])


def to_owner(block, section):
    return block, only_to_core(block, section), only_to_mate(block, section), only_across(block, section)


def late(block, after):
    return lax.optimization_barrier((block, after))[0]


def local(inputs, cotangent, w_up, w_down):
    col = ("y", "x_hi")
    section, mate_pos, col_pos = (lax.axis_index(name) for name in ("section", "x_lo", col))
    first = section == 0
    own_up, own_down = w_up[0], w_down[0]
    tokens, width = inputs.shape[1:]
    half_len = tokens // 2
    rings = lax.axis_size("z")
    piece = (tokens // rings, own_up.shape[1] // 2)
    blocks = (half_len // piece[0], 2) + piece

    def half_of(array, which):
        return lax.dynamic_slice_in_dim(array, which * half_len, half_len, 0)

    def batch(array, which):
        return lax.dynamic_index_in_dim(array, which, 0, keepdims=False)

    def halves_of(pair, which):
        return lax.dynamic_slice_in_dim(pair, which * half_len, half_len, 1)

    other_up = to_other_core(own_up)
    ends = jnp.stack([batch(inputs, section), batch(cotangent, section)])
    bases = halves_of(ends, mate_pos), to_mate(halves_of(ends, 1 - mate_pos))
    mate_down0 = only_to_mate(late(own_down, bases), 0)
    (pre0,) = first_product(0, False, True, inputs, own_up, other_up, blocks)
    arrived = exchange(pre0.reshape((2 * rings, 1) + piece), ("z", "x_lo"))

    other_down = to_other_core(late(own_down, other_up))
    keep, send = first_product(1, True, False, late(cotangent, pre0), own_down, other_down, blocks)
    d_hid1 = keep, to_mate(send)

    mate_down0 = late(mate_down0, arrived)
    down0 = own_down, other_down, mate_down0, only_to_core(mate_down0, 1)
    value0, slope0 = activation(act_first, arrived, 1, outs=1, peers=rings)
    value0 = late(value0, d_hid1)
    mate_up1 = only_to_mate(late(own_up, value0), 1)
    hid0 = exchange(value0, "z").reshape(blocks[:2] + (1,) + piece)
    part = narrow(0, True, hid0, down0, lax.axis_size(col))
    mate_up1 = late(mate_up1, part)
    up1 = own_up, other_up, mate_up1, only_to_core(mate_up1, 0)
    arrived = exchange(part, col)

    pre1, x1 = widen(1, False, arrived, 0, bases, up1, blocks, d_hid1)
    hid0s = to_owner(late(hid0, pre1), 0)
    arrived = exchange(pre1.reshape((rings, 2) + piece), "z")
    (acts1,) = activation(act_last, arrived, 2)
    acts1 = late(exchange(acts1, "z").reshape(blocks[:2] + (2,) + piece), hid0s)
    part = narrow(1, False, acts1, up1, lax.axis_size(col))
    arrived = exchange(part, col)

    d_hid0, g1 = widen(0, True, arrived, 1, bases, down0, blocks)
    acts1, both1 = late((acts1, jnp.stack([x1, g1])), d_hid0)
    acts1s = to_owner(acts1, 1)
    arrived = exchange(d_hid0.reshape((rings, 1) + piece), "z")
    near, far = both1[..., :width], both1[..., width:]
    both1 = jnp.stack([near, to_other_core(near), to_mate(far), to_other_core_of_mate(far)])
    both1 = both1.reshape((2, 2) + near.shape)

    def all_tokens(array):
        return jnp.concatenate(
            [
                half_of(batch(array, which), half)
                for half in (mate_pos, 1 - mate_pos)
                for which in (section, 1 - section)
            ]
        )

    x1s, g1s = both1[:, :, 0].reshape(2 * tokens, width), both1[:, :, 1].reshape(2 * tokens, width)
    xs = jnp.where(first, all_tokens(inputs), x1s)
    gs = jnp.where(first, g1s, all_tokens(cotangent))

    (d_pre0,) = activation(act_back, arrived, 1, ins=(slope0,))
    d_pre0 = late(exchange(d_pre0, "z").reshape(blocks[:2] + (1,) + piece), acts1s)
    down_grad = weight_grad(True, late(gs, d_pre0), hid0s, acts1s)
    d_pre0s = late(to_owner(d_pre0, 0), down_grad)

    last = last_product(own_up, own_down, d_pre0s, acts1s)
    xs, d_pre0s = late((xs, d_pre0s), last)
    arrived = exchange(last, col)
    up_grad = weight_grad(False, xs, d_pre0s, acts1s)

    out_len = tokens // lax.axis_size(col)
    per_half = half_len // out_len
    away = jnp.where(col_pos // per_half == mate_pos, 0, 1)
    pieces = lax.dynamic_index_in_dim(both1, away, 0, keepdims=False)
    pieces = lax.dynamic_slice_in_dim(pieces, (col_pos % per_half) * out_len, out_len, 2)
    pieces = jnp.where(first, pieces, pieces[::-1])
    states, grads = kernel_call(
        finish_kernel,
        [shape_of(pieces[:, 0].shape)] * 2,
        [VMEM] * 2,
        [VMEM] * 3,
        [],
        (arrived, pieces[:, 0], pieces[:, 1]),
        flops=100000,
        moved=200000,
    )
    return states[None], grads[None], up_grad[None], down_grad[None]


def solution(mesh):
    sections, rows, cols = mesh.devices.shape
    finer = Mesh(
        mesh.devices.reshape(sections, rows // 2, 2, cols // 2, 2),
        ("section", "z", "x_lo", "y", "x_hi"),
    )
    row, col = ("z", "x_lo"), ("y", "x_hi")
    in_specs = (
        P(None, None, row),
        P(None, None, row),
        P("section", row, col),
        P("section", col, row),
    )
    out_specs = (
        P("section", None, col, row),
        P("section", None, col, row),
        P("section", row, col),
        P("section", col, row),
    )
    return jax.shard_map(local, mesh=finer, in_specs=in_specs, out_specs=out_specs, check_vma=False)
```

```python
import functools

import jax
import jax.numpy as jnp
from jax import lax
from jax.experimental import pallas as pl
from jax.experimental.pallas import tpu as pltpu
from jax.sharding import Mesh, PartitionSpec as P

root_two_over_pi = 0.7978845608028654
cubic = 0.044715
f32 = jnp.float32
bf16 = jnp.bfloat16
CHUNK = 512
VMEM = pl.BlockSpec(memory_space=pltpu.VMEM)
HBM = pl.BlockSpec(memory_space=pltpu.HBM)
ANY = pl.BlockSpec(memory_space=pl.ANY)
LIMIT = pltpu.CompilerParams(vmem_limit_bytes=64 * 1024 * 1024)


def gelu_both(pre):
    inner = root_two_over_pi * (pre + cubic * pre * pre * pre)
    tangent = jnp.tanh(inner)
    value = 0.5 * pre * (1.0 + tangent)
    slope = 0.5 * (1.0 + tangent) + 0.5 * pre * (1.0 - tangent * tangent) * root_two_over_pi * (
        1.0 + 3.0 * cubic * pre * pre
    )
    return value, slope


def dot(left, right, dims):
    return lax.dot_general(left, right, (dims, ((), ())), preferred_element_type=f32)


def shape_of(shape, dtype=bf16):
    return jax.ShapeDtypeStruct(shape, dtype)


def load_weights(layer, by_rows, refs, held, sems):
    mine = lax.axis_index("section") == layer

    def copy(source, part, i):
        where = pl.ds(i * CHUNK, CHUNK)
        block = source.at[where, :] if by_rows else source.at[:, where]
        return pltpu.make_async_copy(block, held.at[part, i], sems.at[part, i])

    def start(which):
        for i in range(held.shape[1]):
            for part, pair in enumerate(refs):
                copy(pair[which], part, i).start()

    pl.when(mine)(lambda: start(0))
    pl.when(jnp.logical_not(mine))(lambda: start(1))
    return lambda part, i: copy(refs[part][0], part, i).wait()


def widen(xs, by_rows, wait, held, put):
    for i in range(held.shape[1]):
        total = None
        for part, x in enumerate(xs):
            wait(part, i)
            got = dot(x, held[part, i], ((1,), (1 if by_rows else 0,)))
            total = got if total is None else total + got
        put(i, total)


def widen_first_kernel(layer, by_rows, mate_at, x_ref, own, other, out_ref, held, sems, stage, out_sems):
    wait = load_weights(layer, by_rows, ((own, other),), held, sems)
    groups, tokens, wide = stage.shape[1 if mate_at == 0 else 0], stage.shape[3], stage.shape[4]
    per_half = wide // CHUNK

    def out_copy(half):
        where = (slice(None),) * (2 if mate_at == 0 else 1) + (half,)
        return pltpu.make_async_copy(stage.at[where], out_ref.at[where], out_sems.at[half])

    def put(i, total):
        half, place = i // per_half, pl.ds((i % per_half) * CHUNK, CHUNK)
        total = total.astype(bf16).reshape(2, groups, tokens, CHUNK)
        for mate in range(2):
            if mate_at == 0:
                stage[mate, :, half, :, place] = total[mate]
            else:
                stage[:, half, mate, :, place] = total[mate]
        if i % per_half == per_half - 1:
            out_copy(half).start()

    widen((x_ref[...],), by_rows, wait, held, put)
    out_copy(0).wait()
    out_copy(1).wait()


def widen_next_kernel(layer, by_rows, riders, arrived, base, own, other, own_mate, other_mate, *rest):
    out_ref, x_out, held, sems, stage, out_sems = rest[riders : riders + 6]
    rides, in_sems = rest[riders + 6 :] if riders else (None, None)
    arrivals = [pltpu.make_async_copy(rest[i], rides.at[i], in_sems.at[i]) for i in range(riders)]
    copies = [
        pltpu.make_async_copy(rides.at[i], out_ref.at[:, :, 1 + i], out_sems.at[2 + i]) for i in range(riders)
    ]
    for copy in arrivals:
        copy.start()
    wait = load_weights(layer, by_rows, ((own, other), (own_mate, other_mate)), held, sems)
    width, per_half = base.shape[1] // 2, stage.shape[3] // CHUNK
    total = arrived[0].astype(f32)
    for i in range(1, arrived.shape[0]):
        total = total + arrived[i].astype(f32)
    x = (base[...].astype(f32) + total).astype(bf16)
    x_out[...] = x
    for arrival, copy in zip(arrivals, copies):
        arrival.wait()
        copy.start()

    def out_copy(half):
        return pltpu.make_async_copy(stage.at[:, half], out_ref.at[:, half, 0], out_sems.at[half])

    def put(i, total):
        half, at = i // per_half, (i % per_half) * CHUNK
        stage[:, half, :, pl.ds(at, CHUNK)] = total.astype(bf16).reshape(stage.shape[0], stage.shape[2], CHUNK)
        if i % per_half == per_half - 1:
            out_copy(half).start()

    widen((x[:, :width], x[:, width:]), by_rows, wait, held, put)
    for copy in [out_copy(0), out_copy(1)] + copies:
        copy.wait()


def narrow(by_rows, which, arrived, wait, held):
    per_half = arrived.shape[4] // CHUNK
    totals = [None, None]
    for i in range(held.shape[1]):
        left = arrived[:, i // per_half, which, :, pl.ds((i % per_half) * CHUNK, CHUNK)]
        left = left.reshape(left.shape[0] * left.shape[1], CHUNK)
        for part in range(2):
            wait(part, i)
            got = dot(left, held[part, i], ((1,), (0 if by_rows else 1,)))
            totals[part] = got if i == 0 else totals[part] + got
    return [total.astype(bf16) for total in totals]


def narrow_kernel(
    layer, by_rows, which, arrived, own, other, own_mate, other_mate, out_ref, held, sems, stage, out_sems
):
    wait = load_weights(layer, by_rows, ((own, other), (own_mate, other_mate)), held, sems)
    near, far = narrow(by_rows, which, arrived, wait, held)
    width = near.shape[1]
    stage[:, :width] = near
    stage[:, width:] = far
    copies = [
        pltpu.make_async_copy(stage, out_ref.at[i], out_sems.at[i]) for i in range(out_ref.shape[0])
    ]
    for copy in copies:
        copy.start()
    for copy in copies:
        copy.wait()


def held_scratch(weight, by_rows, parts):
    units = max(weight.shape)
    chunk = (CHUNK, weight.shape[1]) if by_rows else (weight.shape[0], CHUNK)
    return [
        pltpu.VMEM((parts, units // CHUNK) + chunk, bf16),
        pltpu.SemaphoreType.DMA((parts, units // CHUNK)),
    ]


def kernel_call(body, outs, out_specs, in_specs, scratch, operands, flops=0, moved=0):
    return pl.pallas_call(
        body,
        out_shape=outs,
        in_specs=in_specs,
        out_specs=out_specs,
        scratch_shapes=scratch,
        compiler_params=LIMIT,
        cost_estimate=pl.CostEstimate(flops=flops, bytes_accessed=moved, transcendentals=0),
    )(*operands)


def widen_first(layer, by_rows, mate_at, x, weights, blocks):
    shape = blocks[:mate_at] + (2,) + blocks[mate_at:]
    return kernel_call(
        functools.partial(widen_first_kernel, layer, by_rows, mate_at),
        shape_of(shape),
        HBM,
        [VMEM, HBM, HBM],
        held_scratch(weights[0], by_rows, 1) + [pltpu.VMEM(shape, bf16), pltpu.SemaphoreType.DMA((2,))],
        (x,) + weights[:2],
        flops=2 * x.shape[0] * weights[0].size,
        moved=2 * weights[0].size,
    )


def widen_next(layer, by_rows, arrived, base, weights, blocks, riders=()):
    return kernel_call(
        functools.partial(widen_next_kernel, layer, by_rows, len(riders)),
        (shape_of(blocks[:2] + (1 + len(riders),) + blocks[2:]), shape_of(base.shape)),
        (HBM, VMEM),
        [VMEM, VMEM] + [HBM] * (4 + len(riders)),
        held_scratch(weights[0], by_rows, 2)
        + [pltpu.VMEM(blocks, bf16), pltpu.SemaphoreType.DMA((2 + len(riders),))]
        + ([pltpu.VMEM((len(riders),) + blocks, bf16), pltpu.SemaphoreType.DMA((len(riders),))] if riders else []),
        (arrived, base) + weights + riders,
        flops=4 * base.shape[0] * weights[0].size,
        moved=4 * weights[0].size,
    )


def narrow_next(layer, by_rows, which, arrived, weights, copies):
    tokens, width = arrived.shape[0] * arrived.shape[3], 2 * min(weights[0].shape)
    return kernel_call(
        functools.partial(narrow_kernel, layer, by_rows, which),
        shape_of((copies, tokens, width)),
        HBM,
        [VMEM] + [HBM] * 4,
        held_scratch(weights[0], by_rows, 2)
        + [pltpu.VMEM((tokens, width), bf16), pltpu.SemaphoreType.DMA((copies,))],
        (arrived,) + weights,
        flops=4 * tokens * weights[0].size,
        moved=4 * weights[0].size,
    )


def summed(ref, kind, place):
    total = ref[0, kind, :, place].astype(f32)
    for i in range(1, ref.shape[0]):
        total = total + ref[i, kind, :, place].astype(f32)
    return total


def spread(stage, out_ref, sems):
    copies = [pltpu.make_async_copy(stage, out_ref.at[i], sems.at[i]) for i in range(out_ref.shape[0])]
    for copy in copies:
        copy.start()
    for copy in copies:
        copy.wait()


def act_first_kernel(arrived, out_ref, slope_ref, stage, sems):
    for at in range(0, arrived.shape[3], CHUNK):
        place = pl.ds(at, CHUNK)
        value, slope = gelu_both(summed(arrived, 0, place))
        stage[0, :, place] = value.astype(bf16)
        slope_ref[:, place] = slope
    spread(stage, out_ref, sems)


def act_last_kernel(arrived, out_ref, stage, sems):
    for at in range(0, arrived.shape[3], CHUNK):
        place = pl.ds(at, CHUNK)
        value, slope = gelu_both(summed(arrived, 0, place))
        stage[0, :, place] = (summed(arrived, 1, place) * slope).astype(bf16)
        stage[1, :, place] = value.astype(bf16)
    spread(stage, out_ref, sems)


def act_back_kernel(arrived, slope_ref, out_ref, stage, sems):
    for at in range(0, arrived.shape[3], CHUNK):
        place = pl.ds(at, CHUNK)
        stage[0, :, place] = (summed(arrived, 0, place) * slope_ref[:, place]).astype(bf16)
    spread(stage, out_ref, sems)


def activation(body, kinds, peers, piece, operands, in_specs, slope=False):
    outs, out_specs = [shape_of((peers, kinds) + piece)], [HBM]
    if slope:
        outs, out_specs = outs + [shape_of(piece, f32)], out_specs + [VMEM]
    return kernel_call(
        body,
        outs,
        out_specs,
        in_specs,
        [pltpu.VMEM((kinds,) + piece, bf16), pltpu.SemaphoreType.DMA((peers,))],
        operands,
        flops=2000000,
        moved=2000000,
    )


def finish_kernel(arrived, x1, g1, states, grads):
    total = arrived[0].astype(f32)
    for i in range(1, arrived.shape[0]):
        total = total + arrived[i].astype(f32)

    def ended(base):
        return (base[...].astype(f32) + total).astype(bf16)

    @pl.when(lax.axis_index("section") == 0)
    def _():
        states[...] = x1[...]
        grads[...] = ended(g1)

    @pl.when(lax.axis_index("section") == 1)
    def _():
        states[...] = ended(x1)
        grads[...] = g1[...]


def pick_copies(layer0, layer1, kind, held, sems, start):
    section = lax.axis_index("section")

    def copy(layer, i):
        source = (layer0, layer1)[layer][i].at[:, :, 0 if layer == 0 else kind]
        return pltpu.make_async_copy(source, held.at[i], sems.at[i])

    if start:
        for layer in range(2):

            @pl.when(section == layer)
            def _():
                for i in range(4):
                    copy(layer, i).start()
    else:
        for i in range(4):
            copy(0, i).wait()


def step_chunk(held, step):
    per_half = held.shape[4] // CHUNK
    place = pl.ds(pl.multiple_of((step % per_half) * CHUNK, CHUNK), CHUNK)
    return held[:, :, step // per_half, :, place].reshape(-1, CHUNK)


def grad_down_kernel(g_ref, *refs):
    layer0, layer1, (out_ref, held, sems) = refs[:4], refs[4:8], refs[8:]
    step = pl.program_id(0)

    @pl.when(step == 0)
    def _():
        pick_copies(layer0, layer1, 1, held, sems, True)
        pick_copies(layer0, layer1, 1, held, sems, False)

    out_ref[...] = dot(step_chunk(held, step), g_ref[...], ((0,), (0,)))


def grad_up_kernel(x_ref, *refs):
    layer0, layer1, (out_ref, held, turned, sems) = refs[:4], refs[4:8], refs[8:]
    step = pl.program_id(0)

    @pl.when(step == 0)
    def _():
        pick_copies(layer0, layer1, 0, held, sems, True)
        turned[...] = x_ref[...].T
        pick_copies(layer0, layer1, 0, held, sems, False)

    out_ref[...] = dot(turned[...], step_chunk(held, step), ((1,), (0,)))


def weight_grad(down, narrow, layer0, layer1):
    groups, halves, _, tokens, wide = layer0[0].shape
    units, (all_tokens, width) = halves * wide, narrow.shape
    shape, block = ((units, width), (CHUNK, width)) if down else ((width, units), (width, CHUNK))
    turned = [] if down else [pltpu.VMEM((width, all_tokens), bf16)]
    return pl.pallas_call(
        grad_down_kernel if down else grad_up_kernel,
        out_shape=shape_of(shape, f32),
        grid=(units // CHUNK,),
        in_specs=[pl.BlockSpec(narrow.shape, lambda i: (0, 0))] + [HBM] * 8,
        out_specs=pl.BlockSpec(block, lambda i: (i, 0) if down else (0, i)),
        scratch_shapes=[pltpu.VMEM((4, groups, halves, tokens, wide), bf16)]
        + turned
        + [pltpu.SemaphoreType.DMA((4,))],
        compiler_params=LIMIT,
        cost_estimate=pl.CostEstimate(
            flops=2 * narrow.size * units, bytes_accessed=4 * width * units, transcendentals=0
        ),
    )(narrow, *layer0, *layer1)


def last_kernel(up, down, *refs):
    layer0, layer1, rest = refs[:4], refs[4:8], refs[8:]
    out_ref, held, up_held, down_held, stage, sems, up_sems, down_sems, out_sem = rest
    section, mate_pos = lax.axis_index("section"), lax.axis_index("x_lo")
    groups, halves, tokens, wide = held.shape[1:]
    per_half, count = wide // CHUNK, up_held.shape[0]
    pick_copies(layer0, layer1, 1, held, sems, True)

    def run(weight, by_rows, weight_held, weight_sems):
        copies = []
        for i in range(count):
            where = pl.ds(i * CHUNK, CHUNK)
            source = weight.at[where, :] if by_rows else weight.at[:, where]
            copies.append(pltpu.make_async_copy(source, weight_held.at[i], weight_sems.at[i]))
        for copy in copies:
            copy.start()
        pick_copies(layer0, layer1, 1, held, sems, False)
        total = None
        for i in range(count):
            left = held[:, :, i // per_half, :, pl.ds((i % per_half) * CHUNK, CHUNK)].reshape(-1, CHUNK)
            copies[i].wait()
            got = dot(left, weight_held[i], ((1,), (0 if by_rows else 1,)))
            total = got if total is None else total + got
        total = total.astype(bf16).reshape(4, groups, tokens, -1)
        for i in range(4):
            half = mate_pos if i < 2 else 1 - mate_pos
            which = section if i % 2 == 0 else 1 - section
            stage[pl.ds(half * groups, groups), which] = total[i]

    pl.when(section == 0)(lambda: run(up, False, up_held, up_sems))
    pl.when(section == 1)(lambda: run(down, True, down_held, down_sems))
    copy = pltpu.make_async_copy(stage, out_ref, out_sem)
    copy.start()
    copy.wait()


def last_product(up, down, layer0, layer1):
    groups, halves, _, tokens, wide = layer0[0].shape
    width, units = up.shape
    out = (2 * groups, 2, tokens, width)
    return kernel_call(
        last_kernel,
        shape_of(out),
        HBM,
        [HBM] * 10,
        [
            pltpu.VMEM((4, groups, halves, tokens, wide), bf16),
            pltpu.VMEM((units // CHUNK, width, CHUNK), bf16),
            pltpu.VMEM((units // CHUNK, CHUNK, width), bf16),
            pltpu.VMEM(out, bf16),
            pltpu.SemaphoreType.DMA((4,)),
            pltpu.SemaphoreType.DMA((units // CHUNK,)),
            pltpu.SemaphoreType.DMA((units // CHUNK,)),
            pltpu.SemaphoreType.DMA,
        ],
        (up, down) + layer0 + layer1,
        flops=8 * groups * tokens * up.size,
        moved=6 * up.size,
    )


def exchange(blocks, axes):
    return lax.all_to_all(blocks, axes, 0, 0)


CORES = ("section", "x_lo")


def to_other_core(block):
    return lax.ppermute(block, "section", [(0, 1), (1, 0)])


def to_mate(block):
    return lax.ppermute(block, "x_lo", [(0, 1), (1, 0)])


def to_other_core_of_mate(block):
    return lax.ppermute(block, CORES, [(0, 3), (3, 0), (1, 2), (2, 1)])


def only_to_mate(block, section):
    at = 2 * section
    return lax.ppermute(block, CORES, [(at, at + 1), (at + 1, at)])


def only_to_core(block, section):
    return lax.ppermute(block, "section", [(1 - section, section)])


def to_owner(block, section):
    at, source = 2 * section, 2 * (1 - section)
    across = lax.ppermute(block, CORES, [(source, at + 1), (source + 1, at)])
    return block, only_to_core(block, section), only_to_mate(block, section), across


def late(block, after):
    return lax.optimization_barrier((block, after))[0]


def local(inputs, cotangent, w_up, w_down):
    col = ("y", "x_hi")
    section, mate_pos, col_pos = (lax.axis_index(name) for name in ("section", "x_lo", col))
    first = section == 0
    own_up, own_down = w_up[0], w_down[0]
    tokens, width = inputs.shape[1:]
    half_len = tokens // 2
    rings = lax.axis_size("z")
    piece = (tokens // rings, own_up.shape[1] // 2)
    blocks = (half_len // piece[0], 2) + piece

    def half_of(array, which):
        return lax.dynamic_slice_in_dim(array, which * half_len, half_len, 0)

    def batch(array, which):
        return lax.dynamic_index_in_dim(array, which, 0, keepdims=False)

    def both_widths(array):
        return jnp.concatenate([half_of(array, mate_pos), to_mate(half_of(array, 1 - mate_pos))], axis=1)

    x0, g2 = batch(inputs, section), batch(cotangent, section)
    other_up = to_other_core(own_up)
    first_part = widen_first(0, False, 2, x0, (own_up, other_up), blocks)
    mate_down0 = only_to_mate(late(own_down, other_up), 0)
    arrived = exchange(first_part.reshape((2 * rings, 1) + piece), ("z", "x_lo"))

    other_down = to_other_core(late(own_down, other_up))
    d_hid1 = widen_first(1, True, 0, late(g2, first_part), (own_down, other_down), blocks)
    arrived, mate_down0 = late((arrived, mate_down0), d_hid1)
    d_hid1, given = batch(d_hid1, mate_pos), to_mate(batch(d_hid1, 1 - mate_pos))
    down0 = own_down, other_down, mate_down0, only_to_core(mate_down0, 1)

    value0, slope0 = activation(act_first_kernel, 1, rings, piece, (arrived,), [VMEM], slope=True)
    mate_up1 = only_to_mate(late(own_up, value0), 1)
    hid0 = exchange(value0, "z").reshape(blocks[:2] + (1,) + piece)
    x0_both, g2_both = (both_widths(late(array, value0)) for array in (x0, g2))
    d_hid1 = (d_hid1.astype(f32) + late(given, value0).astype(f32)).astype(bf16)
    hid0 = late(hid0, d_hid1)
    part = narrow_next(0, True, 0, hid0, down0, lax.axis_size(col))
    mate_up1, x0_both, g2_both = late((mate_up1, x0_both, g2_both), part)
    up1 = own_up, other_up, mate_up1, only_to_core(mate_up1, 0)
    arrived = exchange(part, col)

    pre1, x1 = widen_next(1, False, arrived, x0_both, up1, blocks, (d_hid1,))
    hid0s = to_owner(late(hid0, pre1), 0)
    arrived = exchange(pre1.reshape((rings, 2) + piece), "z")
    (acts1,) = activation(act_last_kernel, 2, rings, piece, (arrived,), [VMEM])
    acts1 = late(exchange(acts1, "z").reshape(blocks[:2] + (2,) + piece), hid0s)
    part = narrow_next(1, False, 0, acts1, up1, lax.axis_size(col))
    arrived = exchange(part, col)

    d_hid0, g1 = widen_next(0, True, arrived, g2_both, down0, blocks)
    acts1, both1 = late((acts1, jnp.stack([x1, g1])), d_hid0)
    acts1s = to_owner(acts1, 1)
    arrived = exchange(d_hid0.reshape((rings, 1) + piece), "z")
    near, far = both1[..., :width], both1[..., width:]
    both1 = jnp.stack([near, to_other_core(near), to_mate(far), to_other_core_of_mate(far)])
    both1 = both1.reshape((2, 2) + near.shape)

    def all_tokens(array):
        return jnp.concatenate(
            [
                half_of(batch(array, which), half)
                for half in (mate_pos, 1 - mate_pos)
                for which in (section, 1 - section)
            ]
        )

    x1s, g1s = both1[:, :, 0].reshape(2 * tokens, width), both1[:, :, 1].reshape(2 * tokens, width)
    xs = jnp.where(first, all_tokens(inputs), x1s)
    gs = jnp.where(first, g1s, all_tokens(cotangent))

    (d_pre0,) = activation(act_back_kernel, 1, rings, piece, (arrived, slope0), [VMEM, VMEM])
    d_pre0 = late(exchange(d_pre0, "z").reshape(blocks[:2] + (1,) + piece), acts1s)
    down_grad = weight_grad(True, late(gs, d_pre0), hid0s, acts1s)
    d_pre0s = late(to_owner(d_pre0, 0), down_grad)

    last = last_product(own_up, own_down, d_pre0s, acts1s)
    xs, d_pre0s = late((xs, d_pre0s), last)
    arrived = exchange(last, col)
    up_grad = weight_grad(False, xs, d_pre0s, acts1s)

    out_len = tokens // lax.axis_size(col)
    per_half = half_len // out_len
    away = jnp.where(col_pos // per_half == mate_pos, 0, 1)
    pieces = lax.dynamic_index_in_dim(both1, away, 0, keepdims=False)
    pieces = lax.dynamic_slice_in_dim(pieces, (col_pos % per_half) * out_len, out_len, 2)
    pieces = jnp.where(first, pieces, pieces[::-1])
    states, grads = kernel_call(
        finish_kernel,
        [shape_of(pieces[:, 0].shape)] * 2,
        [VMEM] * 2,
        [VMEM] * 3,
        [],
        (arrived, pieces[:, 0], pieces[:, 1]),
        flops=100000,
        moved=200000,
    )
    return states[None], grads[None], up_grad[None], down_grad[None]


def solution(mesh):
    sections, rows, cols = mesh.devices.shape
    finer = Mesh(
        mesh.devices.reshape(sections, rows // 2, 2, cols // 2, 2),
        ("section", "z", "x_lo", "y", "x_hi"),
    )
    row, col = ("z", "x_lo"), ("y", "x_hi")
    in_specs = (
        P(None, None, row),
        P(None, None, row),
        P("section", row, col),
        P("section", col, row),
    )
    out_specs = (
        P("section", None, col, row),
        P("section", None, col, row),
        P("section", row, col),
        P("section", col, row),
    )
    return jax.shard_map(local, mesh=finer, in_specs=in_specs, out_specs=out_specs, check_vma=False)
```

```python
import functools

import jax
import jax.numpy as jnp
from jax import lax
from jax.experimental import pallas as pl
from jax.experimental.pallas import tpu as pltpu
from jax.sharding import Mesh, PartitionSpec as P

root_two_over_pi = 0.7978845608028654
cubic = 0.044715
f32 = jnp.float32
bf16 = jnp.bfloat16
CHUNK = 512
VMEM = pl.BlockSpec(memory_space=pltpu.VMEM)
HBM = pl.BlockSpec(memory_space=pltpu.HBM)
ANY = pl.BlockSpec(memory_space=pl.ANY)
LIMIT = pltpu.CompilerParams(vmem_limit_bytes=64 * 1024 * 1024)


def gelu_both(pre):
    inner = root_two_over_pi * (pre + cubic * pre * pre * pre)
    tangent = jnp.tanh(inner)
    value = 0.5 * pre * (1.0 + tangent)
    slope = 0.5 * (1.0 + tangent) + 0.5 * pre * (1.0 - tangent * tangent) * root_two_over_pi * (
        1.0 + 3.0 * cubic * pre * pre
    )
    return value, slope


def dot(left, right, dims):
    return lax.dot_general(left, right, (dims, ((), ())), preferred_element_type=f32)


def shape_of(shape, dtype=bf16):
    return jax.ShapeDtypeStruct(shape, dtype)


def load_weights(layer, by_rows, refs, held, sems):
    mine = lax.axis_index("section") == layer

    def copy(source, part, i):
        where = pl.ds(i * CHUNK, CHUNK)
        block = source.at[where, :] if by_rows else source.at[:, where]
        return pltpu.make_async_copy(block, held.at[part, i], sems.at[part, i])

    def start(which):
        for i in range(held.shape[1]):
            for part, pair in enumerate(refs):
                copy(pair[which], part, i).start()

    pl.when(mine)(lambda: start(0))
    pl.when(jnp.logical_not(mine))(lambda: start(1))
    return lambda part, i: copy(refs[part][0], part, i).wait()


def widen(xs, by_rows, wait, held, put):
    for i in range(held.shape[1]):
        total = None
        for part, x in enumerate(xs):
            wait(part, i)
            got = dot(x, held[part, i], ((1,), (1 if by_rows else 0,)))
            total = got if total is None else total + got
        put(i, total)


def widen_first_kernel(layer, by_rows, mate_at, x_ref, own, other, out_ref, held, sems, stage, out_sems):
    wait = load_weights(layer, by_rows, ((own, other),), held, sems)
    groups, tokens, wide = stage.shape[1 if mate_at == 0 else 0], stage.shape[3], stage.shape[4]
    per_half = wide // CHUNK

    def out_copy(half):
        where = (slice(None),) * (2 if mate_at == 0 else 1) + (half,)
        return pltpu.make_async_copy(stage.at[where], out_ref.at[where], out_sems.at[half])

    def put(i, total):
        half, place = i // per_half, pl.ds((i % per_half) * CHUNK, CHUNK)
        total = total.astype(bf16).reshape(2, groups, tokens, CHUNK)
        for mate in range(2):
            if mate_at == 0:
                stage[mate, :, half, :, place] = total[mate]
            else:
                stage[:, half, mate, :, place] = total[mate]
        if i % per_half == per_half - 1:
            out_copy(half).start()

    widen((x_ref[lax.axis_index("section")],), by_rows, wait, held, put)
    out_copy(0).wait()
    out_copy(1).wait()


def widen_next_kernel(layer, by_rows, riders, arrived, base, own, other, own_mate, other_mate, *rest):
    out_ref, x_out, held, sems, stage, out_sems = rest[riders : riders + 6]
    rides, in_sems = rest[riders + 6 :] if riders else (None, None)
    arrivals = [pltpu.make_async_copy(rest[i], rides.at[i], in_sems.at[i]) for i in range(riders)]
    copies = [
        pltpu.make_async_copy(rides.at[i], out_ref.at[:, :, 1 + i], out_sems.at[2 + i]) for i in range(riders)
    ]
    for copy in arrivals:
        copy.start()
    wait = load_weights(layer, by_rows, ((own, other), (own_mate, other_mate)), held, sems)
    width, per_half = base.shape[1] // 2, stage.shape[3] // CHUNK
    total = arrived[0].astype(f32)
    for i in range(1, arrived.shape[0]):
        total = total + arrived[i].astype(f32)
    x = (base[...].astype(f32) + total).astype(bf16)
    x_out[...] = x
    for arrival, copy in zip(arrivals, copies):
        arrival.wait()
        copy.start()

    def out_copy(half):
        return pltpu.make_async_copy(stage.at[:, half], out_ref.at[:, half, 0], out_sems.at[half])

    def put(i, total):
        half, at = i // per_half, (i % per_half) * CHUNK
        stage[:, half, :, pl.ds(at, CHUNK)] = total.astype(bf16).reshape(stage.shape[0], stage.shape[2], CHUNK)
        if i % per_half == per_half - 1:
            out_copy(half).start()

    widen((x[:, :width], x[:, width:]), by_rows, wait, held, put)
    for copy in [out_copy(0), out_copy(1)] + copies:
        copy.wait()


def narrow(by_rows, which, arrived, wait, held):
    per_half = arrived.shape[4] // CHUNK
    totals = [None, None]
    for i in range(held.shape[1]):
        left = arrived[:, i // per_half, which, :, pl.ds((i % per_half) * CHUNK, CHUNK)]
        left = left.reshape(left.shape[0] * left.shape[1], CHUNK)
        for part in range(2):
            wait(part, i)
            got = dot(left, held[part, i], ((1,), (0 if by_rows else 1,)))
            totals[part] = got if i == 0 else totals[part] + got
    return [total.astype(bf16) for total in totals]


def narrow_kernel(
    layer, by_rows, which, arrived, own, other, own_mate, other_mate, out_ref, held, sems, stage, out_sems
):
    wait = load_weights(layer, by_rows, ((own, other), (own_mate, other_mate)), held, sems)
    near, far = narrow(by_rows, which, arrived, wait, held)
    width = near.shape[1]
    stage[:, :width] = near
    stage[:, width:] = far
    copies = [
        pltpu.make_async_copy(stage, out_ref.at[i], out_sems.at[i]) for i in range(out_ref.shape[0])
    ]
    for copy in copies:
        copy.start()
    for copy in copies:
        copy.wait()


def held_scratch(weight, by_rows, parts):
    units = max(weight.shape)
    chunk = (CHUNK, weight.shape[1]) if by_rows else (weight.shape[0], CHUNK)
    return [
        pltpu.VMEM((parts, units // CHUNK) + chunk, bf16),
        pltpu.SemaphoreType.DMA((parts, units // CHUNK)),
    ]


def kernel_call(body, outs, out_specs, in_specs, scratch, operands, flops=0, moved=0):
    return pl.pallas_call(
        body,
        out_shape=outs,
        in_specs=in_specs,
        out_specs=out_specs,
        scratch_shapes=scratch,
        compiler_params=LIMIT,
        cost_estimate=pl.CostEstimate(flops=flops, bytes_accessed=moved, transcendentals=0),
    )(*operands)


def widen_first(layer, by_rows, mate_at, x, weights, blocks):
    shape = blocks[:mate_at] + (2,) + blocks[mate_at:]
    return kernel_call(
        functools.partial(widen_first_kernel, layer, by_rows, mate_at),
        shape_of(shape),
        HBM,
        [VMEM, HBM, HBM],
        held_scratch(weights[0], by_rows, 1) + [pltpu.VMEM(shape, bf16), pltpu.SemaphoreType.DMA((2,))],
        (x,) + weights[:2],
        flops=2 * x.shape[1] * weights[0].size,
        moved=2 * weights[0].size,
    )


def widen_next(layer, by_rows, arrived, base, weights, blocks, riders=()):
    return kernel_call(
        functools.partial(widen_next_kernel, layer, by_rows, len(riders)),
        (shape_of(blocks[:2] + (1 + len(riders),) + blocks[2:]), shape_of(base.shape)),
        (HBM, VMEM),
        [VMEM, VMEM] + [HBM] * (4 + len(riders)),
        held_scratch(weights[0], by_rows, 2)
        + [pltpu.VMEM(blocks, bf16), pltpu.SemaphoreType.DMA((2 + len(riders),))]
        + ([pltpu.VMEM((len(riders),) + blocks, bf16), pltpu.SemaphoreType.DMA((len(riders),))] if riders else []),
        (arrived, base) + weights + riders,
        flops=4 * base.shape[0] * weights[0].size,
        moved=4 * weights[0].size,
    )


def narrow_next(layer, by_rows, which, arrived, weights, copies):
    tokens, width = arrived.shape[0] * arrived.shape[3], 2 * min(weights[0].shape)
    return kernel_call(
        functools.partial(narrow_kernel, layer, by_rows, which),
        shape_of((copies, tokens, width)),
        HBM,
        [VMEM] + [HBM] * 4,
        held_scratch(weights[0], by_rows, 2)
        + [pltpu.VMEM((tokens, width), bf16), pltpu.SemaphoreType.DMA((copies,))],
        (arrived,) + weights,
        flops=4 * tokens * weights[0].size,
        moved=4 * weights[0].size,
    )


def summed(ref, kind, place):
    total = ref[0, kind, :, place].astype(f32)
    for i in range(1, ref.shape[0]):
        total = total + ref[i, kind, :, place].astype(f32)
    return total


def spread(stage, out_ref, sems):
    copies = [pltpu.make_async_copy(stage, out_ref.at[i], sems.at[i]) for i in range(out_ref.shape[0])]
    for copy in copies:
        copy.start()
    for copy in copies:
        copy.wait()


def act_first_kernel(arrived, out_ref, slope_ref, stage, sems):
    for at in range(0, arrived.shape[3], CHUNK):
        place = pl.ds(at, CHUNK)
        value, slope = gelu_both(summed(arrived, 0, place))
        stage[0, :, place] = value.astype(bf16)
        slope_ref[:, place] = slope
    spread(stage, out_ref, sems)


def act_last_kernel(arrived, out_ref, stage, sems):
    for at in range(0, arrived.shape[3], CHUNK):
        place = pl.ds(at, CHUNK)
        value, slope = gelu_both(summed(arrived, 0, place))
        stage[0, :, place] = (summed(arrived, 1, place) * slope).astype(bf16)
        stage[1, :, place] = value.astype(bf16)
    spread(stage, out_ref, sems)


def act_back_kernel(arrived, slope_ref, out_ref, stage, sems):
    for at in range(0, arrived.shape[3], CHUNK):
        place = pl.ds(at, CHUNK)
        stage[0, :, place] = (summed(arrived, 0, place) * slope_ref[:, place]).astype(bf16)
    spread(stage, out_ref, sems)


def activation(body, kinds, peers, piece, operands, in_specs, slope=False):
    outs, out_specs = [shape_of((peers, kinds) + piece)], [HBM]
    if slope:
        outs, out_specs = outs + [shape_of(piece, f32)], out_specs + [VMEM]
    return kernel_call(
        body,
        outs,
        out_specs,
        in_specs,
        [pltpu.VMEM((kinds,) + piece, bf16), pltpu.SemaphoreType.DMA((peers,))],
        operands,
        flops=2000000,
        moved=2000000,
    )


def finish_kernel(arrived, x1, g1, states, grads):
    total = arrived[0].astype(f32)
    for i in range(1, arrived.shape[0]):
        total = total + arrived[i].astype(f32)

    def ended(base):
        return (base[...].astype(f32) + total).astype(bf16)

    @pl.when(lax.axis_index("section") == 0)
    def _():
        states[...] = x1[...]
        grads[...] = ended(g1)

    @pl.when(lax.axis_index("section") == 1)
    def _():
        states[...] = ended(x1)
        grads[...] = g1[...]


def pick_copies(layer0, layer1, kind, held, sems, start):
    section = lax.axis_index("section")

    def copy(layer, i):
        source = (layer0, layer1)[layer][i].at[:, :, 0 if layer == 0 else kind]
        return pltpu.make_async_copy(source, held.at[i], sems.at[i])

    if start:
        for layer in range(2):

            @pl.when(section == layer)
            def _():
                for i in range(4):
                    copy(layer, i).start()
    else:
        for i in range(4):
            copy(0, i).wait()


def step_chunk(held, step):
    per_half = held.shape[4] // CHUNK
    place = pl.ds(pl.multiple_of((step % per_half) * CHUNK, CHUNK), CHUNK)
    return held[:, :, step // per_half, :, place].reshape(-1, CHUNK)


def fill_tokens(into, layer, full_ref, traded_ref):
    section, mate_pos = lax.axis_index("section"), lax.axis_index("x_lo")
    half_len = full_ref.shape[1] // 2

    @pl.when(section == layer)
    def _():
        for i in range(4):
            half = mate_pos if i < 2 else 1 - mate_pos
            which = section if i % 2 == 0 else 1 - section
            place = pl.ds(pl.multiple_of(half * half_len, half_len), half_len)
            into[pl.ds(i * half_len, half_len), :] = full_ref[which, place, :]

    @pl.when(section != layer)
    def _():
        into[...] = traded_ref[...]


def grad_down_kernel(full_ref, traded_ref, *refs):
    layer0, layer1, (out_ref, held, narrow, sems) = refs[:4], refs[4:8], refs[8:]
    step = pl.program_id(0)

    @pl.when(step == 0)
    def _():
        pick_copies(layer0, layer1, 1, held, sems, True)
        fill_tokens(narrow, 1, full_ref, traded_ref)
        pick_copies(layer0, layer1, 1, held, sems, False)

    out_ref[...] = dot(step_chunk(held, step), narrow[...], ((0,), (0,)))


def grad_up_kernel(full_ref, traded_ref, *refs):
    layer0, layer1, (out_ref, held, narrow, turned, sems) = refs[:4], refs[4:8], refs[8:]
    step = pl.program_id(0)

    @pl.when(step == 0)
    def _():
        pick_copies(layer0, layer1, 0, held, sems, True)
        fill_tokens(narrow, 0, full_ref, traded_ref)
        turned[...] = narrow[...].T
        pick_copies(layer0, layer1, 0, held, sems, False)

    out_ref[...] = dot(turned[...], step_chunk(held, step), ((1,), (0,)))


def weight_grad(down, full, traded, layer0, layer1):
    groups, halves, _, tokens, wide = layer0[0].shape
    units, (all_tokens, width) = halves * wide, traded.shape
    shape, block = ((units, width), (CHUNK, width)) if down else ((width, units), (width, CHUNK))
    turned = [] if down else [pltpu.VMEM((width, all_tokens), bf16)]
    return pl.pallas_call(
        grad_down_kernel if down else grad_up_kernel,
        out_shape=shape_of(shape, f32),
        grid=(units // CHUNK,),
        in_specs=[
            pl.BlockSpec(full.shape, lambda i: (0, 0, 0)),
            pl.BlockSpec(traded.shape, lambda i: (0, 0)),
        ]
        + [HBM] * 8,
        out_specs=pl.BlockSpec(block, lambda i: (i, 0) if down else (0, i)),
        scratch_shapes=[
            pltpu.VMEM((4, groups, halves, tokens, wide), bf16),
            pltpu.VMEM((all_tokens, width), bf16),
        ]
        + turned
        + [pltpu.SemaphoreType.DMA((4,))],
        compiler_params=LIMIT,
        cost_estimate=pl.CostEstimate(
            flops=2 * traded.size * units, bytes_accessed=4 * width * units, transcendentals=0
        ),
    )(full, traded, *layer0, *layer1)


def last_kernel(up, down, *refs):
    layer0, layer1, rest = refs[:4], refs[4:8], refs[8:]
    out_ref, held, up_held, down_held, stage, sems, up_sems, down_sems, out_sem = rest
    section, mate_pos = lax.axis_index("section"), lax.axis_index("x_lo")
    groups, halves, tokens, wide = held.shape[1:]
    per_half, count = wide // CHUNK, up_held.shape[0]
    pick_copies(layer0, layer1, 1, held, sems, True)

    def run(weight, by_rows, weight_held, weight_sems):
        copies = []
        for i in range(count):
            where = pl.ds(i * CHUNK, CHUNK)
            source = weight.at[where, :] if by_rows else weight.at[:, where]
            copies.append(pltpu.make_async_copy(source, weight_held.at[i], weight_sems.at[i]))
        for copy in copies:
            copy.start()
        pick_copies(layer0, layer1, 1, held, sems, False)
        total = None
        for i in range(count):
            left = held[:, :, i // per_half, :, pl.ds((i % per_half) * CHUNK, CHUNK)].reshape(-1, CHUNK)
            copies[i].wait()
            got = dot(left, weight_held[i], ((1,), (0 if by_rows else 1,)))
            total = got if total is None else total + got
        total = total.astype(bf16).reshape(4, groups, tokens, -1)
        for i in range(4):
            half = mate_pos if i < 2 else 1 - mate_pos
            which = section if i % 2 == 0 else 1 - section
            stage[pl.ds(half * groups, groups), which] = total[i]

    pl.when(section == 0)(lambda: run(up, False, up_held, up_sems))
    pl.when(section == 1)(lambda: run(down, True, down_held, down_sems))
    copy = pltpu.make_async_copy(stage, out_ref, out_sem)
    copy.start()
    copy.wait()


def last_product(up, down, layer0, layer1):
    groups, halves, _, tokens, wide = layer0[0].shape
    width, units = up.shape
    out = (2 * groups, 2, tokens, width)
    return kernel_call(
        last_kernel,
        shape_of(out),
        HBM,
        [HBM] * 10,
        [
            pltpu.VMEM((4, groups, halves, tokens, wide), bf16),
            pltpu.VMEM((units // CHUNK, width, CHUNK), bf16),
            pltpu.VMEM((units // CHUNK, CHUNK, width), bf16),
            pltpu.VMEM(out, bf16),
            pltpu.SemaphoreType.DMA((4,)),
            pltpu.SemaphoreType.DMA((units // CHUNK,)),
            pltpu.SemaphoreType.DMA((units // CHUNK,)),
            pltpu.SemaphoreType.DMA,
        ],
        (up, down) + layer0 + layer1,
        flops=8 * groups * tokens * up.size,
        moved=6 * up.size,
    )


def exchange(blocks, axes):
    return lax.all_to_all(blocks, axes, 0, 0)


CORES = ("section", "x_lo")


def to_other_core(block):
    return lax.ppermute(block, "section", [(0, 1), (1, 0)])


def to_mate(block):
    return lax.ppermute(block, "x_lo", [(0, 1), (1, 0)])


def to_other_core_of_mate(block):
    return lax.ppermute(block, CORES, [(0, 3), (3, 0), (1, 2), (2, 1)])


def only_to_mate(block, section):
    at = 2 * section
    return lax.ppermute(block, CORES, [(at, at + 1), (at + 1, at)])


def only_to_core(block, section):
    return lax.ppermute(block, "section", [(1 - section, section)])


def to_owner(block, section):
    at, source = 2 * section, 2 * (1 - section)
    across = lax.ppermute(block, CORES, [(source, at + 1), (source + 1, at)])
    return block, only_to_core(block, section), only_to_mate(block, section), across


def late(block, after):
    return lax.optimization_barrier((block, after))[0]


def local(inputs, cotangent, w_up, w_down):
    col = ("y", "x_hi")
    section, mate_pos, col_pos = (lax.axis_index(name) for name in ("section", "x_lo", col))
    first = section == 0
    own_up, own_down = w_up[0], w_down[0]
    tokens, width = inputs.shape[1:]
    half_len = tokens // 2
    rings = lax.axis_size("z")
    piece = (tokens // rings, own_up.shape[1] // 2)
    blocks = (half_len // piece[0], 2) + piece

    def half_of(array, which):
        return lax.dynamic_slice_in_dim(array, which * half_len, half_len, 0)

    def batch(array, which):
        return lax.dynamic_index_in_dim(array, which, 0, keepdims=False)

    def both_widths(array):
        def cut(half):
            place = section, half * half_len, 0
            return lax.dynamic_slice(array, place, (1, half_len, width))[0]

        return jnp.concatenate([cut(mate_pos), to_mate(cut(1 - mate_pos))], axis=1)

    other_up = to_other_core(own_up)
    first_part = widen_first(0, False, 2, inputs, (own_up, other_up), blocks)
    mate_down0 = only_to_mate(late(own_down, other_up), 0)
    arrived = exchange(first_part.reshape((2 * rings, 1) + piece), ("z", "x_lo"))

    other_down = to_other_core(late(own_down, other_up))
    d_hid1 = widen_first(1, True, 0, late(cotangent, first_part), (own_down, other_down), blocks)
    arrived, mate_down0 = late((arrived, mate_down0), d_hid1)
    d_hid1, given = batch(d_hid1, mate_pos), to_mate(batch(d_hid1, 1 - mate_pos))
    down0 = own_down, other_down, mate_down0, only_to_core(mate_down0, 1)

    value0, slope0 = activation(act_first_kernel, 1, rings, piece, (arrived,), [VMEM], slope=True)
    mate_up1 = only_to_mate(late(own_up, (value0, given)), 1)
    hid0 = exchange(value0, "z").reshape(blocks[:2] + (1,) + piece)
    x0_both, g2_both = (both_widths(late(array, value0)) for array in (inputs, cotangent))
    d_hid1 = (d_hid1.astype(f32) + late(given, value0).astype(f32)).astype(bf16)
    hid0 = late(hid0, d_hid1)
    part = narrow_next(0, True, 0, hid0, down0, lax.axis_size(col))
    mate_up1, x0_both, g2_both = late((mate_up1, x0_both, g2_both), part)
    up1 = own_up, other_up, mate_up1, only_to_core(mate_up1, 0)
    arrived = exchange(part, col)

    pre1, x1 = widen_next(1, False, arrived, x0_both, up1, blocks, (d_hid1,))
    hid0s = to_owner(late(hid0, pre1), 0)
    arrived = exchange(pre1.reshape((rings, 2) + piece), "z")
    (acts1,) = activation(act_last_kernel, 2, rings, piece, (arrived,), [VMEM])
    acts1 = late(exchange(acts1, "z").reshape(blocks[:2] + (2,) + piece), hid0s)
    part = narrow_next(1, False, 0, acts1, up1, lax.axis_size(col))
    arrived = exchange(part, col)

    d_hid0, g1 = widen_next(0, True, arrived, g2_both, down0, blocks)
    acts1, both1 = late((acts1, jnp.stack([x1, g1])), d_hid0)
    acts1s = to_owner(acts1, 1)
    arrived = exchange(d_hid0.reshape((rings, 1) + piece), "z")
    near, far = both1[..., :width], both1[..., width:]
    both1 = jnp.stack([near, to_other_core(near), to_mate(far), to_other_core_of_mate(far)])
    both1 = both1.reshape((2, 2) + near.shape)

    x1s, g1s = both1[:, :, 0].reshape(2 * tokens, width), both1[:, :, 1].reshape(2 * tokens, width)

    (d_pre0,) = activation(act_back_kernel, 1, rings, piece, (arrived, slope0), [VMEM, VMEM])
    d_pre0 = late(exchange(d_pre0, "z").reshape(blocks[:2] + (1,) + piece), acts1s)
    down_grad = weight_grad(True, cotangent, late(g1s, d_pre0), hid0s, acts1s)
    d_pre0s = late(to_owner(d_pre0, 0), down_grad)

    last = last_product(own_up, own_down, d_pre0s, acts1s)
    x1s, d_pre0s = late((x1s, d_pre0s), last)
    arrived = exchange(last, col)
    up_grad = weight_grad(False, inputs, x1s, d_pre0s, acts1s)

    out_len = tokens // lax.axis_size(col)
    per_half = half_len // out_len
    away = jnp.where(col_pos // per_half == mate_pos, 0, 1)
    pieces = lax.dynamic_index_in_dim(both1, away, 0, keepdims=False)
    pieces = lax.dynamic_slice_in_dim(pieces, (col_pos % per_half) * out_len, out_len, 2)
    pieces = jnp.where(first, pieces, pieces[::-1])
    states, grads = kernel_call(
        finish_kernel,
        [shape_of(pieces[:, 0].shape)] * 2,
        [VMEM] * 2,
        [VMEM] * 3,
        [],
        (arrived, pieces[:, 0], pieces[:, 1]),
        flops=100000,
        moved=200000,
    )
    return states[None], grads[None], up_grad[None], down_grad[None]


def solution(mesh):
    sections, rows, cols = mesh.devices.shape
    finer = Mesh(
        mesh.devices.reshape(sections, rows // 2, 2, cols // 2, 2),
        ("section", "z", "x_lo", "y", "x_hi"),
    )
    row, col = ("z", "x_lo"), ("y", "x_hi")
    in_specs = (
        P(None, None, row),
        P(None, None, row),
        P("section", row, col),
        P("section", col, row),
    )
    out_specs = (
        P("section", None, col, row),
        P("section", None, col, row),
        P("section", row, col),
        P("section", col, row),
    )
    return jax.shard_map(local, mesh=finer, in_specs=in_specs, out_specs=out_specs, check_vma=False)
```

```python
import functools

import jax
import jax.numpy as jnp
from jax import lax
from jax.experimental import pallas as pl
from jax.experimental.pallas import tpu as pltpu
from jax.sharding import Mesh, PartitionSpec as P

root_two_over_pi = 0.7978845608028654
cubic = 0.044715
f32 = jnp.float32
bf16 = jnp.bfloat16
CHUNK = 512
VMEM = pl.BlockSpec(memory_space=pltpu.VMEM)
HBM = pl.BlockSpec(memory_space=pltpu.HBM)
ANY = pl.BlockSpec(memory_space=pl.ANY)
LIMIT = pltpu.CompilerParams(vmem_limit_bytes=64 * 1024 * 1024)


def gelu_both(pre):
    inner = root_two_over_pi * (pre + cubic * pre * pre * pre)
    tangent = jnp.tanh(inner)
    value = 0.5 * pre * (1.0 + tangent)
    slope = 0.5 * (1.0 + tangent) + 0.5 * pre * (1.0 - tangent * tangent) * root_two_over_pi * (
        1.0 + 3.0 * cubic * pre * pre
    )
    return value, slope


def dot(left, right, dims):
    return lax.dot_general(left, right, (dims, ((), ())), preferred_element_type=f32)


def shape_of(shape, dtype=bf16):
    return jax.ShapeDtypeStruct(shape, dtype)


def load_weights(layer, by_rows, refs, held, sems):
    mine = lax.axis_index("section") == layer

    def copy(source, part, i):
        where = pl.ds(i * CHUNK, CHUNK)
        block = source.at[where, :] if by_rows else source.at[:, where]
        return pltpu.make_async_copy(block, held.at[part, i], sems.at[part, i])

    def start(which):
        for i in range(held.shape[1]):
            for part, pair in enumerate(refs):
                copy(pair[which], part, i).start()

    pl.when(mine)(lambda: start(0))
    pl.when(jnp.logical_not(mine))(lambda: start(1))
    return lambda part, i: copy(refs[part][0], part, i).wait()


def widen(xs, by_rows, wait, held, put):
    for i in range(held.shape[1]):
        total = None
        for part, x in enumerate(xs):
            wait(part, i)
            got = dot(x, held[part, i], ((1,), (1 if by_rows else 0,)))
            total = got if total is None else total + got
        put(i, total)


def widen_first_kernel(layer, by_rows, mate_at, x_ref, own, other, out_ref, held, sems, stage, out_sems):
    wait = load_weights(layer, by_rows, ((own, other),), held, sems)
    groups, tokens, wide = stage.shape[1 if mate_at == 0 else 0], stage.shape[3], stage.shape[4]
    per_half = wide // CHUNK

    def out_copy(half):
        where = (slice(None),) * (2 if mate_at == 0 else 1) + (half,)
        return pltpu.make_async_copy(stage.at[where], out_ref.at[where], out_sems.at[half])

    def put(i, total):
        half, place = i // per_half, pl.ds((i % per_half) * CHUNK, CHUNK)
        total = total.astype(bf16).reshape(2, groups, tokens, CHUNK)
        for mate in range(2):
            if mate_at == 0:
                stage[mate, :, half, :, place] = total[mate]
            else:
                stage[:, half, mate, :, place] = total[mate]
        if i % per_half == per_half - 1:
            out_copy(half).start()

    widen((x_ref[lax.axis_index("section")],), by_rows, wait, held, put)
    out_copy(0).wait()
    out_copy(1).wait()


def widen_next_kernel(layer, by_rows, riders, arrived, base, own, other, own_mate, other_mate, *rest):
    out_ref, x_out, held, sems, stage, out_sems = rest[riders : riders + 6]
    rides, in_sems = rest[riders + 6 :] if riders else (None, None)
    arrivals = [pltpu.make_async_copy(rest[i], rides.at[i], in_sems.at[i]) for i in range(riders)]
    copies = [
        pltpu.make_async_copy(rides.at[i], out_ref.at[:, :, 1 + i], out_sems.at[2 + i]) for i in range(riders)
    ]
    for copy in arrivals:
        copy.start()
    wait = load_weights(layer, by_rows, ((own, other), (own_mate, other_mate)), held, sems)
    width, per_half = base.shape[1] // 2, stage.shape[3] // CHUNK
    total = arrived[0].astype(f32)
    for i in range(1, arrived.shape[0]):
        total = total + arrived[i].astype(f32)
    x = (base[...].astype(f32) + total).astype(bf16)
    x_out[...] = x
    for arrival, copy in zip(arrivals, copies):
        arrival.wait()
        copy.start()

    def out_copy(half):
        return pltpu.make_async_copy(stage.at[:, half], out_ref.at[:, half, 0], out_sems.at[half])

    def put(i, total):
        half, at = i // per_half, (i % per_half) * CHUNK
        stage[:, half, :, pl.ds(at, CHUNK)] = total.astype(bf16).reshape(stage.shape[0], stage.shape[2], CHUNK)
        if i % per_half == per_half - 1:
            out_copy(half).start()

    widen((x[:, :width], x[:, width:]), by_rows, wait, held, put)
    for copy in [out_copy(0), out_copy(1)] + copies:
        copy.wait()


def narrow(by_rows, which, arrived, wait, held):
    per_half = arrived.shape[4] // CHUNK
    totals = [None, None]
    for i in range(held.shape[1]):
        left = arrived[:, i // per_half, which, :, pl.ds((i % per_half) * CHUNK, CHUNK)]
        left = left.reshape(left.shape[0] * left.shape[1], CHUNK)
        for part in range(2):
            wait(part, i)
            got = dot(left, held[part, i], ((1,), (0 if by_rows else 1,)))
            totals[part] = got if i == 0 else totals[part] + got
    return [total.astype(bf16) for total in totals]


def narrow_kernel(
    layer, by_rows, which, arrived, own, other, own_mate, other_mate, out_ref, held, sems, stage, out_sems
):
    wait = load_weights(layer, by_rows, ((own, other), (own_mate, other_mate)), held, sems)
    near, far = narrow(by_rows, which, arrived, wait, held)
    width = near.shape[1]
    stage[:, :width] = near
    stage[:, width:] = far
    copies = [
        pltpu.make_async_copy(stage, out_ref.at[i], out_sems.at[i]) for i in range(out_ref.shape[0])
    ]
    for copy in copies:
        copy.start()
    for copy in copies:
        copy.wait()


def held_scratch(weight, by_rows, parts):
    units = max(weight.shape)
    chunk = (CHUNK, weight.shape[1]) if by_rows else (weight.shape[0], CHUNK)
    return [
        pltpu.VMEM((parts, units // CHUNK) + chunk, bf16),
        pltpu.SemaphoreType.DMA((parts, units // CHUNK)),
    ]


def kernel_call(body, outs, out_specs, in_specs, scratch, operands, flops=0, moved=0):
    return pl.pallas_call(
        body,
        out_shape=outs,
        in_specs=in_specs,
        out_specs=out_specs,
        scratch_shapes=scratch,
        compiler_params=LIMIT,
        cost_estimate=pl.CostEstimate(flops=flops, bytes_accessed=moved, transcendentals=0),
    )(*operands)


def widen_first(layer, by_rows, mate_at, x, weights, blocks):
    shape = blocks[:mate_at] + (2,) + blocks[mate_at:]
    return kernel_call(
        functools.partial(widen_first_kernel, layer, by_rows, mate_at),
        shape_of(shape),
        HBM,
        [VMEM, HBM, HBM],
        held_scratch(weights[0], by_rows, 1) + [pltpu.VMEM(shape, bf16), pltpu.SemaphoreType.DMA((2,))],
        (x,) + weights[:2],
        flops=2 * x.shape[1] * weights[0].size,
        moved=2 * weights[0].size,
    )


def widen_next(layer, by_rows, arrived, base, weights, blocks, riders=()):
    return kernel_call(
        functools.partial(widen_next_kernel, layer, by_rows, len(riders)),
        (shape_of(blocks[:2] + (1 + len(riders),) + blocks[2:]), shape_of(base.shape)),
        (HBM, VMEM),
        [VMEM, VMEM] + [HBM] * (4 + len(riders)),
        held_scratch(weights[0], by_rows, 2)
        + [pltpu.VMEM(blocks, bf16), pltpu.SemaphoreType.DMA((2 + len(riders),))]
        + ([pltpu.VMEM((len(riders),) + blocks, bf16), pltpu.SemaphoreType.DMA((len(riders),))] if riders else []),
        (arrived, base) + weights + riders,
        flops=4 * base.shape[0] * weights[0].size,
        moved=4 * weights[0].size,
    )


def narrow_next(layer, by_rows, which, arrived, weights, copies):
    tokens, width = arrived.shape[0] * arrived.shape[3], 2 * min(weights[0].shape)
    return kernel_call(
        functools.partial(narrow_kernel, layer, by_rows, which),
        shape_of((copies, tokens, width)),
        HBM,
        [VMEM] + [HBM] * 4,
        held_scratch(weights[0], by_rows, 2)
        + [pltpu.VMEM((tokens, width), bf16), pltpu.SemaphoreType.DMA((copies,))],
        (arrived,) + weights,
        flops=4 * tokens * weights[0].size,
        moved=4 * weights[0].size,
    )


def summed(ref, kind, place):
    total = ref[0, kind, :, place].astype(f32)
    for i in range(1, ref.shape[0]):
        total = total + ref[i, kind, :, place].astype(f32)
    return total


def spread(stage, out_ref, sems):
    copies = [pltpu.make_async_copy(stage, out_ref.at[i], sems.at[i]) for i in range(out_ref.shape[0])]
    for copy in copies:
        copy.start()
    for copy in copies:
        copy.wait()


def act_first_kernel(arrived, out_ref, slope_ref, stage, sems):
    for at in range(0, arrived.shape[3], CHUNK):
        place = pl.ds(at, CHUNK)
        value, slope = gelu_both(summed(arrived, 0, place))
        stage[0, :, place] = value.astype(bf16)
        slope_ref[:, place] = slope
    spread(stage, out_ref, sems)


def act_last_kernel(arrived, out_ref, stage, sems):
    for at in range(0, arrived.shape[3], CHUNK):
        place = pl.ds(at, CHUNK)
        value, slope = gelu_both(summed(arrived, 0, place))
        stage[0, :, place] = (summed(arrived, 1, place) * slope).astype(bf16)
        stage[1, :, place] = value.astype(bf16)
    spread(stage, out_ref, sems)


def act_back_kernel(arrived, slope_ref, out_ref, stage, sems):
    for at in range(0, arrived.shape[3], CHUNK):
        place = pl.ds(at, CHUNK)
        stage[0, :, place] = (summed(arrived, 0, place) * slope_ref[:, place]).astype(bf16)
    spread(stage, out_ref, sems)


def activation(body, kinds, peers, piece, operands, in_specs, slope=False):
    outs, out_specs = [shape_of((peers, kinds) + piece)], [HBM]
    if slope:
        outs, out_specs = outs + [shape_of(piece, f32)], out_specs + [VMEM]
    return kernel_call(
        body,
        outs,
        out_specs,
        in_specs,
        [pltpu.VMEM((kinds,) + piece, bf16), pltpu.SemaphoreType.DMA((peers,))],
        operands,
        flops=2000000,
        moved=2000000,
    )


def finish_kernel(arrived, x1, g1, states, grads):
    total = arrived[0].astype(f32)
    for i in range(1, arrived.shape[0]):
        total = total + arrived[i].astype(f32)

    def ended(base):
        return (base[...].astype(f32) + total).astype(bf16)

    @pl.when(lax.axis_index("section") == 0)
    def _():
        states[...] = x1[...]
        grads[...] = ended(g1)

    @pl.when(lax.axis_index("section") == 1)
    def _():
        states[...] = ended(x1)
        grads[...] = g1[...]


def pick_copies(layer0, layer1, kind, held, sems, start):
    section = lax.axis_index("section")

    def copy(layer, i):
        source = (layer0, layer1)[layer][i].at[:, :, 0 if layer == 0 else kind]
        return pltpu.make_async_copy(source, held.at[i], sems.at[i])

    if start:
        for layer in range(2):

            @pl.when(section == layer)
            def _():
                for i in range(4):
                    copy(layer, i).start()
    else:
        for i in range(4):
            copy(0, i).wait()


def step_chunk(held, step):
    per_half = held.shape[4] // CHUNK
    place = pl.ds(pl.multiple_of((step % per_half) * CHUNK, CHUNK), CHUNK)
    return held[:, :, step // per_half, :, place].reshape(-1, CHUNK)


def fill_tokens(into, layer, full_ref, traded_ref):
    section, mate_pos = lax.axis_index("section"), lax.axis_index("x_lo")
    half_len = full_ref.shape[1] // 2

    @pl.when(section == layer)
    def _():
        for i in range(4):
            half = mate_pos if i < 2 else 1 - mate_pos
            which = section if i % 2 == 0 else 1 - section
            place = pl.ds(pl.multiple_of(half * half_len, half_len), half_len)
            into[pl.ds(i * half_len, half_len), :] = full_ref[which, place, :]

    @pl.when(section != layer)
    def _():
        into[...] = traded_ref[...]


def grad_down_kernel(full_ref, traded_ref, *refs):
    layer0, layer1, (out_ref, held, narrow, sems) = refs[:4], refs[4:8], refs[8:]
    step = pl.program_id(0)

    @pl.when(step == 0)
    def _():
        pick_copies(layer0, layer1, 1, held, sems, True)
        fill_tokens(narrow, 1, full_ref, traded_ref)
        pick_copies(layer0, layer1, 1, held, sems, False)

    out_ref[...] = dot(step_chunk(held, step), narrow[...], ((0,), (0,)))


def grad_up_kernel(full_ref, traded_ref, *refs):
    layer0, layer1, (out_ref, held, narrow, turned, sems) = refs[:4], refs[4:8], refs[8:]
    step = pl.program_id(0)

    @pl.when(step == 0)
    def _():
        pick_copies(layer0, layer1, 0, held, sems, True)
        fill_tokens(narrow, 0, full_ref, traded_ref)
        turned[...] = narrow[...].T
        pick_copies(layer0, layer1, 0, held, sems, False)

    out_ref[...] = dot(turned[...], step_chunk(held, step), ((1,), (0,)))


def weight_grad(down, full, traded, layer0, layer1):
    groups, halves, _, tokens, wide = layer0[0].shape
    units, (all_tokens, width) = halves * wide, traded.shape
    shape, block = ((units, width), (CHUNK, width)) if down else ((width, units), (width, CHUNK))
    turned = [] if down else [pltpu.VMEM((width, all_tokens), bf16)]
    return pl.pallas_call(
        grad_down_kernel if down else grad_up_kernel,
        out_shape=shape_of(shape, f32),
        grid=(units // CHUNK,),
        in_specs=[
            pl.BlockSpec(full.shape, lambda i: (0, 0, 0)),
            pl.BlockSpec(traded.shape, lambda i: (0, 0)),
        ]
        + [HBM] * 8,
        out_specs=pl.BlockSpec(block, lambda i: (i, 0) if down else (0, i)),
        scratch_shapes=[
            pltpu.VMEM((4, groups, halves, tokens, wide), bf16),
            pltpu.VMEM((all_tokens, width), bf16),
        ]
        + turned
        + [pltpu.SemaphoreType.DMA((4,))],
        compiler_params=LIMIT,
        cost_estimate=pl.CostEstimate(
            flops=2 * traded.size * units, bytes_accessed=4 * width * units, transcendentals=0
        ),
    )(full, traded, *layer0, *layer1)


def last_kernel(up, down, *refs):
    layer0, layer1, rest = refs[:4], refs[4:8], refs[8:]
    out_ref, held, up_held, down_held, stage, sems, up_sems, down_sems, out_sem = rest
    section, mate_pos = lax.axis_index("section"), lax.axis_index("x_lo")
    groups, halves, tokens, wide = held.shape[1:]
    per_half, count = wide // CHUNK, up_held.shape[0]
    pick_copies(layer0, layer1, 1, held, sems, True)

    def run(weight, by_rows, weight_held, weight_sems):
        copies = []
        for i in range(count):
            where = pl.ds(i * CHUNK, CHUNK)
            source = weight.at[where, :] if by_rows else weight.at[:, where]
            copies.append(pltpu.make_async_copy(source, weight_held.at[i], weight_sems.at[i]))
        for copy in copies:
            copy.start()
        pick_copies(layer0, layer1, 1, held, sems, False)
        total = None
        for i in range(count):
            left = held[:, :, i // per_half, :, pl.ds((i % per_half) * CHUNK, CHUNK)].reshape(-1, CHUNK)
            copies[i].wait()
            got = dot(left, weight_held[i], ((1,), (0 if by_rows else 1,)))
            total = got if total is None else total + got
        total = total.astype(bf16).reshape(4, groups, tokens, -1)
        for i in range(4):
            half = mate_pos if i < 2 else 1 - mate_pos
            which = section if i % 2 == 0 else 1 - section
            stage[pl.ds(half * groups, groups), which] = total[i]

    pl.when(section == 0)(lambda: run(up, False, up_held, up_sems))
    pl.when(section == 1)(lambda: run(down, True, down_held, down_sems))
    copy = pltpu.make_async_copy(stage, out_ref, out_sem)
    copy.start()
    copy.wait()


def last_product(up, down, layer0, layer1):
    groups, halves, _, tokens, wide = layer0[0].shape
    width, units = up.shape
    out = (2 * groups, 2, tokens, width)
    return kernel_call(
        last_kernel,
        shape_of(out),
        HBM,
        [HBM] * 10,
        [
            pltpu.VMEM((4, groups, halves, tokens, wide), bf16),
            pltpu.VMEM((units // CHUNK, width, CHUNK), bf16),
            pltpu.VMEM((units // CHUNK, CHUNK, width), bf16),
            pltpu.VMEM(out, bf16),
            pltpu.SemaphoreType.DMA((4,)),
            pltpu.SemaphoreType.DMA((units // CHUNK,)),
            pltpu.SemaphoreType.DMA((units // CHUNK,)),
            pltpu.SemaphoreType.DMA,
        ],
        (up, down) + layer0 + layer1,
        flops=8 * groups * tokens * up.size,
        moved=6 * up.size,
    )


def exchange(blocks, axes):
    return lax.all_to_all(blocks, axes, 0, 0)


CORES = ("section", "x_lo")


def to_other_core(block):
    return lax.ppermute(block, "section", [(0, 1), (1, 0)])


def to_mate(block):
    return lax.ppermute(block, "x_lo", [(0, 1), (1, 0)])


def to_other_core_of_mate(block):
    return lax.ppermute(block, CORES, [(0, 3), (3, 0), (1, 2), (2, 1)])


def only_to_mate(block, section):
    at = 2 * section
    return lax.ppermute(block, CORES, [(at, at + 1), (at + 1, at)])


def only_to_core(block, section):
    return lax.ppermute(block, "section", [(1 - section, section)])


def to_owner(block, section):
    at, source = 2 * section, 2 * (1 - section)
    across = lax.ppermute(block, CORES, [(source, at + 1), (source + 1, at)])
    return block, only_to_core(block, section), only_to_mate(block, section), across


def late(block, after):
    return lax.optimization_barrier((block, after))[0]


def local(inputs, cotangent, w_up, w_down):
    col = ("y", "x_hi")
    section, mate_pos, col_pos = (lax.axis_index(name) for name in ("section", "x_lo", col))
    first = section == 0
    own_up, own_down = w_up[0], w_down[0]
    tokens, width = inputs.shape[1:]
    half_len = tokens // 2
    rings = lax.axis_size("z")
    piece = (tokens // rings, own_up.shape[1] // 2)
    blocks = (half_len // piece[0], 2) + piece

    def half_of(array, which):
        return lax.dynamic_slice_in_dim(array, which * half_len, half_len, 0)

    def batch(array, which):
        return lax.dynamic_index_in_dim(array, which, 0, keepdims=False)

    def both_widths(array):
        def cut(half):
            place = section, half * half_len, 0
            return lax.dynamic_slice(array, place, (1, half_len, width))[0]

        return jnp.concatenate([cut(mate_pos), to_mate(cut(1 - mate_pos))], axis=1)

    other_up = to_other_core(own_up)
    first_part = widen_first(0, False, 2, inputs, (own_up, other_up), blocks)
    mate_down0 = only_to_mate(late(own_down, other_up), 0)
    arrived = exchange(first_part.reshape((2 * rings, 1) + piece), ("z", "x_lo"))

    other_down = to_other_core(late(own_down, other_up))
    d_hid1 = widen_first(1, True, 0, late(cotangent, first_part), (own_down, other_down), blocks)
    arrived, mate_down0 = late((arrived, mate_down0), d_hid1)
    d_hid1, given = batch(d_hid1, mate_pos), to_mate(batch(d_hid1, 1 - mate_pos))
    down0 = own_down, other_down, mate_down0, only_to_core(mate_down0, 1)

    value0, slope0 = activation(act_first_kernel, 1, rings, piece, (arrived,), [VMEM], slope=True)
    mate_up1 = only_to_mate(late(own_up, value0), 1)
    hid0 = exchange(value0, "z").reshape(blocks[:2] + (1,) + piece)
    x0_both, g2_both = (both_widths(late(array, value0)) for array in (inputs, cotangent))
    d_hid1 = (d_hid1.astype(f32) + late(given, value0).astype(f32)).astype(bf16)
    hid0 = late(hid0, d_hid1)
    part = narrow_next(0, True, 0, hid0, down0, lax.axis_size(col))
    mate_up1, x0_both, g2_both = late((mate_up1, x0_both, g2_both), part)
    up1 = own_up, other_up, mate_up1, only_to_core(mate_up1, 0)
    arrived = exchange(part, col)

    pre1, x1 = widen_next(1, False, arrived, x0_both, up1, blocks, (d_hid1,))
    hid0s = to_owner(late(hid0, pre1), 0)
    arrived = exchange(pre1.reshape((rings, 2) + piece), "z")
    (acts1,) = activation(act_last_kernel, 2, rings, piece, (arrived,), [VMEM])
    acts1 = late(exchange(acts1, "z").reshape(blocks[:2] + (2,) + piece), hid0s)
    part = narrow_next(1, False, 0, acts1, up1, lax.axis_size(col))
    arrived = exchange(part, col)

    d_hid0, g1 = widen_next(0, True, arrived, g2_both, down0, blocks)
    acts1, both1 = late((acts1, jnp.stack([x1, g1])), d_hid0)
    acts1s = to_owner(acts1, 1)
    arrived = exchange(d_hid0.reshape((rings, 1) + piece), "z")
    near, far = both1[..., :width], both1[..., width:]
    both1 = jnp.stack([near, to_other_core(near), to_mate(far), to_other_core_of_mate(far)])
    both1 = both1.reshape((2, 2) + near.shape)

    x1s, g1s = both1[:, :, 0].reshape(2 * tokens, width), both1[:, :, 1].reshape(2 * tokens, width)

    (d_pre0,) = activation(act_back_kernel, 1, rings, piece, (arrived, slope0), [VMEM, VMEM])
    d_pre0 = late(exchange(d_pre0, "z").reshape(blocks[:2] + (1,) + piece), acts1s)
    down_grad = weight_grad(True, cotangent, late(g1s, d_pre0), hid0s, acts1s)
    d_pre0s = late(to_owner(d_pre0, 0), down_grad)

    last = last_product(own_up, own_down, d_pre0s, acts1s)
    x1s, d_pre0s = late((x1s, d_pre0s), last)
    arrived = exchange(last, col)
    up_grad = weight_grad(False, inputs, x1s, d_pre0s, acts1s)

    out_len = tokens // lax.axis_size(col)
    per_half = half_len // out_len
    away = jnp.where(col_pos // per_half == mate_pos, 0, 1)
    pieces = lax.dynamic_index_in_dim(both1, away, 0, keepdims=False)
    pieces = lax.dynamic_slice_in_dim(pieces, (col_pos % per_half) * out_len, out_len, 2)
    pieces = jnp.where(first, pieces, pieces[::-1])
    states, grads = kernel_call(
        finish_kernel,
        [shape_of(pieces[:, 0].shape)] * 2,
        [VMEM] * 2,
        [VMEM] * 3,
        [],
        (arrived, pieces[:, 0], pieces[:, 1]),
        flops=100000,
        moved=200000,
    )
    return states[None], grads[None], up_grad[None], down_grad[None]


def solution(mesh):
    sections, rows, cols = mesh.devices.shape
    finer = Mesh(
        mesh.devices.reshape(sections, rows // 2, 2, cols // 2, 2),
        ("section", "z", "x_lo", "y", "x_hi"),
    )
    row, col = ("z", "x_lo"), ("y", "x_hi")
    in_specs = (
        P(None, None, row),
        P(None, None, row),
        P("section", row, col),
        P("section", col, row),
    )
    out_specs = (
        P("section", None, col, row),
        P("section", None, col, row),
        P("section", row, col),
        P("section", col, row),
    )
    return jax.shard_map(local, mesh=finer, in_specs=in_specs, out_specs=out_specs, check_vma=False)
```
